32 devices in a mesh: gx: 2 (over x), gy: 4 (over y, core), gz: 4 (over z).
Axes of the slice: x: 2, y: 2, z: 4, core: 2. Of those that a mesh axis runs over, the one named last changes fastest.
Arguments:
- populations: float32 [19, 16, 64, 512], P(None, 'gx', 'gy', 'gz'), may hold values from 0.01 to 0.06
- adjoint_next: float32 [19, 16, 64, 512], P(None, 'gx', 'gy', 'gz'), may hold values from -6 to 6
Outputs:
- adjoint_before: float32 [19, 16, 64, 512], P(None, 'gx', 'gy', 'gz')
The draws below stay inside these ranges and needn't reach their ends.
All inputs are finite; a program needn't handle non-finite values.
Results may differ from the reference program's by a relative error of at most 0.00002.
Values sent between devices are 32-bit elements; how exact they have to be, the bound alone decides.
No kernel may reach another device: no remote copies, remote signals or barrier semaphores. Data moves between devices by JAX's collectives and lax.ppermute only.
A program may use at most 64 MiB of HBM per device.

```python
import math
import jax
import jax.numpy as jnp
from jax import lax

Q = 19
NX = 16
NY = 64
NZ = 512
N_GX = 2


def block_levels(own_key, shape, pieces, least, high):
    def one(axis_at, parts):
        steps = jax.random.uniform(jax.random.fold_in(jax.random.fold_in(own_key, 6), axis_at), (parts,), jnp.float32, least / len(pieces), high / len(pieces))
        return jnp.repeat(jnp.exp(steps), shape[axis_at] // parts).reshape((-1,) + (1,) * (len(shape) - axis_at - 1))

    level = one(*pieces[0])
    for cut in pieces[1:]:
        level = level * one(*cut)
    return level


def gaussian(rng, dims, deviation, bound, split=(), held_as=jnp.bfloat16):
    drawn = jax.random.normal(rng, dims, jnp.float32) * deviation
    if len(split) > 0:
        drawn = block_levels(rng, dims, split, -0.22, 0.18) * drawn
    return jnp.clip(drawn, min=-bound, max=bound).astype(held_as)


def setup_inputs(seed: int = 0) -> dict:
    keys = jax.random.split(jax.random.key(seed), 3)
    return {
        "populations": jnp.clip(jnp.exp(math.log(0.06) - 1.7917595 * jax.random.uniform(keys[0], (Q, NX, NY, NZ), jnp.float32) ** block_levels(keys[0], (Q, NX, NY, NZ), ((1, 2), (2, 4), (3, 4)), -0.2, 0.2)), 0.01, 0.06),
        "adjoint_next": gaussian(keys[1], (Q, NX, NY, NZ), 1.0, 6.0, ((1, 2), (2, 4), (3, 4)), jnp.float32),
    }


DIRECTIONS = ((0, 0, 0), (1, 0, 0), (-1, 0, 0), (0, 1, 0), (0, -1, 0), (0, 0, 1), (0, 0, -1), (1, 1, 0), (-1, -1, 0), (1, -1, 0), (-1, 1, 0), (1, 0, 1), (-1, 0, -1), (1, 0, -1), (-1, 0, 1), (0, 1, 1), (0, -1, -1), (0, 1, -1), (0, -1, 1))
WEIGHTS = (1.0 / 3.0,) + (1.0 / 18.0,) * 6 + (1.0 / 36.0,) * 12
RELAX_TIME = 0.8
COUPLING = -5.5

def project(vector, member):
    return DIRECTIONS[member][0] * vector[0] + DIRECTIONS[member][1] * vector[1] + DIRECTIONS[member][2] * vector[2]

def summed(populations):
    density = populations[0]
    for member in range(1, 19):
        density = density + populations[member]
    return density

def collide(populations, force_field):
    density = summed(populations)
    velocity = []
    for component in range(3):
        moment = 0.5 * force_field[component]
        for member in range(1, 19):
            heading = DIRECTIONS[member][component]
            if heading == 1:
                moment = moment + populations[member]
            elif heading == -1:
                moment = moment - populations[member]
        velocity.append(moment / density)
    speed_sq = velocity[0] * velocity[0] + velocity[1] * velocity[1] + velocity[2] * velocity[2]
    along_force = velocity[0] * force_field[0] + velocity[1] * force_field[1] + velocity[2] * force_field[2]
    results = []
    for member in range(19):
        lattice_u = project(velocity, member)
        lattice_f = project(force_field, member)
        equilibrium = WEIGHTS[member] * density * (1.0 + 3.0 * lattice_u + 4.5 * lattice_u * lattice_u - 1.5 * speed_sq)
        source = WEIGHTS[member] * (3.0 * (lattice_f - along_force) + 9.0 * lattice_u * lattice_f)
        results.append(populations[member] - (populations[member] - equilibrium) / RELAX_TIME + (1.0 - 0.5 / RELAX_TIME) * source)
    return jnp.stack(results)

def shifted(field_in, offset, direction_sign):
    return jnp.roll(field_in, (-direction_sign * offset[0], -direction_sign * offset[1], -direction_sign * offset[2]), (0, 1, 2))

def by_blocks(values_in):
    leading = values_in.shape[0]
    return values_in.reshape(leading, N_GX, NX // N_GX, NY, NZ).transpose(1, 0, 2, 3, 4)

def from_blocks(values_in):
    leading = values_in.shape[1]
    return values_in.transpose(1, 0, 2, 3, 4).reshape(leading, NX, NY, NZ)

def pulled(block_items):
    populations, force_field, arrived = block_items
    unused, pullback = jax.vjp(collide, populations, force_field)
    return pullback(arrived)

def reference(populations, adjoint_next):
    density = summed(populations)
    decay_factor = jnp.exp(-density)
    potential = 1.0 - decay_factor
    gradient = [jnp.zeros_like(potential) for component in range(3)]
    for member in range(1, 19):
        neighbour = WEIGHTS[member] * shifted(potential, DIRECTIONS[member], 1)
        for component in range(3):
            if DIRECTIONS[member][component] != 0:
                gradient[component] = gradient[component] + DIRECTIONS[member][component] * neighbour
    force_field = jnp.stack([-COUPLING * potential * gradient[component] for component in range(3)])
    arrived = jnp.stack([shifted(adjoint_next[member], DIRECTIONS[member], 1) for member in range(19)])
    pop_bar, force_bar = lax.map(pulled, (by_blocks(populations), by_blocks(force_field), by_blocks(arrived)))
    pop_bar = from_blocks(pop_bar)
    force_bar = from_blocks(force_bar)
    flux_field = potential[None] * force_bar
    remote = jnp.zeros_like(potential)
    for member in range(1, 19):
        share_part = WEIGHTS[member] * project(flux_field, member)
        remote = remote + shifted(share_part, DIRECTIONS[member], -1)
    local_part = force_bar[0] * gradient[0] + force_bar[1] * gradient[1] + force_bar[2] * gradient[2]
    potential_bar = -COUPLING * (local_part + remote)
    return pop_bar + (potential_bar * decay_factor)[None]
```

```python
import jax
import jax.numpy as jnp
from jax import lax
from jax.experimental import pallas as pl
from jax.experimental.pallas import tpu as pltpu
from jax.sharding import PartitionSpec as P

DIRECTIONS = (
    (0, 0, 0),
    (1, 0, 0),
    (-1, 0, 0),
    (0, 1, 0),
    (0, -1, 0),
    (0, 0, 1),
    (0, 0, -1),
    (1, 1, 0),
    (-1, -1, 0),
    (1, -1, 0),
    (-1, 1, 0),
    (1, 0, 1),
    (-1, 0, -1),
    (1, 0, -1),
    (-1, 0, 1),
    (0, 1, 1),
    (0, -1, -1),
    (0, 1, -1),
    (0, -1, 1),
)
W0, W1, W2 = 1.0 / 3.0, 1.0 / 18.0, 1.0 / 36.0
RELAX_TIME = 0.8
COUPLING = -5.5
INV_TAU = 1.0 / RELAX_TIME
KAPPA = 1.0 - 0.5 / RELAX_TIME

RHO, MOM, FIELDS = 19, 20, 23
ROWS = 24
F32 = jnp.float32
VM = pl.BlockSpec(memory_space=pltpu.VMEM)
HB = pl.BlockSpec(memory_space=pl.ANY)


def deep_fields(dim, side):
    return [i for i in range(19) if DIRECTIONS[i][dim] == side] + [RHO]


def side_fields(dim, side):
    return deep_fields(dim, side) + [i for i in range(19) if DIRECTIONS[i][dim] == 0] + [MOM, MOM + 1, MOM + 2]


def side_entries(dim, side):
    return [(f, d) for d in (0, 1) for f in (side_fields(dim, side) if d == 0 else deep_fields(dim, side))]


def lane_ids(rows):
    return lax.broadcasted_iota(jnp.int32, (rows, 128), 1)


def lroll(v, amount):
    amount = amount % 128
    return v if isinstance(amount, int) and amount == 0 else pltpu.roll(v, amount, 1)


def yroll(v, c):
    return v if c == 0 else pltpu.roll(v, (-c) % ROWS, 0)


def call(body, ins, outs, scratch=(), aliases=None, name=None, in_specs=None, out_specs=None):
    return pl.pallas_call(
        body,
        in_specs=in_specs or [VM] * len(ins),
        out_specs=out_specs or [VM] * len(outs),
        out_shape=[jax.ShapeDtypeStruct(s, F32) for s in outs],
        scratch_shapes=list(scratch),
        input_output_aliases=aliases or {},
        name=name,
        compiler_params=pltpu.CompilerParams(vmem_limit_bytes=20 * 2**20),
    )(*ins)


def load_kernel(pop_hbm, adj_hbm, ext, mini, zlow, zhigh, xmsg, pops, sems):
    nx = pop_hbm.shape[1]
    copies = []
    for f in range(19):
        c = pltpu.make_async_copy(pop_hbm.at[f], pops.at[f], sems.at[f])
        c.start()
        copies.append(c)
    for f in range(19):
        c = pltpu.make_async_copy(adj_hbm.at[f], ext.at[f, pl.ds(2, nx), pl.ds(0, 16), :], sems.at[19 + f])
        c.start()
        copies.append(c)
    for c in copies[:19]:
        c.wait()

    def moments(x, _):
        rho = pops[0, x]
        mom = [None] * 3
        for i in range(1, 19):
            p = pops[i, x]
            rho = rho + p
            for k in range(3):
                c = DIRECTIONS[i][k]
                if c:
                    mom[k] = (p if c > 0 else -p) if mom[k] is None else (mom[k] + p if c > 0 else mom[k] - p)
        ext[RHO, x + 2, pl.ds(0, 16), :] = rho
        for k in range(3):
            ext[MOM + k, x + 2, pl.ds(0, 16), :] = mom[k]
        return 0

    lax.fori_loop(0, nx, moments, 0)
    for c in copies[19:]:
        c.wait()
    lane = lane_ids(16)

    def edges(f, _):
        e = lroll(ext[f, 2, pl.ds(0, 16), :], 10)
        for x in range(1, nx):
            e = jnp.where(lane // 4 == x + 2, lroll(ext[f, x + 2, pl.ds(0, 16), :], 4 * x + 10), e)
        mini[f, pl.ds(0, 16), :] = jnp.where(lane < 64, e, lroll(e, 64))
        return 0

    lax.fori_loop(0, FIELDS, edges, 0)
    for side, msg in ((-1, zlow), (1, zhigh)):
        fields = side_fields(2, side)
        for t in range(msg.shape[0]):
            acc = None
            for j in range(8 * t, min(8 * t + 8, len(fields))):
                q = j % 8
                b, p = q // 2, q % 2
                if side < 0:
                    v = lroll(mini[fields[j], pl.ds(0, 16), :], 32 * b + 2 * p - 72)
                else:
                    v = lroll(mini[fields[j], pl.ds(0, 16), :], 32 * b + 2 * p - 10)
                acc = v if acc is None else jnp.where((lane // 32 == b) & ((lane % 4) // 2 == p), v, acc)
            msg[t] = acc
    for s, side in enumerate((-1, 1)):
        for e, (f, d) in enumerate(side_entries(0, side)):
            plane = (nx + 1 - d) if side < 0 else (2 + d)
            xmsg[s, e] = ext[f, plane, pl.ds(0, 16), :]


def zy_kernel(ext, mini_in, rlow, rhigh, mini, ylow, yhigh):
    lane = lane_ids(16)
    for f in range(FIELDS):
        mini[f, pl.ds(0, 16), :] = mini_in[f, pl.ds(0, 16), :]
    for side, msg in ((-1, rlow), (1, rhigh)):
        if side < 0:
            keep = (lane >= 8) & (lane < 40) & (lane % 4 < 2)
        else:
            keep = (lane >= 72) & (lane < 104) & (lane % 4 >= 2)
        for j, f in enumerate(side_fields(2, side)):
            q = j % 8
            b, p = q // 2, q % 2
            back = 8 - 32 * b - 2 * p if side < 0 else 74 - 32 * b - 2 * p
            mini[f, pl.ds(0, 16), :] = jnp.where(keep, lroll(msg[j // 8], back), mini[f, pl.ds(0, 16), :])
    for side, msg in ((-1, ylow), (1, yhigh)):
        entries = side_entries(1, side)
        for e, (f, d) in enumerate(entries):
            row = 15 - d if side < 0 else d
            msg[pl.ds(8 * e, 8), :] = ext[f, pl.ds(2, 8), row, :]
            msg[pl.ds(8 * len(entries) + e, 1), :] = mini[f, pl.ds(row, 1), :]


def yx_kernel(ext_in, mini_in, rlow, rhigh, ext, mini, xmsg):
    lane = lane_ids(ROWS)
    for side, msg in ((-1, rlow), (1, rhigh)):
        entries = side_entries(1, side)
        for e, (f, d) in enumerate(entries):
            row = 23 - d if side < 0 else 16 + d
            ext[f, pl.ds(2, 8), row, :] = msg[pl.ds(8 * e, 8), :]
            mini[f, pl.ds(row, 1), :] = msg[pl.ds(8 * len(entries) + e, 1), :]
    tile_row = lax.broadcasted_iota(jnp.int32, (8, 128), 0)
    for s, side in enumerate((-1, 1)):
        entries = side_entries(0, side)
        for e in range(0, len(entries), 2):
            pair = []
            for f, d in entries[e : e + 2]:
                plane = 9 - d if side < 0 else 2 + d
                pair.append(ext[f, plane, pl.ds(16, 8), :])
            xmsg[s, pl.ds(4 * e, 8), :] = jnp.where(tile_row < 4, pltpu.roll(pair[0], 2, 0), pltpu.roll(pair[1], 6, 0))
        fields = side_fields(0, side)
        for t in range(3):
            acc = None
            for j in range(8 * t, min(8 * t + 8, len(fields))):
                q = j % 8
                v = lroll(mini[fields[j]], 8 * q - (32 if side < 0 else 8))
                acc = v if acc is None else jnp.where((lane % 64) // 8 == q, v, acc)
            xmsg[s, pl.ds(4 * len(entries) + ROWS * t, ROWS), :] = acc


def cell(b, rho, mom, psi, g):
    pairs = {}
    for i in range(1, 19, 2):
        pairs[i] = (b[i] + b[i + 1], b[i] - b[i + 1])
    s = {i: v[0] for i, v in pairs.items()}
    d = {i: v[1] for i, v in pairs.items()}
    sxy, sxz, syz = s[7] + s[9], s[11] + s[13], s[15] + s[17]
    a0 = W0 * b[0] + W1 * (s[1] + s[3] + s[5]) + W2 * (sxy + sxz + syz)
    a1 = (
        (3 * W1) * d[1] + (3 * W2) * ((d[7] + d[9]) + (d[11] + d[13])),
        (3 * W1) * d[3] + (3 * W2) * ((d[7] - d[9]) + (d[15] + d[17])),
        (3 * W1) * d[5] + (3 * W2) * ((d[11] - d[13]) + (d[15] - d[17])),
    )
    a03 = 3.0 * a0
    bxx = (9 * W1) * s[1] + (9 * W2) * (sxy + sxz) - a03
    byy = (9 * W1) * s[3] + (9 * W2) * (sxy + syz) - a03
    bzz = (9 * W1) * s[5] + (9 * W2) * (sxz + syz) - a03
    bxy = (9 * W2) * (s[7] - s[9])
    bxz = (9 * W2) * (s[11] - s[13])
    byz = (9 * W2) * (s[15] - s[17])
    force = [(-COUPLING * psi) * gk for gk in g]
    inv = 1.0 / rho
    u = [(m + 0.5 * fk) * inv for m, fk in zip(mom, force)]

    def apply(v):
        return (
            bxx * v[0] + bxy * v[1] + bxz * v[2],
            bxy * v[0] + byy * v[1] + byz * v[2],
            bxz * v[0] + byz * v[1] + bzz * v[2],
        )

    w = [p + q for p, q in zip(a1, apply(u))]
    bf = [(KAPPA * inv) * q for q in apply(force)]
    force_bar = [p + 0.5 * q for p, q in zip(w, bf)]
    return a0, a1, u, w, bf, force_bar


def dot(p, q):
    return p[0] * q[0] + p[1] * q[1] + p[2] * q[2]


def last_kernel(ext_in, mini_in, r1, r2, out_hbm, ext, mini, psi, zs, zd, flux, out, sems):
    nx = 8
    lane = lane_ids(ROWS)
    first, last = lane == 0, lane == 127
    for s, side in enumerate((-1, 1)):
        entries = side_entries(0, side)
        for e, (f, d) in enumerate(entries):
            plane = 1 - d if side < 0 else 10 + d
            ext[f, plane, pl.ds(0, 16), :] = r1[s, e]
            tile = r2[s, pl.ds(8 * (e // 2), 8), :]
            ext[f, plane, pl.ds(16, 8), :] = pltpu.roll(tile, 6 if e % 2 == 0 else 2, 0)
        keep = (lane % 64) // 8 == (0 if side < 0 else 5)
        for j, f in enumerate(side_fields(0, side)):
            q = j % 8
            v = r2[s, pl.ds(4 * len(entries) + ROWS * (j // 8), ROWS), :]
            mini[f] = jnp.where(keep, lroll(v, (0 if side < 0 else 40) - 8 * q), mini[f])

    def zsh(v, small, plane, c):
        if c > 0:
            return lroll(jnp.where(first, lroll(small, 62 - 4 * plane + 128), v), 127)
        return lroll(jnp.where(last, lroll(small, 126 - 4 * plane), v), 1)

    mpsi = 1.0 - jnp.exp(-mini[RHO])

    def msh(v, c):
        return lroll(yroll(v, c[1]), -4 * c[0] - c[2])

    def mgrad(v):
        ys = yroll(v, 1) + yroll(v, -1)
        zp, zm = lroll(v, -1), lroll(v, 1)
        xp, xm = lroll(v, -4), lroll(v, 4)
        qx = W1 * v + W2 * (ys + zp + zm)
        qy = W1 * v + W2 * (xp + xm + zp + zm)
        qz = W1 * v + W2 * (xp + xm + ys)
        return (
            lroll(qx, -4) - lroll(qx, 4),
            yroll(qy, 1) - yroll(qy, -1),
            lroll(qz, -1) - lroll(qz, 1),
        )

    mg = mgrad(mpsi)
    mb = [msh(mini[i], DIRECTIONS[i]) for i in range(19)]
    mfb = cell(mb, mini[RHO], [mini[MOM + k] for k in range(3)], mpsi, mg)[5]
    mflux = [mpsi * v for v in mfb]

    def potential(p, _):
        v = 1.0 - jnp.exp(-ext[RHO, p])
        psi[p] = v
        a, b = zsh(v, mpsi, p, 1), zsh(v, mpsi, p, -1)
        zs[p] = a + b
        zd[p] = a - b
        return 0

    lax.fori_loop(0, nx + 4, potential, 0)

    def collide(p, own):
        v, xp, xm = psi[p], psi[p + 1], psi[p - 1]
        qxp = W1 * xp + W2 * (yroll(xp, 1) + yroll(xp, -1) + zs[p + 1])
        qxm = W1 * xm + W2 * (yroll(xm, 1) + yroll(xm, -1) + zs[p - 1])
        qy = W1 * v + W2 * (xp + xm + zs[p])
        zz = zd[p]
        g = (
            qxp - qxm,
            yroll(qy, 1) - yroll(qy, -1),
            W1 * zz + W2 * (zd[p + 1] + zd[p - 1] + yroll(zz, 1) + yroll(zz, -1)),
        )
        b = []
        for i in range(19):
            cx, cy, cz = DIRECTIONS[i]
            a = ext[i, p + cx]
            if cz:
                a = zsh(a, mini[i], p + cx, cz)
            b.append(yroll(a, cy))
        a0, a1, u, w, bf, fb = cell(b, ext[RHO, p], [ext[MOM + k, p] for k in range(3)], v, g)
        for k in range(3):
            flux[k, p] = v * fb[k]
        if own:
            top = lambda a: a[:16]
            vv = [top(INV_TAU * wk + bk) for wk, bk in zip(w, bf)]
            uu = [top(a) for a in u]
            base = INV_TAU * (top(a0) + 0.5 * dot([top(p_ + q_) for p_, q_ in zip(a1, w)], uu)) - dot(vv, uu)
            base = base + (-COUPLING * (1.0 - top(v))) * top(dot(fb, g))
            x = p - 2
            for i in range(19):
                o = (1.0 - INV_TAU) * top(b[i]) + base
                for k in range(3):
                    if DIRECTIONS[i][k] > 0:
                        o = o + vv[k]
                    elif DIRECTIONS[i][k] < 0:
                        o = o - vv[k]
                out[i, x] = o

    collide(1, False)
    collide(nx + 2, False)

    def own_plane(p, _):
        collide(p, True)
        return 0

    lax.fori_loop(2, nx + 2, own_plane, 0)

    def z_of_flux(p, _):
        fx, fy, fz = flux[0, p], flux[1, p], flux[2, p]
        sx = zsh(fx, mflux[0], p, 1) + zsh(fx, mflux[0], p, -1)
        zs[p] = W1 * fx + W2 * (yroll(fx, 1) + yroll(fx, -1) + sx)
        zd[p] = zsh(fz, mflux[2], p, 1) - zsh(fz, mflux[2], p, -1)
        return 0

    lax.fori_loop(1, nx + 3, z_of_flux, 0)

    def finish(p, _):
        fy = flux[1, p]
        sy = zsh(fy, mflux[1], p, 1) + zsh(fy, mflux[1], p, -1)
        qy = W1 * fy + W2 * (flux[1, p + 1] + flux[1, p - 1] + sy)
        zz = zd[p]
        div = (
            (zs[p + 1] - zs[p - 1])
            + (yroll(qy, 1) - yroll(qy, -1))
            + (W1 * zz + W2 * (zd[p + 1] + zd[p - 1] + yroll(zz, 1) + yroll(zz, -1)))
        )
        term = ((COUPLING * (1.0 - psi[p])) * div)[:16]
        x = p - 2
        for i in range(19):
            out[i, x] = out[i, x] + term
        pltpu.make_async_copy(out.at[:, x], out_hbm.at[:, x], sems.at[x]).start()
        return 0

    lax.fori_loop(2, nx + 2, finish, 0)
    for x in range(nx):
        pltpu.make_async_copy(out.at[:, x], out_hbm.at[:, x], sems.at[x]).wait()


def swap(low, high, axis):
    n = lax.axis_size(axis)
    up = [(i, (i + 1) % n) for i in range(n)]
    return lax.ppermute(low, axis, up), lax.ppermute(high, axis, [(j, i) for i, j in up])


def swap_both(msg, axis):
    n = lax.axis_size(axis)
    if n == 2:
        return lax.ppermute(msg, axis, [(0, 1), (1, 0)])
    return jnp.stack(swap(msg[0], msg[1], axis))


def per_device(populations, adjoint_next):
    nx = populations.shape[1]
    ext_shape, mini_shape = (FIELDS, nx + 4, ROWS, 128), (FIELDS, ROWS, 128)
    ext, mini, zlow, zhigh, xmsg = call(
        load_kernel,
        (populations, adjoint_next),
        (ext_shape, mini_shape, (3, 16, 128), (3, 16, 128), (2, 24, 16, 128)),
        scratch=[pltpu.VMEM((19, nx, 16, 128), F32), pltpu.SemaphoreType.DMA((38,))],
        in_specs=[HB, HB],
        name="load",
    )
    zlow, zhigh = swap(zlow, zhigh, "gz")
    x1 = swap_both(xmsg, "gx")
    mini, ylow, yhigh = call(
        zy_kernel,
        (ext, mini, zlow, zhigh),
        (mini_shape, (24 * 9, 128), (24 * 9, 128)),
        name="zy",
    )
    ylow, yhigh = swap(ylow, yhigh, "gy")
    ext, mini, xmsg2 = call(
        yx_kernel,
        (ext, mini, ylow, yhigh),
        (ext_shape, mini_shape, (2, 24 * 4 + 3 * ROWS, 128)),
        aliases={0: 0, 1: 1},
        name="yx",
    )
    x2 = swap_both(xmsg2, "gx")
    scratch = [
        pltpu.VMEM((nx + 4, ROWS, 128), F32),
        pltpu.VMEM((nx + 4, ROWS, 128), F32),
        pltpu.VMEM((nx + 4, ROWS, 128), F32),
        pltpu.VMEM((3, nx + 4, ROWS, 128), F32),
        pltpu.VMEM((19, nx, 16, 128), F32),
        pltpu.SemaphoreType.DMA((nx,)),
    ]

    def last(ext_in, mini_in, r1, r2, out_hbm, ext_out, mini_out, *rest):
        last_kernel(ext_in, mini_in, r1, r2, out_hbm, ext_out, mini_out, *rest)

    out, _, _ = call(
        last,
        (ext, mini, x1, x2),
        (populations.shape, ext_shape, mini_shape),
        scratch=scratch,
        aliases={0: 1, 1: 2},
        out_specs=[HB, VM, VM],
        name="last",
    )
    return out


def solution(mesh):
    return jax.shard_map(
        per_device,
        mesh=mesh,
        in_specs=(P(None, "gx", "gy", "gz"), P(None, "gx", "gy", "gz")),
        out_specs=P(None, "gx", "gy", "gz"),
        check_vma=False,
    )
```

```python
import jax
import jax.numpy as jnp
from jax import lax
from jax.experimental import pallas as pl
from jax.experimental.pallas import tpu as pltpu
from jax.sharding import PartitionSpec as P

DIRECTIONS = (
    (0, 0, 0),
    (1, 0, 0),
    (-1, 0, 0),
    (0, 1, 0),
    (0, -1, 0),
    (0, 0, 1),
    (0, 0, -1),
    (1, 1, 0),
    (-1, -1, 0),
    (1, -1, 0),
    (-1, 1, 0),
    (1, 0, 1),
    (-1, 0, -1),
    (1, 0, -1),
    (-1, 0, 1),
    (0, 1, 1),
    (0, -1, -1),
    (0, 1, -1),
    (0, -1, 1),
)
W0, W1, W2 = 1.0 / 3.0, 1.0 / 18.0, 1.0 / 36.0
RELAX_TIME = 0.8
COUPLING = -5.5
INV_TAU = 1.0 / RELAX_TIME
KAPPA = 1.0 - 0.5 / RELAX_TIME

RHO, MOM, FIELDS = 19, 20, 23
ROWS = 24
F32 = jnp.float32
VM = pl.BlockSpec(memory_space=pltpu.VMEM)
HB = pl.BlockSpec(memory_space=pltpu.HBM)


def deep_fields(dim, side):
    return [i for i in range(19) if DIRECTIONS[i][dim] == side] + [RHO]


def side_fields(dim, side):
    return deep_fields(dim, side) + [i for i in range(19) if DIRECTIONS[i][dim] == 0] + [MOM, MOM + 1, MOM + 2]


def side_entries(dim, side):
    return [(f, d) for d in (0, 1) for f in (side_fields(dim, side) if d == 0 else deep_fields(dim, side))]


def edge_entries(side):
    found = []
    for up in (-1, 1):
        for dx in (0, 1):
            for dy in (0, 1):
                row = 23 - dy if up < 0 else 16 + dy
                across = deep_fields(0, side) if dx else side_fields(0, side)
                along = deep_fields(1, up) if dy else side_fields(1, up)
                found += [(f, dx, row) for f in across if f in along]
    return found


EDGE_LINES = -(-len(edge_entries(1)) // 8) * 8


def is_odd(axis, rows):
    return jnp.full((rows, 128), lax.axis_index(axis) % 2, jnp.int32) == 1


def lane_ids(rows):
    return lax.broadcasted_iota(jnp.int32, (rows, 128), 1)


def lroll(v, amount):
    amount = amount % 128
    return v if isinstance(amount, int) and amount == 0 else pltpu.roll(v, amount, 1)


def yroll(v, c):
    return v if c == 0 else pltpu.roll(v, (-c) % ROWS, 0)


def call(body, ins, outs, scratch=(), aliases=None, name=None, in_specs=None, out_specs=None):
    return pl.pallas_call(
        body,
        in_specs=in_specs or [VM] * len(ins),
        out_specs=out_specs or [VM] * len(outs),
        out_shape=[jax.ShapeDtypeStruct(s, F32) for s in outs],
        scratch_shapes=list(scratch),
        input_output_aliases=aliases or {},
        name=name,
        compiler_params=pltpu.CompilerParams(vmem_limit_bytes=20 * 2**20),
    )(*ins)


def load_kernel(pop_hbm, adj_hbm, ext, mini, za, zb, pops, sems):
    nx = pop_hbm.shape[1]
    lane = lane_ids(16)
    group = lane // 4
    chunks = [(f, min(4, 19 - f)) for f in range(0, 19, 4)]
    copies = []
    for k, (f, n) in enumerate(chunks):
        own = ext.at[pl.ds(f, n), pl.ds(2, nx), pl.ds(0, 16), :]
        copies.append(pltpu.make_async_copy(adj_hbm.at[pl.ds(f, n)], own, sems.at[k]))
    for k, (f, n) in enumerate(chunks):
        copies.append(pltpu.make_async_copy(pop_hbm.at[pl.ds(f, n)], pops.at[pl.ds(f, n)], sems.at[5 + k]))
    for c in copies:
        c.start()

    def edges(f):
        e = lroll(ext[f, 2, pl.ds(0, 16), :], 10)
        for x in range(1, nx):
            e = jnp.where(group == x + 2, lroll(ext[f, x + 2, pl.ds(0, 16), :], 4 * x + 10), e)
        mini[f, pl.ds(0, 16), :] = e

    for k, (f, n) in enumerate(chunks):
        copies[k].wait()
        for i in range(n):
            edges(f + i)
    for c in copies[5:]:
        c.wait()

    def moments(x, _):
        rho = pops[0, x]
        mom = [None] * 3
        for i in range(1, 19):
            p = pops[i, x]
            rho = rho + p
            for k in range(3):
                c = DIRECTIONS[i][k]
                if c:
                    mom[k] = (p if c > 0 else -p) if mom[k] is None else (mom[k] + p if c > 0 else mom[k] - p)
        ext[RHO, x + 2, pl.ds(0, 16), :] = rho
        for k in range(3):
            ext[MOM + k, x + 2, pl.ds(0, 16), :] = mom[k]
        return 0

    lax.fori_loop(0, nx, moments, 0, unroll=2)
    for f in range(RHO, FIELDS):
        edges(f)
    odd = is_odd("gz", 16)
    for t in range(za.shape[0]):
        made = []
        for side in (-1, 1):
            fields = side_fields(2, side)
            acc = None
            for j in range(8 * t, min(8 * t + 8, len(fields))):
                q = j % 8
                b, p = q // 2, q % 2
                v = lroll(mini[fields[j], pl.ds(0, 16), :], 32 * b + 2 * p - (8 if side < 0 else 10))
                acc = v if acc is None else jnp.where((lane // 32 == b) & ((lane % 4) // 2 == p), v, acc)
            made.append(acc)
        za[t] = jnp.where(odd, made[0], made[1])
        zb[t] = jnp.where(odd, made[1], made[0])


def x_kernel(ext, xmsg):
    nx = ext.shape[1] - 4
    for s, side in enumerate((-1, 1)):
        for e, (f, d) in enumerate(side_entries(0, side)):
            plane = (nx + 1 - d) if side < 0 else (2 + d)
            xmsg[s, e] = lroll(ext[f, plane, pl.ds(0, 16), :], -DIRECTIONS[f][2] if f < 19 else 0)


def turn_kernel(ext_in, ext):
    nx = ext.shape[1] - 4
    moving = [i for i in range(19) if DIRECTIONS[i][2]]

    def plane(p, _):
        turned = [lroll(ext_in[i, p, pl.ds(0, 16), :], -DIRECTIONS[i][2]) for i in moving]
        for i, v in zip(moving, turned):
            ext[i, p, pl.ds(0, 16), :] = v
        return 0

    lax.fori_loop(2, nx + 2, plane, 0)


Z_PAIRS = ((5, 6), (11, 13), (14, 12), (15, 17), (18, 16))


def z_ends(above, below):
    return jnp.where(lane_ids(above.shape[0]) % 4 == 0, lroll(above, 62), below)


def close_pairs(p, pairs, ends, ext):
    lane = lane_ids(16)
    found = []
    for (up, down), e in zip(pairs, ends):
        g = lroll(e, 255 - 4 * p)
        found.append((up, jnp.where(lane == 127, g, ext[up, p, pl.ds(0, 16), :])))
        found.append((down, jnp.where(lane == 0, g, ext[down, p, pl.ds(0, 16), :])))
    return found


def zy_kernel(ext_in, mini_in, ra, rb, ext, mini, ya, yb, ends):
    nx = ext.shape[1] - 4
    lane = lane_ids(16)
    for f in range(FIELDS):
        e = mini_in[f, pl.ds(0, 16), :]
        if f == RHO or (f < 19 and DIRECTIONS[f][2] < 0):
            e = jnp.where(lane < 64, e, lroll(e, 64))
        mini[f, pl.ds(0, 16), :] = e
    odd = is_odd("gz", 16)
    for side in (-1, 1):
        msg = [jnp.where(odd, rb[t], ra[t]) if side < 0 else jnp.where(odd, ra[t], rb[t]) for t in range(ra.shape[0])]
        if side < 0:
            keep = (lane >= 8) & (lane < 40) & (lane % 4 < 2)
        else:
            keep = (lane >= 72) & (lane < 104) & (lane % 4 >= 2)
        for j, f in enumerate(side_fields(2, side)):
            q = j % 8
            b, p = q // 2, q % 2
            back = 8 - 32 * b - 2 * p if side < 0 else 74 - 32 * b - 2 * p
            mini[f, pl.ds(0, 16), :] = jnp.where(keep, lroll(msg[j // 8], back), mini[f, pl.ds(0, 16), :])
    for k, (up, down) in enumerate(Z_PAIRS):
        ends[k] = z_ends(mini[up, pl.ds(0, 16), :], mini[down, pl.ds(0, 16), :])

    def close(p, _):
        closed = close_pairs(p, Z_PAIRS, [ends[k] for k in range(len(Z_PAIRS))], ext_in)
        for f, v in closed:
            ext[f, p, pl.ds(0, 16), :] = v
        return 0

    lax.fori_loop(2, nx + 2, close, 0)
    odd = is_odd("gy", 8)
    low, high = side_entries(1, -1), side_entries(1, 1)
    for e in range(len(low)):
        v = ext[low[e][0], pl.ds(2, 8), 15 - low[e][1], :]
        w = ext[high[e][0], pl.ds(2, 8), high[e][1], :]
        ya[pl.ds(8 * e, 8), :] = jnp.where(odd, v, w)
        yb[pl.ds(8 * e, 8), :] = jnp.where(odd, w, v)
    odd = is_odd("gy", 1)
    for e in range(len(low)):
        v = mini[low[e][0], pl.ds(15 - low[e][1], 1), :]
        w = mini[high[e][0], pl.ds(high[e][1], 1), :]
        ya[pl.ds(8 * len(low) + e, 1), :] = jnp.where(odd, v, w)
        yb[pl.ds(8 * len(low) + e, 1), :] = jnp.where(odd, w, v)


def yx_kernel(ext_in, mini_in, ra, rb, ext, mini, xmsg):
    lane = lane_ids(ROWS)
    odd8, odd1 = is_odd("gy", 8), is_odd("gy", 1)
    for side in (-1, 1):
        first, second = (rb, ra) if side < 0 else (ra, rb)
        entries = side_entries(1, side)
        for e, (f, d) in enumerate(entries):
            row = 23 - d if side < 0 else 16 + d
            main, small = pl.ds(8 * e, 8), pl.ds(8 * len(entries) + e, 1)
            ext[f, pl.ds(2, 8), row, :] = jnp.where(odd8, first[main, :], second[main, :])
            mini[f, pl.ds(row, 1), :] = jnp.where(odd1, first[small, :], second[small, :])
    group = (lane % 64) // 4
    for s, side in enumerate((-1, 1)):
        for e, (f, dx, row) in enumerate(edge_entries(side)):
            plane = 9 - dx if side < 0 else 2 + dx
            xmsg[s, pl.ds(e, 1), :] = ext[f, plane, pl.ds(row, 1), :]
        entries = side_entries(0, side)
        for t in range(2):
            acc = None
            for e in range(16 * t, min(16 * t + 16, len(entries))):
                f, d = entries[e]
                v = lroll(mini[f], 4 * (e % 16) - 4 * (9 - d if side < 0 else 2 + d))
                acc = v if acc is None else jnp.where(group == e % 16, v, acc)
            xmsg[s, pl.ds(EDGE_LINES + ROWS * t, ROWS), :] = acc


def cell(b, rho, mom, psi, g):
    pairs = {}
    for i in range(1, 19, 2):
        pairs[i] = (b[i] + b[i + 1], b[i] - b[i + 1])
    s = {i: v[0] for i, v in pairs.items()}
    d = {i: v[1] for i, v in pairs.items()}
    sxy, sxz, syz = s[7] + s[9], s[11] + s[13], s[15] + s[17]
    a0 = W0 * b[0] + W1 * (s[1] + s[3] + s[5]) + W2 * (sxy + sxz + syz)
    a1 = (
        (3 * W1) * d[1] + (3 * W2) * ((d[7] + d[9]) + (d[11] + d[13])),
        (3 * W1) * d[3] + (3 * W2) * ((d[7] - d[9]) + (d[15] + d[17])),
        (3 * W1) * d[5] + (3 * W2) * ((d[11] - d[13]) + (d[15] - d[17])),
    )
    a03 = 3.0 * a0
    bxx = (9 * W1) * s[1] + (9 * W2) * (sxy + sxz) - a03
    byy = (9 * W1) * s[3] + (9 * W2) * (sxy + syz) - a03
    bzz = (9 * W1) * s[5] + (9 * W2) * (sxz + syz) - a03
    bxy = (9 * W2) * (s[7] - s[9])
    bxz = (9 * W2) * (s[11] - s[13])
    byz = (9 * W2) * (s[15] - s[17])
    force = [(-COUPLING * psi) * gk for gk in g]
    inv = 1.0 / rho
    u = [(m + 0.5 * fk) * inv for m, fk in zip(mom, force)]

    def apply(v):
        return (
            bxx * v[0] + bxy * v[1] + bxz * v[2],
            bxy * v[0] + byy * v[1] + byz * v[2],
            bxz * v[0] + byz * v[1] + bzz * v[2],
        )

    w = [p + q for p, q in zip(a1, apply(u))]
    bf = [(KAPPA * inv) * q for q in apply(force)]
    force_bar = [p + 0.5 * q for p, q in zip(w, bf)]
    return a0, a1, u, w, bf, force_bar


def dot(p, q):
    return p[0] * q[0] + p[1] * q[1] + p[2] * q[2]


def mini_adjoint(mini):
    def msh(v, c):
        return lroll(yroll(v, c[1]), -4 * c[0] - c[2])

    psi = 1.0 - jnp.exp(-mini[RHO])
    ys = yroll(psi, 1) + yroll(psi, -1)
    zsum = lroll(psi, -1) + lroll(psi, 1)
    xsum = lroll(psi, -4) + lroll(psi, 4)
    qx = W1 * psi + W2 * (ys + zsum)
    qy = W1 * psi + W2 * (xsum + zsum)
    qz = W1 * psi + W2 * (xsum + ys)
    g = (lroll(qx, -4) - lroll(qx, 4), yroll(qy, 1) - yroll(qy, -1), lroll(qz, -1) - lroll(qz, 1))
    b = [msh(mini[i], DIRECTIONS[i]) for i in range(19)]
    force_bar = cell(b, mini[RHO], [mini[MOM + k] for k in range(3)], psi, g)[5]
    fx, fy, fz = (psi * v for v in force_bar)
    across = W2 * ((lroll(fx, -4) - lroll(fx, 4)) + (yroll(fy, 1) - yroll(fy, -1)))
    along = W1 * fz + W2 * ((lroll(fz, -4) + lroll(fz, 4)) + (yroll(fz, 1) + yroll(fz, -1)))
    return z_ends(psi, psi), z_ends(across + along, across - along)


def zpair(above, below, ends, plane):
    lane = lane_ids(above.shape[0])
    g = lroll(ends, 255 - 4 * plane)
    return jnp.where(lane == 127, g, lroll(above, 127)), jnp.where(lane == 0, g, lroll(below, 1))


def potential(p, ext, ends, psi, zs, zd):
    v = 1.0 - jnp.exp(-ext[RHO, p])
    psi[p] = v
    a, b = zpair(v, v, ends, p)
    zs[p] = a + b
    zd[p] = a - b


def collide(p, ext, psi, zs, zd, flux, out):
    v, xp, xm = psi[p], psi[p + 1], psi[p - 1]
    qxp = W1 * xp + W2 * (yroll(xp, 1) + yroll(xp, -1) + zs[p + 1])
    qxm = W1 * xm + W2 * (yroll(xm, 1) + yroll(xm, -1) + zs[p - 1])
    qy = W1 * v + W2 * (xp + xm + zs[p])
    zz = zd[p]
    g = (
        qxp - qxm,
        yroll(qy, 1) - yroll(qy, -1),
        W1 * zz + W2 * (zd[p + 1] + zd[p - 1] + yroll(zz, 1) + yroll(zz, -1)),
    )
    b = [yroll(ext[i, p + DIRECTIONS[i][0]], DIRECTIONS[i][1]) for i in range(19)]
    a0, a1, u, w, bf, fb = cell(b, ext[RHO, p], [ext[MOM + k, p] for k in range(3)], v, g)
    for k in range(3):
        flux[k, p] = v * fb[k]

    def top(a):
        return a[:16]

    vv = [top(INV_TAU * wk + bk) for wk, bk in zip(w, bf)]
    uu = [top(a) for a in u]
    base = INV_TAU * (top(a0) + 0.5 * dot([top(r + q) for r, q in zip(a1, w)], uu)) - dot(vv, uu)
    base = base + (-COUPLING * (1.0 - top(v))) * top(dot(fb, g))
    for i in range(19):
        o = (1.0 - INV_TAU) * top(b[i]) + base
        for k in range(3):
            if DIRECTIONS[i][k] > 0:
                o = o + vv[k]
            elif DIRECTIONS[i][k] < 0:
                o = o - vv[k]
        out[i, p - 1] = o


def finish(p, psi, flux, ends, out):
    fx, fxm, fy = flux[0, p + 1], flux[0, p - 1], flux[1, p]
    fz = flux[2, p]
    xd = fx - fxm
    fyx = flux[1, p + 1] + flux[1, p - 1]
    dx = xd[:16]
    dy = (yroll(fy, 1) - yroll(fy, -1))[:16]
    here = W1 * (dx + dy) + W2 * (
        (yroll(xd, 1) + yroll(xd, -1))[:16] + (yroll(fyx, 1) - yroll(fyx, -1))[:16]
    )
    across = W2 * (dx + dy)
    along = W1 * fz[:16] + W2 * (flux[2, p + 1, pl.ds(0, 16), :] + flux[2, p - 1, pl.ds(0, 16), :] + (yroll(fz, 1) + yroll(fz, -1))[:16])
    a, b = zpair(across + along, across - along, ends[:16], p)
    term = (COUPLING * (1.0 - psi[p, pl.ds(0, 16), :])) * (here + (a + b))
    for i in range(19):
        out[i, p - 1] = out[i, p - 1] + term


def planes(count, of, step):
    def body(k, _):
        step(of(k))
        return 0

    lax.fori_loop(0, count, body, 0)


def send_plane(out, out_hbm, sems, p):
    return pltpu.make_async_copy(out.at[:, p - 1], out_hbm.at[:, p - 2], sems.at[p - 2])


def mid_kernel(ext, mini, out_hbm, psi, zs, zd, flux, out, sems):
    nx = ext.shape[1] - 4
    psi_ends, flux_ends = mini_adjoint(mini)
    for p in range(2, nx + 2):
        potential(p, ext, psi_ends, psi, zs, zd)
    planes(nx - 2, lambda k: k + 3, lambda p: collide(p, ext, psi, zs, zd, flux, out))

    def done(p):
        finish(p, psi, flux, flux_ends, out)
        send_plane(out, out_hbm, sems, p).start()

    planes(nx - 4, lambda k: k + 4, done)
    for p in range(4, nx):
        send_plane(out, out_hbm, sems, p).wait()


def last_kernel(ext_in, mini_in, r1, r2, psi_in, zs_in, zd_in, flux_in, out_in, hbm_in, ext, mini, psi, zs, zd, flux, out, out_hbm, sems):
    nx = ext.shape[1] - 4
    lane = lane_ids(ROWS)
    group = (lane % 64) // 4
    for s, side in enumerate((-1, 1)):
        entries = side_entries(0, side)
        for e, (f, d) in enumerate(entries):
            plane = 1 - d if side < 0 else nx + 2 + d
            ext[f, plane, pl.ds(0, 16), :] = r1[s, e]
            v = r2[s, pl.ds(EDGE_LINES + ROWS * (e // 16), ROWS), :]
            mini[f] = jnp.where(group == plane, lroll(v, 4 * plane - 4 * (e % 16)), mini[f])
        for e, (f, dx, row) in enumerate(edge_entries(side)):
            plane = 1 - dx if side < 0 else nx + 2 + dx
            ext[f, plane, pl.ds(row, 1), :] = r2[s, pl.ds(e, 1), :]
    ends = [z_ends(mini[up, pl.ds(0, 16), :], mini[down, pl.ds(0, 16), :]) for up, down in Z_PAIRS]
    for p in (0, 1, nx + 2, nx + 3):
        keep = [k for k, (f, _) in enumerate(Z_PAIRS) if DIRECTIONS[f][0] == (-1 if p < 2 else 1) or (p in (1, nx + 2) and DIRECTIONS[f][0] == 0)]
        for f, v in close_pairs(p, [Z_PAIRS[k] for k in keep], [ends[k] for k in keep], ext):
            ext[f, p, pl.ds(0, 16), :] = v
    psi_ends, flux_ends = mini_adjoint(mini)
    for p in (0, 1, nx + 2, nx + 3):
        potential(p, ext, psi_ends, psi, zs, zd)

    def outer(low, k):
        return low + k + jnp.where(k >= 2, nx - 2, 0)

    planes(4, lambda k: outer(1, k), lambda p: collide(p, ext, psi, zs, zd, flux, out))

    def done(p):
        finish(p, psi, flux, flux_ends, out)
        send_plane(out, out_hbm, sems, p).start()

    planes(4, lambda k: outer(2, k) - jnp.where(k >= 2, 2, 0), done)
    for p in (2, 3, nx, nx + 1):
        send_plane(out, out_hbm, sems, p).wait()


def swap(low, high, axis):
    n = lax.axis_size(axis)
    up = [(i, (i + 1) % n) for i in range(n)]
    return lax.ppermute(low, axis, up), lax.ppermute(high, axis, [(j, i) for i, j in up])


def exchange(a, b, axis):
    n = lax.axis_size(axis)
    swaps = [[], []]
    for i in range(n):
        j = (i + 1) % n
        swaps[1 - i % 2] += [(i, j), (j, i)]
    return lax.ppermute(a, axis, swaps[0]), lax.ppermute(b, axis, swaps[1])


def swap_both(msg, axis):
    n = lax.axis_size(axis)
    if n == 2:
        return lax.ppermute(msg, axis, [(0, 1), (1, 0)])
    return jnp.stack(swap(msg[0], msg[1], axis))


def per_device(populations, adjoint_next):
    nx = populations.shape[1]
    ext_shape, mini_shape, plane_shape = (FIELDS, nx + 4, ROWS, 128), (FIELDS, ROWS, 128), (nx + 4, ROWS, 128)
    ext, mini, za, zb = call(
        load_kernel,
        tuple(pltpu.with_memory_space_constraint(v, pltpu.HBM) for v in (populations, adjoint_next)),
        (ext_shape, mini_shape, (3, 16, 128), (3, 16, 128)),
        scratch=[pltpu.VMEM((19, nx, 16, 128), F32), pltpu.SemaphoreType.DMA((10,))],
        in_specs=[HB, HB],
        name="load",
    )
    (xmsg,) = call(x_kernel, (ext,), ((2, 24, 16, 128),), name="xpack")
    x1 = swap_both(xmsg, "gx")
    za, zb = exchange(za, zb, "gz")
    (ext,) = call(turn_kernel, (ext,), (ext_shape,), aliases={0: 0}, name="turn")
    ext, mini, ya, yb = call(
        zy_kernel,
        (ext, mini, za, zb),
        (ext_shape, mini_shape, (24 * 9, 128), (24 * 9, 128)),
        scratch=[pltpu.VMEM((len(Z_PAIRS), 16, 128), F32)],
        aliases={0: 0, 1: 1},
        name="zy",
    )
    ya, yb = exchange(ya, yb, "gy")
    ext, mini, xmsg2 = call(
        yx_kernel,
        (ext, mini, ya, yb),
        (ext_shape, mini_shape, (2, EDGE_LINES + 2 * ROWS, 128)),
        aliases={0: 0, 1: 1},
        name="yx",
    )
    x2 = swap_both(xmsg2, "gx")
    work = (plane_shape, plane_shape, plane_shape, (3, *plane_shape), (19, nx + 2, 16, 128))
    out, *parts = call(
        mid_kernel,
        (ext, mini),
        (populations.shape, *work),
        scratch=[pltpu.SemaphoreType.DMA((nx,))],
        out_specs=[HB] + [VM] * len(work),
        name="mid",
    )
    return call(
        last_kernel,
        (ext, mini, x1, x2, *parts, out),
        (ext_shape, mini_shape, *work, populations.shape),
        scratch=[pltpu.SemaphoreType.DMA((nx,))],
        aliases={0: 0, 1: 1, **{4 + i: 2 + i for i in range(len(work) + 1)}},
        in_specs=[VM] * (4 + len(work)) + [HB],
        out_specs=[VM] * (2 + len(work)) + [HB],
        name="last",
    )[-1]


def solution(mesh):
    return jax.shard_map(
        per_device,
        mesh=mesh,
        in_specs=(P(None, "gx", "gy", "gz"), P(None, "gx", "gy", "gz")),
        out_specs=P(None, "gx", "gy", "gz"),
        check_vma=False,
    )
```

```python
import jax
import jax.numpy as jnp
from jax import lax
from jax.experimental import pallas as pl
from jax.experimental.pallas import tpu as pltpu
from jax.sharding import PartitionSpec as P

DIRECTIONS = (
    (0, 0, 0),
    (1, 0, 0),
    (-1, 0, 0),
    (0, 1, 0),
    (0, -1, 0),
    (0, 0, 1),
    (0, 0, -1),
    (1, 1, 0),
    (-1, -1, 0),
    (1, -1, 0),
    (-1, 1, 0),
    (1, 0, 1),
    (-1, 0, -1),
    (1, 0, -1),
    (-1, 0, 1),
    (0, 1, 1),
    (0, -1, -1),
    (0, 1, -1),
    (0, -1, 1),
)
W0, W1, W2 = 1.0 / 3.0, 1.0 / 18.0, 1.0 / 36.0
RELAX_TIME = 0.8
COUPLING = -5.5
INV_TAU = 1.0 / RELAX_TIME
KAPPA = 1.0 - 0.5 / RELAX_TIME

RHO, MOM, FIELDS = 19, 20, 23
ROWS = 24
F32 = jnp.float32
COSTLY = pl.CostEstimate(flops=10**10, bytes_accessed=10**6, transcendentals=0)
VM = pl.BlockSpec(memory_space=pltpu.VMEM)
HB = pl.BlockSpec(memory_space=pltpu.HBM)


def deep_fields(dim, side):
    return [i for i in range(19) if DIRECTIONS[i][dim] == side] + [RHO]


def side_fields(dim, side):
    return deep_fields(dim, side) + [i for i in range(19) if DIRECTIONS[i][dim] == 0] + [MOM, MOM + 1, MOM + 2]


def side_entries(dim, side):
    return [(f, d) for d in (0, 1) for f in (side_fields(dim, side) if d == 0 else deep_fields(dim, side))]


def edge_entries(side):
    found = []
    for up in (-1, 1):
        for dx in (0, 1):
            for dy in (0, 1):
                row = 23 - dy if up < 0 else 16 + dy
                across = deep_fields(0, side) if dx else side_fields(0, side)
                along = deep_fields(1, up) if dy else side_fields(1, up)
                found += [(f, dx, row) for f in across if f in along]
    return found


def z_pieces(side):
    deep = deep_fields(2, side)
    shallow = side_fields(2, side)[len(deep) :]
    found = [(f, u, 0) for u, f in enumerate(deep)]
    return found + [(f, len(deep) + k // 2, 1 + k % 2) for k, f in enumerate(shallow)]


def z_place(side, unit, kind):
    block, pair = unit % 8 // 2, unit % 2
    start = 32 * block + 2 * pair
    if side < 0:
        shift, slots = start - 8, {0: (0, 1), 1: (1,), 2: (0,)}[kind]
        shift -= kind == 2
    else:
        shift, slots = start - 10, {0: (0, 1), 1: (0,), 2: (1,)}[kind]
        shift += kind == 2
    return block, shift, [2 * pair + k for k in slots]


def x_pieces(side):
    found, group = [], 0
    for d in (0, 1):
        fields = [f for f in (deep_fields(0, side) if d else side_fields(0, side))]
        up = [f for f in fields if f < 19 and DIRECTIONS[f][2] > 0]
        down = [f for f in fields if f < 19 and DIRECTIONS[f][2] < 0]
        flat = [f for f in fields if f > RHO or (f < 19 and DIRECTIONS[f][2] == 0)]
        for a, b in zip(up, down):
            found += [(a, d, group, 0, (2,), (2, 3)), (b, d, group, 0, (0, 1), (1,))]
            group += 1
        for k, f in enumerate(flat):
            found.append((f, d, group + k // 3, k % 3 - 1, (1,), (2,)))
        group += -(-len(flat) // 3)
        found.append((RHO, d, group, 0, (0, 1, 2), (1, 2, 3)))
        group += 1
    assert group <= 16
    return found


def slot_mask(lane, shift, low, high):
    four = lane % 4
    inside = [None, None]
    for half, slots in enumerate((low, high)):
        for k in slots:
            hit = four == k + shift
            inside[half] = hit if inside[half] is None else inside[half] | hit
    return ((lane < 64) & inside[0]) | ((lane >= 64) & inside[1])


EDGE_LINES = -(-len(edge_entries(1)) // 8) * 8


def lane_ids(rows):
    return lax.broadcasted_iota(jnp.int32, (rows, 128), 1)


def lroll(v, amount):
    amount = amount % 128
    return v if isinstance(amount, int) and amount == 0 else pltpu.roll(v, amount, 1)


def yroll(v, c):
    return v if c == 0 else pltpu.roll(v, (-c) % ROWS, 0)


def call(body, ins, outs, scratch=(), aliases=None, name=None, in_specs=None, out_specs=None, cost=None):
    return pl.pallas_call(
        body,
        in_specs=in_specs or [VM] * len(ins),
        out_specs=out_specs or [VM] * len(outs),
        out_shape=[jax.ShapeDtypeStruct(s, F32) for s in outs],
        scratch_shapes=list(scratch),
        input_output_aliases=aliases or {},
        name=name,
        cost_estimate=cost,
        compiler_params=pltpu.CompilerParams(vmem_limit_bytes=20 * 2**20),
    )(*ins)


def load_kernel(pop_hbm, adj_hbm, ext, mini, za, zb, pops, sems):
    nx = pop_hbm.shape[1]
    lane = lane_ids(16)
    group = lane // 4
    chunks = [(f, min(4, 19 - f)) for f in range(0, 19, 4)]
    copies = []
    for k, (f, n) in enumerate(chunks):
        own = ext.at[pl.ds(f, n), pl.ds(2, nx), pl.ds(0, 16), :]
        copies.append(pltpu.make_async_copy(adj_hbm.at[pl.ds(f, n)], own, sems.at[k]))
    for k, (f, n) in enumerate(chunks):
        copies.append(pltpu.make_async_copy(pop_hbm.at[pl.ds(f, n)], pops.at[pl.ds(f, n)], sems.at[5 + k]))
    for c in copies:
        c.start()

    def edges(f):
        e = lroll(ext[f, 2, pl.ds(0, 16), :], 10)
        for x in range(1, nx):
            e = jnp.where(group == x + 2, lroll(ext[f, x + 2, pl.ds(0, 16), :], 4 * x + 10), e)
        mini[f, pl.ds(0, 16), :] = e

    for k, (f, n) in enumerate(chunks):
        copies[k].wait()
        for i in range(n):
            edges(f + i)
    for c in copies[5:]:
        c.wait()

    def moments(x, _):
        rho = pops[0, x]
        mom = [None] * 3
        for i in range(1, 19):
            p = pops[i, x]
            rho = rho + p
            for k in range(3):
                c = DIRECTIONS[i][k]
                if c:
                    mom[k] = (p if c > 0 else -p) if mom[k] is None else (mom[k] + p if c > 0 else mom[k] - p)
        ext[RHO, x + 2, pl.ds(0, 16), :] = rho
        for k in range(3):
            ext[MOM + k, x + 2, pl.ds(0, 16), :] = mom[k]
        return 0

    lax.fori_loop(0, nx, moments, 0, unroll=2)
    for f in range(RHO, FIELDS):
        edges(f)
    for side, msg in ((-1, za), (1, zb)):
        tiles = [None, None]
        for f, unit, kind in z_pieces(side):
            block, shift, slots = z_place(side, unit, kind)
            v = lroll(mini[f, pl.ds(0, 16), :], shift)
            here = lane % 4 == slots[0]
            for k in slots[1:]:
                here = here | (lane % 4 == k)
            t = unit // 8
            tiles[t] = v if tiles[t] is None else jnp.where((lane // 32 == block) & here, v, tiles[t])
        msg[pl.ds(0, 16), :] = tiles[0]
        msg[pl.ds(16, 8), :] = jnp.where(lane[:8] < 64, tiles[1][:8], lroll(tiles[1][8:], 64))


def z_part(f):
    return DIRECTIONS[f][2] if f < 19 else 0


def pack_kernel(ext, xmsg, ya, yb):
    nx = ext.shape[1] - 4
    for s, side in enumerate((-1, 1)):
        for e, (f, d) in enumerate(side_entries(0, side)):
            plane = (nx + 1 - d) if side < 0 else (2 + d)
            xmsg[s, e] = lroll(ext[f, plane, pl.ds(0, 16), :], -z_part(f))
    for side, msg in ((-1, ya), (1, yb)):
        for e, (f, d) in enumerate(side_entries(1, side)):
            msg[pl.ds(8 * e, 8), :] = ext[f, pl.ds(2, 8), 15 - d if side < 0 else d, :]
    for side, msg in ((-1, ya), (1, yb)):
        for e, (f, d) in enumerate(side_entries(1, side)):
            if z_part(f):
                msg[pl.ds(8 * e, 8), :] = lroll(msg[pl.ds(8 * e, 8), :], -z_part(f))


Z_PAIRS = ((5, 6), (11, 13), (14, 12), (15, 17), (18, 16))


def z_ends(above, below):
    return jnp.where(lane_ids(above.shape[0]) % 4 == 0, lroll(above, 62), below)


def close_pairs(p, pairs, ends, ext, rows):
    lane = lane_ids(rows.size)
    found = []
    for (up, down), e in zip(pairs, ends):
        g = lroll(e, 255 - 4 * p)
        found.append((up, jnp.where(lane == 127, g, ext[up, p, rows, :])))
        found.append((down, jnp.where(lane == 0, g, ext[down, p, rows, :])))
    return found


def zy_kernel(mini_in, ra, rb, ya_in, yb_in, mini, ya, yb):
    lane = lane_ids(16)
    for f in range(FIELDS):
        e = mini_in[f, pl.ds(0, 16), :]
        if f == RHO or z_part(f) < 0:
            e = jnp.where(lane < 64, e, lroll(e, 64))
        mini[f, pl.ds(0, 16), :] = e
    for side, msg in ((-1, ra), (1, rb)):
        second = msg[pl.ds(16, 8), :]
        tiles = (msg[pl.ds(0, 16), :], jnp.concatenate([second, lroll(second, 64)], axis=0))
        start, slots = (8, (0, 1)) if side < 0 else (72, (2, 3))
        near = slots[1] if side < 0 else slots[0]
        inside = (lane >= start) & (lane < start + 32)
        for f, unit, kind in z_pieces(side):
            shift = z_place(side, unit, kind)[1]
            keep = inside & ((lane % 4 // 2 == slots[0] // 2) if kind == 0 else (lane % 4 == near))
            v = lroll(tiles[unit // 8], -shift + (0 if side < 0 else 64))
            mini[f, pl.ds(0, 16), :] = jnp.where(keep, v, mini[f, pl.ds(0, 16), :])
    for side, msg in ((-1, ya), (1, yb)):
        entries = side_entries(1, side)
        for e, (f, d) in enumerate(entries):
            msg[pl.ds(8 * len(entries) + e, 1), :] = mini[f, pl.ds(15 - d if side < 0 else d, 1), :]


def turn_kernel(ext_in, mini, ext, ends):
    nx = ext.shape[1] - 4
    lane = lane_ids(16)
    rows = pl.ds(0, 16)
    for k, (up, down) in enumerate(Z_PAIRS):
        ends[k] = z_ends(mini[up, rows, :], mini[down, rows, :])

    def turn(p, _):
        found = []
        for k, (up, down) in enumerate(Z_PAIRS):
            g = lroll(ends[k], 255 - 4 * p)
            found.append((up, jnp.where(lane == 127, g, lroll(ext_in[up, p, rows, :], 127))))
            found.append((down, jnp.where(lane == 0, g, lroll(ext_in[down, p, rows, :], 1))))
        for f, v in found:
            ext[f, p, rows, :] = v
        return 0

    lax.fori_loop(2, nx + 2, turn, 0, unroll=2)


def yx_kernel(ext_in, mini_in, ra, rb, ext, mini, xmsg):
    lane = lane_ids(ROWS)
    for side, msg in ((-1, ra), (1, rb)):
        entries = side_entries(1, side)
        for e, (f, d) in enumerate(entries):
            row = 23 - d if side < 0 else 16 + d
            main, small = pl.ds(8 * e, 8), pl.ds(8 * len(entries) + e, 1)
            ext[f, pl.ds(2, 8), row, :] = msg[main, :]
            mini[f, pl.ds(row, 1), :] = msg[small, :]
    group = (lane % 64) // 4
    for s, side in enumerate((-1, 1)):
        for e, (f, dx, row) in enumerate(edge_entries(side)):
            plane = 9 - dx if side < 0 else 2 + dx
            xmsg[s, pl.ds(e, 1), :] = ext[f, plane, pl.ds(row, 1), :]
        acc = None
        for f, d, g, shift, low, high in x_pieces(side):
            plane = 9 - d if side < 0 else 2 + d
            v = lroll(mini[f], 4 * g - 4 * plane + shift)
            acc = v if acc is None else jnp.where((group == g) & slot_mask(lane, shift, low, high), v, acc)
        xmsg[s, pl.ds(EDGE_LINES, ROWS), :] = acc


def cell(b, rho, mom, psi, g):
    pairs = {}
    for i in range(1, 19, 2):
        pairs[i] = (b[i] + b[i + 1], b[i] - b[i + 1])
    s = {i: v[0] for i, v in pairs.items()}
    d = {i: v[1] for i, v in pairs.items()}
    sxy, sxz, syz = s[7] + s[9], s[11] + s[13], s[15] + s[17]
    a0 = W0 * b[0] + W1 * (s[1] + s[3] + s[5]) + W2 * (sxy + sxz + syz)
    a1 = (
        (3 * W1) * d[1] + (3 * W2) * ((d[7] + d[9]) + (d[11] + d[13])),
        (3 * W1) * d[3] + (3 * W2) * ((d[7] - d[9]) + (d[15] + d[17])),
        (3 * W1) * d[5] + (3 * W2) * ((d[11] - d[13]) + (d[15] - d[17])),
    )
    a03 = 3.0 * a0
    bxx = (9 * W1) * s[1] + (9 * W2) * (sxy + sxz) - a03
    byy = (9 * W1) * s[3] + (9 * W2) * (sxy + syz) - a03
    bzz = (9 * W1) * s[5] + (9 * W2) * (sxz + syz) - a03
    bxy = (9 * W2) * (s[7] - s[9])
    bxz = (9 * W2) * (s[11] - s[13])
    byz = (9 * W2) * (s[15] - s[17])
    force = [(-COUPLING * psi) * gk for gk in g]
    inv = 1.0 / rho
    u = [(m + 0.5 * fk) * inv for m, fk in zip(mom, force)]

    def apply(v):
        return (
            bxx * v[0] + bxy * v[1] + bxz * v[2],
            bxy * v[0] + byy * v[1] + byz * v[2],
            bxz * v[0] + byz * v[1] + bzz * v[2],
        )

    w = [p + q for p, q in zip(a1, apply(u))]
    bf = [(KAPPA * inv) * q for q in apply(force)]
    force_bar = [p + 0.5 * q for p, q in zip(w, bf)]
    return a0, a1, u, w, bf, force_bar


def dot(p, q):
    return p[0] * q[0] + p[1] * q[1] + p[2] * q[2]


def mini_adjoint(mini):
    def msh(v, c):
        return lroll(yroll(v, c[1]), -4 * c[0] - c[2])

    psi = 1.0 - jnp.exp(-mini[RHO])
    ys = yroll(psi, 1) + yroll(psi, -1)
    zsum = lroll(psi, -1) + lroll(psi, 1)
    xsum = lroll(psi, -4) + lroll(psi, 4)
    qx = W1 * psi + W2 * (ys + zsum)
    qy = W1 * psi + W2 * (xsum + zsum)
    qz = W1 * psi + W2 * (xsum + ys)
    g = (lroll(qx, -4) - lroll(qx, 4), yroll(qy, 1) - yroll(qy, -1), lroll(qz, -1) - lroll(qz, 1))
    b = [msh(mini[i], DIRECTIONS[i]) for i in range(19)]
    force_bar = cell(b, mini[RHO], [mini[MOM + k] for k in range(3)], psi, g)[5]
    fx, fy, fz = (psi * v for v in force_bar)
    across = W2 * ((lroll(fx, -4) - lroll(fx, 4)) + (yroll(fy, 1) - yroll(fy, -1)))
    along = W1 * fz + W2 * ((lroll(fz, -4) + lroll(fz, 4)) + (yroll(fz, 1) + yroll(fz, -1)))
    return z_ends(psi, psi), z_ends(across + along, across - along)


def zpair(above, below, ends, plane):
    lane = lane_ids(above.shape[0])
    g = lroll(ends, 255 - 4 * plane)
    return jnp.where(lane == 127, g, lroll(above, 127)), jnp.where(lane == 0, g, lroll(below, 1))


def potential(p, ext, ends, psi, zs, zd):
    v = 1.0 - jnp.exp(-ext[RHO, p])
    psi[p] = v
    a, b = zpair(v, v, ends, p)
    zs[p] = a + b
    zd[p] = a - b


def collide(p, ext, psi, zs, zd, flux, out):
    v, xp, xm = psi[p], psi[p + 1], psi[p - 1]
    qxp = W1 * xp + W2 * (yroll(xp, 1) + yroll(xp, -1) + zs[p + 1])
    qxm = W1 * xm + W2 * (yroll(xm, 1) + yroll(xm, -1) + zs[p - 1])
    qy = W1 * v + W2 * (xp + xm + zs[p])
    zz = zd[p]
    g = (
        qxp - qxm,
        yroll(qy, 1) - yroll(qy, -1),
        W1 * zz + W2 * (zd[p + 1] + zd[p - 1] + yroll(zz, 1) + yroll(zz, -1)),
    )
    b = [yroll(ext[i, p + DIRECTIONS[i][0]], DIRECTIONS[i][1]) for i in range(19)]
    a0, a1, u, w, bf, fb = cell(b, ext[RHO, p], [ext[MOM + k, p] for k in range(3)], v, g)
    for k in range(3):
        flux[k, p] = v * fb[k]

    def top(a):
        return a[:16]

    vv = [top(INV_TAU * wk + bk) for wk, bk in zip(w, bf)]
    uu = [top(a) for a in u]
    base = INV_TAU * (top(a0) + 0.5 * dot([top(r + q) for r, q in zip(a1, w)], uu)) - dot(vv, uu)
    base = base + (-COUPLING * (1.0 - top(v))) * top(dot(fb, g))
    for i in range(19):
        o = (1.0 - INV_TAU) * top(b[i]) + base
        for k in range(3):
            if DIRECTIONS[i][k] > 0:
                o = o + vv[k]
            elif DIRECTIONS[i][k] < 0:
                o = o - vv[k]
        out[i, p - 1] = o


def finish(p, psi, flux, ends, out):
    fx, fxm, fy = flux[0, p + 1], flux[0, p - 1], flux[1, p]
    fz = flux[2, p]
    xd = fx - fxm
    fyx = flux[1, p + 1] + flux[1, p - 1]
    dx = xd[:16]
    dy = (yroll(fy, 1) - yroll(fy, -1))[:16]
    here = W1 * (dx + dy) + W2 * (
        (yroll(xd, 1) + yroll(xd, -1))[:16] + (yroll(fyx, 1) - yroll(fyx, -1))[:16]
    )
    across = W2 * (dx + dy)
    along = W1 * fz[:16] + W2 * (flux[2, p + 1, pl.ds(0, 16), :] + flux[2, p - 1, pl.ds(0, 16), :] + (yroll(fz, 1) + yroll(fz, -1))[:16])
    a, b = zpair(across + along, across - along, ends[:16], p)
    term = (COUPLING * (1.0 - psi[p, pl.ds(0, 16), :])) * (here + (a + b))
    for i in range(19):
        out[i, p - 1] = out[i, p - 1] + term


def planes(count, of, step, unroll=4):
    def body(k, _):
        step(of(k))
        return 0

    lax.fori_loop(0, count, body, 0, unroll=unroll)


def send_plane(out, out_hbm, sems, p):
    return pltpu.make_async_copy(out.at[:, p - 1], out_hbm.at[:, p - 2], sems.at[p - 2])


def mid_kernel(ext_in, mini, ext, out_hbm, psi, zs, zd, flux, out, ends, sems):
    nx = ext.shape[1] - 4
    rows = pl.ds(16, 8)
    for k, (up, down) in enumerate(Z_PAIRS):
        ends[k] = z_ends(mini[up, rows, :], mini[down, rows, :])

    def close(p, _):
        for f, v in close_pairs(p, Z_PAIRS, [ends[k] for k in range(len(Z_PAIRS))], ext_in, rows):
            ext[f, p, rows, :] = v
        return 0

    lax.fori_loop(2, nx + 2, close, 0, unroll=4)
    psi_ends, flux_ends = mini_adjoint(mini)
    for p in range(2, nx + 2):
        potential(p, ext, psi_ends, psi, zs, zd)
    planes(nx - 2, lambda k: k + 3, lambda p: collide(p, ext, psi, zs, zd, flux, out))

    def done(p):
        finish(p, psi, flux, flux_ends, out)
        send_plane(out, out_hbm, sems, p).start()

    planes(nx - 4, lambda k: k + 4, done)
    for p in range(4, nx):
        send_plane(out, out_hbm, sems, p).wait()


def last_kernel(ext_in, mini_in, r1, r2, psi_in, zs_in, zd_in, flux_in, out_in, hbm_in, ext, mini, psi, zs, zd, flux, out, out_hbm, sems):
    nx = ext.shape[1] - 4
    lane = lane_ids(ROWS)
    group = (lane % 64) // 4
    for s, side in enumerate((-1, 1)):
        entries = side_entries(0, side)
        for e, (f, d) in enumerate(entries):
            plane = 1 - d if side < 0 else nx + 2 + d
            ext[f, plane, pl.ds(0, 16), :] = r1[s, e]
        for e, (f, dx, row) in enumerate(edge_entries(side)):
            plane = 1 - dx if side < 0 else nx + 2 + dx
            ext[f, plane, pl.ds(row, 1), :] = r2[s, pl.ds(e, 1), :]
        small = r2[s, pl.ds(EDGE_LINES, ROWS), :]
        for f, d, g, shift, low, high in x_pieces(side):
            plane = 1 - d if side < 0 else nx + 2 + d
            keep = (group == plane) & slot_mask(lane, 0, low, high)
            mini[f] = jnp.where(keep, lroll(small, 4 * plane - 4 * g - shift), mini[f])
    rows = pl.ds(0, ROWS)
    ends = [z_ends(mini[up], mini[down]) for up, down in Z_PAIRS]
    for p in (0, 1, nx + 2, nx + 3):
        keep = [k for k, (f, _) in enumerate(Z_PAIRS) if DIRECTIONS[f][0] == (-1 if p < 2 else 1) or (p in (1, nx + 2) and DIRECTIONS[f][0] == 0)]
        for f, v in close_pairs(p, [Z_PAIRS[k] for k in keep], [ends[k] for k in keep], ext, rows):
            ext[f, p] = v
    psi_ends, flux_ends = mini_adjoint(mini)
    for p in (0, 1, nx + 2, nx + 3):
        potential(p, ext, psi_ends, psi, zs, zd)

    def outer(low, k):
        return low + k + jnp.where(k >= 2, nx - 2, 0)

    def done(p):
        finish(p, psi, flux, flux_ends, out)
        send_plane(out, out_hbm, sems, p).start()

    planes(4, lambda k: outer(1, k), lambda p: collide(p, ext, psi, zs, zd, flux, out))
    planes(4, lambda k: outer(2, k) - jnp.where(k >= 2, 2, 0), done)
    for p in (2, 3, nx, nx + 1):
        send_plane(out, out_hbm, sems, p).wait()


def swap(low, high, axis):
    n = lax.axis_size(axis)
    up = [(i, (i + 1) % n) for i in range(n)]
    return lax.ppermute(low, axis, up), lax.ppermute(high, axis, [(j, i) for i, j in up])


def swap_both(msg, axis):
    n = lax.axis_size(axis)
    if n == 2:
        return lax.ppermute(msg, axis, [(0, 1), (1, 0)])
    return jnp.stack(swap(msg[0], msg[1], axis))


def per_device(populations, adjoint_next):
    nx = populations.shape[1]
    ext_shape, mini_shape, plane_shape = (FIELDS, nx + 4, ROWS, 128), (FIELDS, ROWS, 128), (nx + 4, ROWS, 128)
    ext, mini, za, zb = call(
        load_kernel,
        tuple(pltpu.with_memory_space_constraint(v, pltpu.HBM) for v in (populations, adjoint_next)),
        (ext_shape, mini_shape, (24, 128), (24, 128)),
        scratch=[pltpu.VMEM((19, nx, 16, 128), F32), pltpu.SemaphoreType.DMA((10,))],
        in_specs=[HB, HB],
        name="load",
    )
    xmsg, ya, yb = call(
        pack_kernel, (ext,), ((2, 24, 16, 128), (24 * 9, 128), (24 * 9, 128)), name="pack", cost=COSTLY
    )
    x1 = swap_both(xmsg, "gx")
    za, zb = swap(za, zb, "gz")
    mini, ya, yb = call(
        zy_kernel,
        (mini, za, zb, ya, yb),
        (mini_shape, ya.shape, yb.shape),
        aliases={0: 0, 3: 1, 4: 2},
        name="zy",
    )
    ya, yb = swap(ya, yb, "gy")
    (ext,) = call(
        turn_kernel,
        (ext, mini),
        (ext_shape,),
        scratch=[pltpu.VMEM((len(Z_PAIRS), 16, 128), F32)],
        aliases={0: 0},
        name="turn",
        cost=COSTLY,
    )
    ext, mini, xmsg2 = call(
        yx_kernel,
        (ext, mini, ya, yb),
        (ext_shape, mini_shape, (2, EDGE_LINES + ROWS, 128)),
        aliases={0: 0, 1: 1},
        name="yx",
    )
    x2 = swap_both(xmsg2, "gx")
    work = (plane_shape, plane_shape, plane_shape, (3, *plane_shape), (19, nx + 2, 16, 128))
    ext, out, *parts = call(
        mid_kernel,
        (ext, mini),
        (ext_shape, populations.shape, *work),
        scratch=[pltpu.VMEM((len(Z_PAIRS), 8, 128), F32), pltpu.SemaphoreType.DMA((nx,))],
        aliases={0: 0},
        out_specs=[VM, HB] + [VM] * len(work),
        name="mid",
    )
    return call(
        last_kernel,
        (ext, mini, x1, x2, *parts, out),
        (ext_shape, mini_shape, *work, populations.shape),
        scratch=[pltpu.SemaphoreType.DMA((nx,))],
        aliases={0: 0, 1: 1, **{4 + i: 2 + i for i in range(len(work) + 1)}},
        in_specs=[VM] * (4 + len(work)) + [HB],
        out_specs=[VM] * (2 + len(work)) + [HB],
        name="last",
    )[-1]


def solution(mesh):
    return jax.shard_map(
        per_device,
        mesh=mesh,
        in_specs=(P(None, "gx", "gy", "gz"), P(None, "gx", "gy", "gz")),
        out_specs=P(None, "gx", "gy", "gz"),
        check_vma=False,
    )
```

```python
import jax
import jax.numpy as jnp
from jax import lax
from jax.experimental import pallas as pl
from jax.experimental.pallas import tpu as pltpu
from jax.sharding import PartitionSpec as P

DIRECTIONS = (
    (0, 0, 0),
    (1, 0, 0),
    (-1, 0, 0),
    (0, 1, 0),
    (0, -1, 0),
    (0, 0, 1),
    (0, 0, -1),
    (1, 1, 0),
    (-1, -1, 0),
    (1, -1, 0),
    (-1, 1, 0),
    (1, 0, 1),
    (-1, 0, -1),
    (1, 0, -1),
    (-1, 0, 1),
    (0, 1, 1),
    (0, -1, -1),
    (0, 1, -1),
    (0, -1, 1),
)
W0, W1, W2 = 1.0 / 3.0, 1.0 / 18.0, 1.0 / 36.0
RELAX_TIME = 0.8
COUPLING = -5.5
INV_TAU = 1.0 / RELAX_TIME
KAPPA = 1.0 - 0.5 / RELAX_TIME

RHO, MOM, FIELDS = 19, 20, 23
ROWS = 24
F32 = jnp.float32
COSTLY = pl.CostEstimate(flops=10**10, bytes_accessed=10**6, transcendentals=0)
VM = pl.BlockSpec(memory_space=pltpu.VMEM)
HB = pl.BlockSpec(memory_space=pltpu.HBM)


def deep_fields(dim, side):
    return [i for i in range(19) if DIRECTIONS[i][dim] == side] + [RHO]


def side_fields(dim, side):
    return deep_fields(dim, side) + [i for i in range(19) if DIRECTIONS[i][dim] == 0] + [MOM, MOM + 1, MOM + 2]


def side_entries(dim, side):
    return [(f, d) for d in (0, 1) for f in (side_fields(dim, side) if d == 0 else deep_fields(dim, side))]


def edge_entries(side, up):
    found = []
    for dx in (0, 1):
        for dy in (0, 1):
            across = deep_fields(0, side) if dx else side_fields(0, side)
            along = deep_fields(1, up) if dy else side_fields(1, up)
            found += [(f, dx, dy) for f in across if f in along]
    return sorted(found, key=lambda entry: z_part(entry[0]))


def z_pieces(side):
    deep = deep_fields(2, side)
    shallow = side_fields(2, side)[len(deep) :]
    found = [(f, u, 0) for u, f in enumerate(deep)]
    return found + [(f, len(deep) + k // 2, 1 + k % 2) for k, f in enumerate(shallow)]


def z_place(side, unit, kind):
    block, pair = unit % 8 // 2, unit % 2
    start = 32 * block + 2 * pair
    if side < 0:
        shift, slots = start - 8, {0: (0, 1), 1: (1,), 2: (0,)}[kind]
        shift -= kind == 2
    else:
        shift, slots = start - 10, {0: (0, 1), 1: (0,), 2: (1,)}[kind]
        shift += kind == 2
    return block, shift, [2 * pair + k for k in slots]


def x_units(side):
    found, group = [], 0
    deep = deep_fields(0, side)
    for depths, fields in ((2, deep), (1, side_fields(0, side)[len(deep) :])):
        up = [f for f in fields if z_part(f) > 0]
        down = [f for f in fields if z_part(f) < 0]
        flat = [f for f in fields if f != RHO and z_part(f) == 0]
        sets = [[(0, ((a, (2,), (2, 3)), (b, (0, 1), (1,))))] for a, b in zip(up, down)]
        for k in range(0, len(flat), 3):
            sets.append([(n - 1, ((f, (1,), (2,)),)) for n, f in enumerate(flat[k : k + 3])])
        if RHO in fields:
            sets.append([(0, ((RHO, (0, 1, 2), (1, 2, 3)),))])
        for units in sets:
            groups = (group,) if depths == 1 else (group + 1, group) if side < 0 else (group, group + 1)
            found += [(groups, shift, parts) for shift, parts in units]
            group += depths
    assert group <= 16
    return found


def any_group(group, groups):
    hit = group == groups[0]
    for g in groups[1:]:
        hit = hit | (group == g)
    return hit


def slot_mask(lane, shift, low, high):
    four = lane % 4
    inside = [None, None]
    for half, slots in enumerate((low, high)):
        for k in slots:
            hit = four == k + shift
            inside[half] = hit if inside[half] is None else inside[half] | hit
    return ((lane < 64) & inside[0]) | ((lane >= 64) & inside[1])


def z_part(f):
    return DIRECTIONS[f][2] if f < 19 else 0


CORNER = len(edge_entries(1, 1))
EDGE_LINES = -(-(2 * CORNER + 4) // 8) * 8


def lane_ids(rows):
    return lax.broadcasted_iota(jnp.int32, (rows, 128), 1)


def lroll(v, amount):
    amount = amount % 128
    return v if isinstance(amount, int) and amount == 0 else pltpu.roll(v, amount, 1)


def yroll(v, c):
    return v if c == 0 else pltpu.roll(v, (-c) % ROWS, 0)


def call(body, ins, outs, scratch=(), aliases=None, name=None, in_specs=None, out_specs=None, cost=None):
    return pl.pallas_call(
        body,
        in_specs=in_specs or [VM] * len(ins),
        out_specs=out_specs or [VM] * len(outs),
        out_shape=[jax.ShapeDtypeStruct(s, F32) for s in outs],
        scratch_shapes=list(scratch),
        input_output_aliases=aliases or {},
        name=name,
        cost_estimate=cost,
        compiler_params=pltpu.CompilerParams(vmem_limit_bytes=20 * 2**20),
    )(*ins)


def load_kernel(pop_hbm, adj_hbm, ext, mini, ya, yb, pops, sems):
    nx = pop_hbm.shape[1]
    lane = lane_ids(16)
    group = lane // 4
    chunks = [(f, min(4, 19 - f)) for f in range(0, 19, 4)]
    copies = []
    for k, (f, n) in enumerate(chunks):
        own = ext.at[pl.ds(f, n), pl.ds(2, nx), pl.ds(0, 16), :]
        copies.append(pltpu.make_async_copy(adj_hbm.at[pl.ds(f, n)], own, sems.at[k]))
    for k, (f, n) in enumerate(chunks):
        copies.append(pltpu.make_async_copy(pop_hbm.at[pl.ds(f, n)], pops.at[pl.ds(f, n)], sems.at[5 + k]))
    for c in copies:
        c.start()

    def edges(f):
        e = lroll(ext[f, 2, pl.ds(0, 16), :], 10)
        for x in range(1, nx):
            e = jnp.where(group == x + 2, lroll(ext[f, x + 2, pl.ds(0, 16), :], 4 * x + 10), e)
        mini[f, pl.ds(0, 16), :] = e

    for k, (f, n) in enumerate(chunks):
        copies[k].wait()
        for i in range(n):
            edges(f + i)
    for c in copies[5:]:
        c.wait()

    def moments(x, _):
        rho = pops[0, x]
        mom = [None] * 3
        for i in range(1, 19):
            p = pops[i, x]
            rho = rho + p
            for k in range(3):
                c = DIRECTIONS[i][k]
                if c:
                    mom[k] = (p if c > 0 else -p) if mom[k] is None else (mom[k] + p if c > 0 else mom[k] - p)
        ext[RHO, x + 2, pl.ds(0, 16), :] = rho
        for k in range(3):
            ext[MOM + k, x + 2, pl.ds(0, 16), :] = mom[k]
        return 0

    lax.fori_loop(0, nx, moments, 0, unroll=2)
    for f in range(RHO, FIELDS):
        edges(f)
    place = lax.broadcasted_iota(jnp.int32, (EDGE_LINES, 128), 0)
    for up, msg in ((-1, ya), (1, yb)):
        entries = side_entries(1, up)
        for e, (f, d) in enumerate(entries):
            msg[pl.ds(e, 1), :] = mini[f, pl.ds(15 - d if up < 0 else d, 1), :]
        lines = [(side, *entry) for side in (-1, 1) for entry in edge_entries(side, up)]
        for e, (side, f, dx, dy) in enumerate(lines):
            plane = nx + 1 - dx if side < 0 else 2 + dx
            msg[pl.ds(len(entries) + e, 1), :] = ext[f, plane, pl.ds(15 - dy if up < 0 else dy, 1), :]
        v = msg[pl.ds(len(entries), EDGE_LINES), :]
        turned = v
        for step in (-1, 1):
            here = None
            for k in (0, 1):
                hits = [e for e in range(CORNER) if z_part(lines[CORNER * k + e][1]) == step]
                hit = (place >= CORNER * k + hits[0]) & (place <= CORNER * k + hits[-1])
                here = hit if here is None else here | hit
            turned = jnp.where(here, lroll(v, -step), turned)
        msg[pl.ds(len(entries), EDGE_LINES), :] = turned


def x_kernel(ext, xmsg):
    nx = ext.shape[1] - 4
    for s, side in enumerate((-1, 1)):
        for e, (f, d) in enumerate(side_entries(0, side)):
            plane = (nx + 1 - d) if side < 0 else (2 + d)
            xmsg[s, e] = lroll(ext[f, plane, pl.ds(0, 16), :], -z_part(f))


def yz_kernel(mini_in, ra, rb, mini, za, zb):
    lane = lane_ids(ROWS)
    for side, msg in ((-1, ra), (1, rb)):
        entries = side_entries(1, side)
        for e, (f, d) in enumerate(entries):
            mini[f, pl.ds(23 - d if side < 0 else 16 + d, 1), :] = msg[pl.ds(e, 1), :]
    for side, msg in ((-1, za), (1, zb)):
        tiles = [None, None]
        for f, unit, kind in z_pieces(side):
            block, shift, slots = z_place(side, unit, kind)
            v = lroll(mini[f], shift)
            here = lane % 4 == slots[0]
            for k in slots[1:]:
                here = here | (lane % 4 == k)
            t = unit // 8
            tiles[t] = v if tiles[t] is None else jnp.where((lane // 32 == block) & here, v, tiles[t])
        msg[pl.ds(0, ROWS), :] = tiles[0]
        msg[pl.ds(ROWS, 8), :] = jnp.where(lane[:8] < 64, tiles[1][:8], lroll(tiles[1][8:16], 64))
        msg[pl.ds(ROWS + 8, 8), :] = tiles[1][16:]


def y_entries(side):
    found = []
    for f, d in side_entries(1, side):
        cx = DIRECTIONS[f][0] if f < 19 else 0
        found.append((f, d, 3 + cx))
    return sorted(found, key=lambda entry: z_part(entry[0]))


def y_kernel(ext, mini, ya, yb):
    for side, msg in ((-1, ya), (1, yb)):
        entries = y_entries(side)
        six = ext.shape[1] - 6
        msg[pl.ds(six * len(entries), 8), :] = jnp.zeros((8, 128), F32)
        for e, (f, d, first) in enumerate(entries):
            msg[pl.ds(six * e, six), :] = ext[f, pl.ds(first, six), 15 - d if side < 0 else d, :]
        for step in (-1, 1):
            hits = [e for e, (f, _, _) in enumerate(entries) if z_part(f) == step]
            start, stop = six * hits[0], six * (hits[-1] + 1)
            low, high = start // 8 * 8, -(-stop // 8) * 8
            v = msg[pl.ds(low, high - low), :]
            place = low + lax.broadcasted_iota(jnp.int32, v.shape, 0)
            msg[pl.ds(low, high - low), :] = jnp.where((place >= start) & (place < stop), lroll(v, -step), v)


Z_PAIRS = ((5, 6), (11, 13), (14, 12), (15, 17), (18, 16))


def z_ends(above, below):
    return jnp.where(lane_ids(above.shape[0]) % 4 == 0, lroll(above, 62), below)


def close_pairs(p, pairs, ends, ext, rows):
    lane = lane_ids(rows.size)
    found = []
    for (up, down), e in zip(pairs, ends):
        g = lroll(e, 255 - 4 * p)
        found.append((up, jnp.where(lane == 127, g, ext[up, p, rows, :])))
        found.append((down, jnp.where(lane == 0, g, ext[down, p, rows, :])))
    return found


def zx_kernel(mini_in, ra, rb, ya, yb, mini, xmsg):
    lane = lane_ids(ROWS)
    for f in range(FIELDS):
        e = mini_in[f]
        if f == RHO or z_part(f) < 0:
            e = jnp.where(lane < 64, e, lroll(e, 64))
        mini[f] = e
    for side, msg in ((-1, ra), (1, rb)):
        second = msg[pl.ds(ROWS, 8), :]
        tiles = (msg[pl.ds(0, ROWS), :], jnp.concatenate([second, lroll(second, 64), msg[pl.ds(ROWS + 8, 8), :]], axis=0))
        start, slots = (8, (0, 1)) if side < 0 else (72, (2, 3))
        near = slots[1] if side < 0 else slots[0]
        inside = (lane >= start) & (lane < start + 32)
        for f, unit, kind in z_pieces(side):
            shift = z_place(side, unit, kind)[1]
            keep = inside & ((lane % 4 // 2 == slots[0] // 2) if kind == 0 else (lane % 4 == near))
            v = lroll(tiles[unit // 8], -shift + (0 if side < 0 else 64))
            mini[f] = jnp.where(keep, v, mini[f])
    group = (lane % 64) // 4
    for s, side in enumerate((-1, 1)):
        acc = None
        for groups, shift, parts in x_units(side):
            v = mini[parts[0][0]]
            for f, low, high in parts[1:]:
                v = jnp.where(slot_mask(lane, 0, low, high), mini[f], v)
            v = lroll(v, 4 * groups[0] - 4 * (9 if side < 0 else 2) + shift)
            if acc is None:
                acc = v
            else:
                here = any_group(group, groups)
                if parts[0][1:] == ((1,), (2,)):
                    here = here & slot_mask(lane, shift, (1,), (2,))
                acc = jnp.where(here, v, acc)
        xmsg[s, pl.ds(EDGE_LINES - 8, 8), :] = pltpu.roll(acc[16:], 6, 0)
        xmsg[s, pl.ds(EDGE_LINES, 16), :] = acc[:16]
        for k, msg in enumerate((ya, yb)):
            start = len(side_entries(1, 1)) + CORNER * s
            xmsg[s, pl.ds(CORNER * k, CORNER), :] = msg[pl.ds(start, CORNER), :]


def turn_kernel(ext_in, mini, ext, psi_ends, flux_ends, psi, zs, zd, ends):
    nx = ext.shape[1] - 4
    lane = lane_ids(16)
    rows = pl.ds(0, 16)
    for k, (up, down) in enumerate(Z_PAIRS):
        ends[k] = z_ends(mini[up, rows, :], mini[down, rows, :])

    def turn(p, _):
        found = []
        for k, (up, down) in enumerate(Z_PAIRS):
            g = lroll(ends[k], 255 - 4 * p)
            found.append((up, jnp.where(lane == 127, g, lroll(ext_in[up, p, rows, :], 127))))
            found.append((down, jnp.where(lane == 0, g, lroll(ext_in[down, p, rows, :], 1))))
        for f, v in found:
            ext[f, p, rows, :] = v
        return 0

    lax.fori_loop(2, nx + 2, turn, 0, unroll=2)
    psi_ends[...], flux_ends[...] = mini_adjoint(mini)
    for p in range(2, nx + 2):
        potential(p, ext, psi_ends, psi, zs, zd, rows)


def cell(b, rho, mom, psi, g):
    pairs = {}
    for i in range(1, 19, 2):
        pairs[i] = (b[i] + b[i + 1], b[i] - b[i + 1])
    s = {i: v[0] for i, v in pairs.items()}
    d = {i: v[1] for i, v in pairs.items()}
    sxy, sxz, syz = s[7] + s[9], s[11] + s[13], s[15] + s[17]
    a0 = W0 * b[0] + W1 * (s[1] + s[3] + s[5]) + W2 * (sxy + sxz + syz)
    a1 = (
        (3 * W1) * d[1] + (3 * W2) * ((d[7] + d[9]) + (d[11] + d[13])),
        (3 * W1) * d[3] + (3 * W2) * ((d[7] - d[9]) + (d[15] + d[17])),
        (3 * W1) * d[5] + (3 * W2) * ((d[11] - d[13]) + (d[15] - d[17])),
    )
    a03 = 3.0 * a0
    bxx = (9 * W1) * s[1] + (9 * W2) * (sxy + sxz) - a03
    byy = (9 * W1) * s[3] + (9 * W2) * (sxy + syz) - a03
    bzz = (9 * W1) * s[5] + (9 * W2) * (sxz + syz) - a03
    bxy = (9 * W2) * (s[7] - s[9])
    bxz = (9 * W2) * (s[11] - s[13])
    byz = (9 * W2) * (s[15] - s[17])
    force = [(-COUPLING * psi) * gk for gk in g]
    inv = 1.0 / rho
    u = [(m + 0.5 * fk) * inv for m, fk in zip(mom, force)]

    def apply(v):
        return (
            bxx * v[0] + bxy * v[1] + bxz * v[2],
            bxy * v[0] + byy * v[1] + byz * v[2],
            bxz * v[0] + byz * v[1] + bzz * v[2],
        )

    w = [p + q for p, q in zip(a1, apply(u))]
    bf = [(KAPPA * inv) * q for q in apply(force)]
    force_bar = [p + 0.5 * q for p, q in zip(w, bf)]
    return a0, a1, u, w, bf, force_bar


def dot(p, q):
    return p[0] * q[0] + p[1] * q[1] + p[2] * q[2]


def mini_adjoint(mini):
    def msh(v, c):
        return lroll(yroll(v, c[1]), -4 * c[0] - c[2])

    psi = 1.0 - jnp.exp(-mini[RHO])
    ys = yroll(psi, 1) + yroll(psi, -1)
    zsum = lroll(psi, -1) + lroll(psi, 1)
    xsum = lroll(psi, -4) + lroll(psi, 4)
    qx = W1 * psi + W2 * (ys + zsum)
    qy = W1 * psi + W2 * (xsum + zsum)
    qz = W1 * psi + W2 * (xsum + ys)
    g = (lroll(qx, -4) - lroll(qx, 4), yroll(qy, 1) - yroll(qy, -1), lroll(qz, -1) - lroll(qz, 1))
    b = [msh(mini[i], DIRECTIONS[i]) for i in range(19)]
    force_bar = cell(b, mini[RHO], [mini[MOM + k] for k in range(3)], psi, g)[5]
    fx, fy, fz = (psi * v for v in force_bar)
    across = W2 * ((lroll(fx, -4) - lroll(fx, 4)) + (yroll(fy, 1) - yroll(fy, -1)))
    along = W1 * fz + W2 * ((lroll(fz, -4) + lroll(fz, 4)) + (yroll(fz, 1) + yroll(fz, -1)))
    return z_ends(psi, psi), z_ends(across + along, across - along)


def zpair(above, below, ends, plane):
    lane = lane_ids(above.shape[0])
    g = lroll(ends, 255 - 4 * plane)
    return jnp.where(lane == 127, g, lroll(above, 127)), jnp.where(lane == 0, g, lroll(below, 1))


def potential(p, ext, ends, psi, zs, zd, rows):
    v = 1.0 - jnp.exp(-ext[RHO, p, rows, :])
    psi[p, rows, :] = v
    a, b = zpair(v, v, ends[rows, :], p)
    zs[p, rows, :] = a + b
    zd[p, rows, :] = a - b


def collide(p, ext, psi, zs, zd, flux, out):
    v, xp, xm = psi[p], psi[p + 1], psi[p - 1]
    qxp = W1 * xp + W2 * (yroll(xp, 1) + yroll(xp, -1) + zs[p + 1])
    qxm = W1 * xm + W2 * (yroll(xm, 1) + yroll(xm, -1) + zs[p - 1])
    qy = W1 * v + W2 * (xp + xm + zs[p])
    zz = zd[p]
    g = (
        qxp - qxm,
        yroll(qy, 1) - yroll(qy, -1),
        W1 * zz + W2 * (zd[p + 1] + zd[p - 1] + yroll(zz, 1) + yroll(zz, -1)),
    )
    b = [yroll(ext[i, p + DIRECTIONS[i][0]], DIRECTIONS[i][1]) for i in range(19)]
    a0, a1, u, w, bf, fb = cell(b, ext[RHO, p], [ext[MOM + k, p] for k in range(3)], v, g)
    for k in range(3):
        flux[k, p] = v * fb[k]

    def top(a):
        return a[:16]

    vv = [top(INV_TAU * wk + bk) for wk, bk in zip(w, bf)]
    uu = [top(a) for a in u]
    base = INV_TAU * (top(a0) + 0.5 * dot([top(r + q) for r, q in zip(a1, w)], uu)) - dot(vv, uu)
    base = base + (-COUPLING * (1.0 - top(v))) * top(dot(fb, g))
    for i in range(19):
        o = (1.0 - INV_TAU) * top(b[i]) + base
        for k in range(3):
            if DIRECTIONS[i][k] > 0:
                o = o + vv[k]
            elif DIRECTIONS[i][k] < 0:
                o = o - vv[k]
        out[i, p - 1] = o


def finish(p, psi, flux, ends, out):
    fx, fxm, fy = flux[0, p + 1], flux[0, p - 1], flux[1, p]
    fz = flux[2, p]
    xd = fx - fxm
    fyx = flux[1, p + 1] + flux[1, p - 1]
    dx = xd[:16]
    dy = (yroll(fy, 1) - yroll(fy, -1))[:16]
    here = W1 * (dx + dy) + W2 * (
        (yroll(xd, 1) + yroll(xd, -1))[:16] + (yroll(fyx, 1) - yroll(fyx, -1))[:16]
    )
    across = W2 * (dx + dy)
    along = W1 * fz[:16] + W2 * (flux[2, p + 1, pl.ds(0, 16), :] + flux[2, p - 1, pl.ds(0, 16), :] + (yroll(fz, 1) + yroll(fz, -1))[:16])
    a, b = zpair(across + along, across - along, ends[pl.ds(0, 16), :], p)
    term = (COUPLING * (1.0 - psi[p, pl.ds(0, 16), :])) * (here + (a + b))
    for i in range(19):
        out[i, p - 1] = out[i, p - 1] + term


def planes(count, of, step, unroll=4):
    def body(k, _):
        step(of(k))
        return 0

    lax.fori_loop(0, count, body, 0, unroll=unroll)


def send_plane(out, out_hbm, sems, p):
    return pltpu.make_async_copy(out.at[:, p - 1], out_hbm.at[:, p - 2], sems.at[p - 2])


def mid_kernel(ext_in, mini, sa, sb, ra, rb, psi_ends, flux_ends, psi_in, zs_in, zd_in, ext, out_hbm, psi, zs, zd, flux, out, ends, sems):
    nx = ext.shape[1] - 4
    rows = pl.ds(16, 8)
    for up, small, large in ((-1, sa, ra), (1, sb, rb)):
        for e, (f, d, first) in enumerate(y_entries(up)):
            ext[f, pl.ds(first, nx - 2), 23 - d if up < 0 else 16 + d, :] = large[pl.ds((nx - 2) * e, nx - 2), :]
        lines = [(side, *entry) for side in (-1, 1) for entry in edge_entries(side, up)]
        for e, (side, f, dx, dy) in enumerate(lines):
            plane, row = nx + 1 - dx if side < 0 else 2 + dx, 23 - dy if up < 0 else 16 + dy
            ext[f, plane, pl.ds(row, 1), :] = small[pl.ds(len(side_entries(1, up)) + e, 1), :]
    for k, (up, down) in enumerate(Z_PAIRS):
        ends[k] = z_ends(mini[up, rows, :], mini[down, rows, :])

    def close(p, _):
        for f, v in close_pairs(p, Z_PAIRS, [ends[k] for k in range(len(Z_PAIRS))], ext, rows):
            ext[f, p, rows, :] = v
        return 0

    lax.fori_loop(2, nx + 2, close, 0, unroll=4)
    for p in range(2, nx + 2):
        potential(p, ext, psi_ends, psi, zs, zd, rows)
    planes(nx - 2, lambda k: k + 3, lambda p: collide(p, ext, psi, zs, zd, flux, out))

    def done(p):
        finish(p, psi, flux, flux_ends, out)
        send_plane(out, out_hbm, sems, p).start()

    planes(nx - 4, lambda k: k + 4, done)
    for p in range(4, nx):
        send_plane(out, out_hbm, sems, p).wait()


def fill_kernel(ext_in, r1, ext):
    nx = ext.shape[1] - 4
    for s, side in enumerate((-1, 1)):
        for e, (f, d) in enumerate(side_entries(0, side)):
            ext[f, 1 - d if side < 0 else nx + 2 + d, pl.ds(0, 16), :] = r1[s, e]


def last_kernel(ext_in, mini_in, r2, psi_in, zs_in, zd_in, flux_in, out_in, hbm_in, ext, mini, psi, zs, zd, flux, out, out_hbm, psi_ends, flux_ends, sems):
    nx = ext.shape[1] - 4
    lane = lane_ids(ROWS)
    group = (lane % 64) // 4
    for s, side in enumerate((-1, 1)):
        lines = [(up, *entry) for up in (-1, 1) for entry in edge_entries(side, up)]
        for e, (up, f, dx, dy) in enumerate(lines):
            plane, row = 1 - dx if side < 0 else nx + 2 + dx, 23 - dy if up < 0 else 16 + dy
            ext[f, plane, pl.ds(row, 1), :] = r2[s, pl.ds(e, 1), :]
        small = jnp.concatenate([r2[s, pl.ds(EDGE_LINES, 16), :], pltpu.roll(r2[s, pl.ds(EDGE_LINES - 8, 8), :], 2, 0)], axis=0)
        for groups, shift, parts in x_units(side):
            near = 1 if side < 0 else nx + 2
            here = any_group(group, (near, near + side)[: len(groups)])
            v = lroll(small, 4 * near - 4 * groups[0] - shift)
            for f, low, high in parts:
                mini[f] = jnp.where(here & slot_mask(lane, 0, low, high), v, mini[f])
    ends = [z_ends(mini[up], mini[down]) for up, down in Z_PAIRS]
    for p in (0, 1, nx + 2, nx + 3):
        keep = [k for k, (f, _) in enumerate(Z_PAIRS) if DIRECTIONS[f][0] == (-1 if p < 2 else 1) or (p in (1, nx + 2) and DIRECTIONS[f][0] == 0)]
        for f, v in close_pairs(p, [Z_PAIRS[k] for k in keep], [ends[k] for k in keep], ext, pl.ds(0, ROWS)):
            ext[f, p] = v
    psi_ends[...], flux_ends[...] = mini_adjoint(mini)
    for p in (0, 1, nx + 2, nx + 3):
        potential(p, ext, psi_ends, psi, zs, zd, pl.ds(0, ROWS))

    def outer(low, k):
        return low + k + jnp.where(k >= 2, nx - 2, 0)

    def done(p):
        finish(p, psi, flux, flux_ends, out)
        send_plane(out, out_hbm, sems, p).start()

    planes(4, lambda k: outer(1, k), lambda p: collide(p, ext, psi, zs, zd, flux, out))
    planes(4, lambda k: outer(2, k) - jnp.where(k >= 2, 2, 0), done)
    for p in (2, 3, nx, nx + 1):
        send_plane(out, out_hbm, sems, p).wait()


def swap(low, high, axis):
    n = lax.axis_size(axis)
    up = [(i, (i + 1) % n) for i in range(n)]
    return lax.ppermute(low, axis, up), lax.ppermute(high, axis, [(j, i) for i, j in up])


def swap_both(msg, axis):
    n = lax.axis_size(axis)
    if n == 2:
        return lax.ppermute(msg, axis, [(0, 1), (1, 0)])
    return jnp.stack(swap(msg[0], msg[1], axis))


def per_device(populations, adjoint_next):
    nx = populations.shape[1]
    ext_shape, mini_shape, plane_shape = (FIELDS, nx + 4, ROWS, 128), (FIELDS, ROWS, 128), (nx + 4, ROWS, 128)
    small_y = (len(side_entries(1, 1)) + EDGE_LINES, 128)
    ext, mini, ya, yb = call(
        load_kernel,
        tuple(pltpu.with_memory_space_constraint(v, pltpu.HBM) for v in (populations, adjoint_next)),
        (ext_shape, mini_shape, small_y, small_y),
        scratch=[pltpu.VMEM((19, nx, 16, 128), F32), pltpu.SemaphoreType.DMA((10,))],
        in_specs=[HB, HB],
        name="load",
    )
    (xmsg,) = call(x_kernel, (ext,), ((2, 24, 16, 128),), name="xpack", cost=COSTLY)
    x1 = swap_both(xmsg, "gx")
    ya, yb = swap(ya, yb, "gy")
    mini, za, zb = call(
        yz_kernel,
        (mini, ya, yb),
        (mini_shape, (ROWS + 16, 128), (ROWS + 16, 128)),
        aliases={0: 0},
        name="yz",
    )
    y2a, y2b = call(y_kernel, (ext, mini), ((24 * (nx - 2) + 8, 128), (24 * (nx - 2) + 8, 128)), name="ypack", cost=COSTLY)
    y2a, y2b = swap(y2a, y2b, "gy")
    za, zb = swap(za, zb, "gz")
    mini, xmsg2 = call(
        zx_kernel,
        (mini, za, zb, ya, yb),
        (mini_shape, (2, EDGE_LINES + 16, 128)),
        aliases={0: 0},
        name="zx",
    )
    tile, out_shape = (ROWS, 128), (19, nx + 2, 16, 128)
    ext, psi_ends, flux_ends, psi, zs, zd = call(
        turn_kernel,
        (ext, mini),
        (ext_shape, tile, tile, plane_shape, plane_shape, plane_shape),
        scratch=[pltpu.VMEM((len(Z_PAIRS), 16, 128), F32)],
        aliases={0: 0},
        name="turn",
    )
    x2 = swap_both(xmsg2, "gx")
    ext, out, psi, zs, zd, flux, part = call(
        mid_kernel,
        (ext, mini, ya, yb, y2a, y2b, psi_ends, flux_ends, psi, zs, zd),
        (ext_shape, populations.shape, plane_shape, plane_shape, plane_shape, (3, *plane_shape), out_shape),
        scratch=[pltpu.VMEM((len(Z_PAIRS), 8, 128), F32), pltpu.SemaphoreType.DMA((nx,))],
        aliases={0: 0, 8: 2, 9: 3, 10: 4},
        out_specs=[VM, HB] + [VM] * 5,
        name="mid",
    )
    (ext,) = call(fill_kernel, (ext, x1), (ext_shape,), aliases={0: 0}, name="fill")
    return call(
        last_kernel,
        (ext, mini, x2, psi, zs, zd, flux, part, out),
        (ext_shape, mini_shape, plane_shape, plane_shape, plane_shape, (3, *plane_shape), out_shape, populations.shape),
        scratch=[pltpu.VMEM(tile, F32), pltpu.VMEM(tile, F32), pltpu.SemaphoreType.DMA((nx,))],
        aliases={0: 0, 1: 1, 3: 2, 4: 3, 5: 4, 6: 5, 7: 6, 8: 7},
        in_specs=[VM] * 8 + [HB],
        out_specs=[VM] * 7 + [HB],
        name="last",
    )[-1]


def solution(mesh):
    return jax.shard_map(
        per_device,
        mesh=mesh,
        in_specs=(P(None, "gx", "gy", "gz"), P(None, "gx", "gy", "gz")),
        out_specs=P(None, "gx", "gy", "gz"),
        check_vma=False,
    )
```

```python
import jax
import jax.numpy as jnp
from jax import lax
from jax.experimental import pallas as pl
from jax.experimental.pallas import tpu as pltpu
from jax.sharding import PartitionSpec as P

DIRECTIONS = (
    (0, 0, 0),
    (1, 0, 0),
    (-1, 0, 0),
    (0, 1, 0),
    (0, -1, 0),
    (0, 0, 1),
    (0, 0, -1),
    (1, 1, 0),
    (-1, -1, 0),
    (1, -1, 0),
    (-1, 1, 0),
    (1, 0, 1),
    (-1, 0, -1),
    (1, 0, -1),
    (-1, 0, 1),
    (0, 1, 1),
    (0, -1, -1),
    (0, 1, -1),
    (0, -1, 1),
)
W0, W1, W2 = 1.0 / 3.0, 1.0 / 18.0, 1.0 / 36.0
RELAX_TIME = 0.8
COUPLING = -5.5
INV_TAU = 1.0 / RELAX_TIME
KAPPA = 1.0 - 0.5 / RELAX_TIME

RHO, MOM, FIELDS = 19, 20, 23
ROWS = 24
F32 = jnp.float32
COSTLY = pl.CostEstimate(flops=10**10, bytes_accessed=10**6, transcendentals=0)
VM = pl.BlockSpec(memory_space=pltpu.VMEM)
HB = pl.BlockSpec(memory_space=pltpu.HBM)


def deep_fields(dim, side):
    return [i for i in range(19) if DIRECTIONS[i][dim] == side] + [RHO]


def side_fields(dim, side):
    return deep_fields(dim, side) + [i for i in range(19) if DIRECTIONS[i][dim] == 0] + [MOM, MOM + 1, MOM + 2]


def side_entries(dim, side):
    return [(f, d) for d in (0, 1) for f in (side_fields(dim, side) if d == 0 else deep_fields(dim, side))]


def edge_entries(side, up):
    found = []
    for dx in (0, 1):
        for dy in (0, 1):
            across = deep_fields(0, side) if dx else side_fields(0, side)
            along = deep_fields(1, up) if dy else side_fields(1, up)
            found += [(f, dx, dy) for f in across if f in along]
    return sorted(found, key=lambda entry: z_part(entry[0]))


def z_pieces(side):
    deep = deep_fields(2, side)
    shallow = side_fields(2, side)[len(deep) :]
    found = [(f, u, 0) for u, f in enumerate(deep)]
    return found + [(f, len(deep) + k // 2, 1 + k % 2) for k, f in enumerate(shallow)]


def z_place(side, unit, kind):
    block, pair = unit % 8 // 2, unit % 2
    start = 32 * block + 2 * pair
    if side < 0:
        shift, slots = start - 8, {0: (0, 1), 1: (1,), 2: (0,)}[kind]
        shift -= kind == 2
    else:
        shift, slots = start - 10, {0: (0, 1), 1: (0,), 2: (1,)}[kind]
        shift += kind == 2
    return block, shift, [2 * pair + k for k in slots]


def x_units(side):
    found, group = [], 0
    deep = deep_fields(0, side)
    for depths, fields in ((2, deep), (1, side_fields(0, side)[len(deep) :])):
        up = [f for f in fields if z_part(f) > 0]
        down = [f for f in fields if z_part(f) < 0]
        flat = [f for f in fields if f != RHO and z_part(f) == 0]
        sets = [[(0, ((a, (2,), (2, 3)), (b, (0, 1), (1,))))] for a, b in zip(up, down)]
        for k in range(0, len(flat), 3):
            sets.append([(n - 1, ((f, (1,), (2,)),)) for n, f in enumerate(flat[k : k + 3])])
        if RHO in fields:
            sets.append([(0, ((RHO, (0, 1, 2), (1, 2, 3)),))])
        for units in sets:
            groups = (group,) if depths == 1 else (group + 1, group) if side < 0 else (group, group + 1)
            found += [(groups, shift, parts) for shift, parts in units]
            group += depths
    assert group <= 16
    return found


def any_group(group, groups):
    hit = group == groups[0]
    for g in groups[1:]:
        hit = hit | (group == g)
    return hit


def slot_mask(lane, shift, low, high):
    four = lane % 4
    inside = [None, None]
    for half, slots in enumerate((low, high)):
        for k in slots:
            hit = four == k + shift
            inside[half] = hit if inside[half] is None else inside[half] | hit
    return ((lane < 64) & inside[0]) | ((lane >= 64) & inside[1])


def z_part(f):
    return DIRECTIONS[f][2] if f < 19 else 0


CORNER = len(edge_entries(1, 1))
EDGE_LINES = -(-(2 * CORNER + 4) // 8) * 8


def by_parity(axis, v, w):
    odd = jnp.full(v.shape, lax.axis_index(axis) % 2, jnp.int32) == 1
    return jnp.where(odd, v, w), jnp.where(odd, w, v)


def lane_ids(rows):
    return lax.broadcasted_iota(jnp.int32, (rows, 128), 1)


def lroll(v, amount):
    amount = amount % 128
    return v if isinstance(amount, int) and amount == 0 else pltpu.roll(v, amount, 1)


def yroll(v, c):
    return v if c == 0 else pltpu.roll(v, (-c) % ROWS, 0)


def call(body, ins, outs, scratch=(), aliases=None, name=None, in_specs=None, out_specs=None, cost=None):
    return pl.pallas_call(
        body,
        in_specs=in_specs or [VM] * len(ins),
        out_specs=out_specs or [VM] * len(outs),
        out_shape=[jax.ShapeDtypeStruct(s, F32) for s in outs],
        scratch_shapes=list(scratch),
        input_output_aliases=aliases or {},
        name=name,
        cost_estimate=cost,
        compiler_params=pltpu.CompilerParams(vmem_limit_bytes=20 * 2**20),
    )(*ins)


def load_kernel(pop_hbm, adj_hbm, ext, mini, ya, yb, pops, sems):
    nx = pop_hbm.shape[1]
    lane = lane_ids(16)
    group = lane // 4
    chunks = [(f, min(4, 19 - f)) for f in range(0, 19, 4)]
    copies = []
    for k, (f, n) in enumerate(chunks):
        own = ext.at[pl.ds(f, n), pl.ds(2, nx), pl.ds(0, 16), :]
        copies.append(pltpu.make_async_copy(adj_hbm.at[pl.ds(f, n)], own, sems.at[k]))
    for k, (f, n) in enumerate(chunks):
        copies.append(pltpu.make_async_copy(pop_hbm.at[pl.ds(f, n)], pops.at[pl.ds(f, n)], sems.at[5 + k]))
    for c in copies:
        c.start()

    def edges(f):
        e = lroll(ext[f, 2, pl.ds(0, 16), :], 10)
        for x in range(1, nx):
            e = jnp.where(group == x + 2, lroll(ext[f, x + 2, pl.ds(0, 16), :], 4 * x + 10), e)
        mini[f, pl.ds(0, 16), :] = e

    for k, (f, n) in enumerate(chunks):
        copies[k].wait()
        for i in range(n):
            edges(f + i)
    for c in copies[5:]:
        c.wait()

    def moments(x, _):
        rho = pops[0, x]
        mom = [None] * 3
        for i in range(1, 19):
            p = pops[i, x]
            rho = rho + p
            for k in range(3):
                c = DIRECTIONS[i][k]
                if c:
                    mom[k] = (p if c > 0 else -p) if mom[k] is None else (mom[k] + p if c > 0 else mom[k] - p)
        ext[RHO, x + 2, pl.ds(0, 16), :] = rho
        for k in range(3):
            ext[MOM + k, x + 2, pl.ds(0, 16), :] = mom[k]
        return 0

    lax.fori_loop(0, nx, moments, 0, unroll=2)
    for f in range(RHO, FIELDS):
        edges(f)
    place = lax.broadcasted_iota(jnp.int32, (EDGE_LINES, 128), 0)
    for up, msg in ((-1, ya), (1, yb)):
        entries = side_entries(1, up)
        for e, (f, d) in enumerate(entries):
            msg[pl.ds(e, 1), :] = mini[f, pl.ds(15 - d if up < 0 else d, 1), :]
        lines = [(side, *entry) for side in (-1, 1) for entry in edge_entries(side, up)]
        for e, (side, f, dx, dy) in enumerate(lines):
            plane = nx + 1 - dx if side < 0 else 2 + dx
            msg[pl.ds(len(entries) + e, 1), :] = ext[f, plane, pl.ds(15 - dy if up < 0 else dy, 1), :]
        v = msg[pl.ds(len(entries), EDGE_LINES), :]
        turned = v
        for step in (-1, 1):
            here = None
            for k in (0, 1):
                hits = [e for e in range(CORNER) if z_part(lines[CORNER * k + e][1]) == step]
                hit = (place >= CORNER * k + hits[0]) & (place <= CORNER * k + hits[-1])
                here = hit if here is None else here | hit
            turned = jnp.where(here, lroll(v, -step), turned)
        msg[pl.ds(len(entries), EDGE_LINES), :] = turned
    ya[...], yb[...] = by_parity("gy", ya[...], yb[...])


def y_entries(side):
    found = []
    for f, d in side_entries(1, side):
        cx = DIRECTIONS[f][0] if f < 19 else 0
        found.append((f, d, 3 + cx))
    return sorted(found, key=lambda entry: z_part(entry[0]))


def y_lines(ext, low, high):
    for side, msg in ((-1, low), (1, high)):
        entries = y_entries(side)
        six = ext.shape[1] - 6
        msg[pl.ds(six * len(entries), 8), :] = jnp.zeros((8, 128), F32)
        for e, (f, d, first) in enumerate(entries):
            msg[pl.ds(six * e, six), :] = ext[f, pl.ds(first, six), 15 - d if side < 0 else d, :]
        for step in (-1, 1):
            hits = [e for e, (f, _, _) in enumerate(entries) if z_part(f) == step]
            start, stop = six * hits[0], six * (hits[-1] + 1)
            bottom, top = start // 8 * 8, -(-stop // 8) * 8
            v = msg[pl.ds(bottom, top - bottom), :]
            place = bottom + lax.broadcasted_iota(jnp.int32, v.shape, 0)
            msg[pl.ds(bottom, top - bottom), :] = jnp.where((place >= start) & (place < stop), lroll(v, -step), v)


def pair_kernel(ext, small, msg, low, high):
    y_lines(ext, low, high)
    msg[pl.ds(0, small.shape[0]), :] = small[...]
    msg[pl.ds(small.shape[0], low.shape[0]), :] = by_parity("gy", low[...], high[...])[1]


def x_kernel(ext, xmsg):
    nx = ext.shape[1] - 4
    for s, side in enumerate((-1, 1)):
        for e, (f, d) in enumerate(side_entries(0, side)):
            plane = (nx + 1 - d) if side < 0 else (2 + d)
            xmsg[s, e] = lroll(ext[f, plane, pl.ds(0, 16), :], -z_part(f))


def yz_kernel(mini_in, ra, rb, mini, za, zb, low, high):
    lane = lane_ids(ROWS)
    low[...], high[...] = by_parity("gy", rb[pl.ds(0, low.shape[0]), :], ra[...])
    for side, msg in ((-1, low), (1, high)):
        entries = side_entries(1, side)
        for e, (f, d) in enumerate(entries):
            mini[f, pl.ds(23 - d if side < 0 else 16 + d, 1), :] = msg[pl.ds(e, 1), :]
    for side, msg in ((-1, za), (1, zb)):
        tiles = [None, None]
        for f, unit, kind in z_pieces(side):
            block, shift, slots = z_place(side, unit, kind)
            v = lroll(mini[f], shift)
            here = lane % 4 == slots[0]
            for k in slots[1:]:
                here = here | (lane % 4 == k)
            t = unit // 8
            tiles[t] = v if tiles[t] is None else jnp.where((lane // 32 == block) & here, v, tiles[t])
        msg[pl.ds(0, ROWS), :] = tiles[0]
        msg[pl.ds(ROWS, 8), :] = jnp.where(lane[:8] < 64, tiles[1][:8], lroll(tiles[1][8:16], 64))
        msg[pl.ds(ROWS + 8, 8), :] = tiles[1][16:]


def y_kernel(ext, mini, msg, low, high):
    y_lines(ext, low, high)
    msg[...] = by_parity("gy", low[...], high[...])[0]


Z_PAIRS = ((5, 6), (11, 13), (14, 12), (15, 17), (18, 16))


def z_ends(above, below):
    return jnp.where(lane_ids(above.shape[0]) % 4 == 0, lroll(above, 62), below)


def close_pairs(p, pairs, ends, ext, rows):
    lane = lane_ids(rows.size)
    found = []
    for (up, down), e in zip(pairs, ends):
        g = lroll(e, 255 - 4 * p)
        found.append((up, jnp.where(lane == 127, g, ext[up, p, rows, :])))
        found.append((down, jnp.where(lane == 0, g, ext[down, p, rows, :])))
    return found


def zx_kernel(mini_in, ra, rb, ya, yb, mini, xmsg):
    lane = lane_ids(ROWS)
    for f in range(FIELDS):
        e = mini_in[f]
        if f == RHO or z_part(f) < 0:
            e = jnp.where(lane < 64, e, lroll(e, 64))
        mini[f] = e
    for side, msg in ((-1, ra), (1, rb)):
        second = msg[pl.ds(ROWS, 8), :]
        tiles = (msg[pl.ds(0, ROWS), :], jnp.concatenate([second, lroll(second, 64), msg[pl.ds(ROWS + 8, 8), :]], axis=0))
        start, slots = (8, (0, 1)) if side < 0 else (72, (2, 3))
        near = slots[1] if side < 0 else slots[0]
        inside = (lane >= start) & (lane < start + 32)
        for f, unit, kind in z_pieces(side):
            shift = z_place(side, unit, kind)[1]
            keep = inside & ((lane % 4 // 2 == slots[0] // 2) if kind == 0 else (lane % 4 == near))
            v = lroll(tiles[unit // 8], -shift + (0 if side < 0 else 64))
            mini[f] = jnp.where(keep, v, mini[f])
    group = (lane % 64) // 4
    for s, side in enumerate((-1, 1)):
        acc = None
        for groups, shift, parts in x_units(side):
            v = mini[parts[0][0]]
            for f, low, high in parts[1:]:
                v = jnp.where(slot_mask(lane, 0, low, high), mini[f], v)
            v = lroll(v, 4 * groups[0] - 4 * (9 if side < 0 else 2) + shift)
            if acc is None:
                acc = v
            else:
                here = any_group(group, groups)
                if parts[0][1:] == ((1,), (2,)):
                    here = here & slot_mask(lane, shift, (1,), (2,))
                acc = jnp.where(here, v, acc)
        xmsg[s, pl.ds(EDGE_LINES - 8, 8), :] = pltpu.roll(acc[16:], 6, 0)
        xmsg[s, pl.ds(EDGE_LINES, 16), :] = acc[:16]
        for k, msg in enumerate((ya, yb)):
            start = len(side_entries(1, 1)) + CORNER * s
            xmsg[s, pl.ds(CORNER * k, CORNER), :] = msg[pl.ds(start, CORNER), :]


def turn_kernel(ext_in, mini, ext, psi_ends, flux_ends, psi, zs, zd, ends):
    nx = ext.shape[1] - 4
    lane = lane_ids(16)
    rows = pl.ds(0, 16)
    for k, (up, down) in enumerate(Z_PAIRS):
        ends[k] = z_ends(mini[up, rows, :], mini[down, rows, :])

    def turn(p, _):
        found = []
        for k, (up, down) in enumerate(Z_PAIRS):
            g = lroll(ends[k], 255 - 4 * p)
            found.append((up, jnp.where(lane == 127, g, lroll(ext_in[up, p, rows, :], 127))))
            found.append((down, jnp.where(lane == 0, g, lroll(ext_in[down, p, rows, :], 1))))
        for f, v in found:
            ext[f, p, rows, :] = v
        return 0

    lax.fori_loop(2, nx + 2, turn, 0, unroll=2)
    psi_ends[...], flux_ends[...] = mini_adjoint(mini)
    for p in range(2, nx + 2):
        potential(p, ext, psi_ends, psi, zs, zd, rows)


def cell(b, rho, mom, psi, g):
    pairs = {}
    for i in range(1, 19, 2):
        pairs[i] = (b[i] + b[i + 1], b[i] - b[i + 1])
    s = {i: v[0] for i, v in pairs.items()}
    d = {i: v[1] for i, v in pairs.items()}
    sxy, sxz, syz = s[7] + s[9], s[11] + s[13], s[15] + s[17]
    a0 = W0 * b[0] + W1 * (s[1] + s[3] + s[5]) + W2 * (sxy + sxz + syz)
    a1 = (
        (3 * W1) * d[1] + (3 * W2) * ((d[7] + d[9]) + (d[11] + d[13])),
        (3 * W1) * d[3] + (3 * W2) * ((d[7] - d[9]) + (d[15] + d[17])),
        (3 * W1) * d[5] + (3 * W2) * ((d[11] - d[13]) + (d[15] - d[17])),
    )
    a03 = 3.0 * a0
    bxx = (9 * W1) * s[1] + (9 * W2) * (sxy + sxz) - a03
    byy = (9 * W1) * s[3] + (9 * W2) * (sxy + syz) - a03
    bzz = (9 * W1) * s[5] + (9 * W2) * (sxz + syz) - a03
    bxy = (9 * W2) * (s[7] - s[9])
    bxz = (9 * W2) * (s[11] - s[13])
    byz = (9 * W2) * (s[15] - s[17])
    force = [(-COUPLING * psi) * gk for gk in g]
    inv = 1.0 / rho
    u = [(m + 0.5 * fk) * inv for m, fk in zip(mom, force)]

    def apply(v):
        return (
            bxx * v[0] + bxy * v[1] + bxz * v[2],
            bxy * v[0] + byy * v[1] + byz * v[2],
            bxz * v[0] + byz * v[1] + bzz * v[2],
        )

    w = [p + q for p, q in zip(a1, apply(u))]
    bf = [(KAPPA * inv) * q for q in apply(force)]
    force_bar = [p + 0.5 * q for p, q in zip(w, bf)]
    return a0, a1, u, w, bf, force_bar


def dot(p, q):
    return p[0] * q[0] + p[1] * q[1] + p[2] * q[2]


def mini_adjoint(mini):
    def msh(v, c):
        return lroll(yroll(v, c[1]), -4 * c[0] - c[2])

    psi = 1.0 - jnp.exp(-mini[RHO])
    ys = yroll(psi, 1) + yroll(psi, -1)
    zsum = lroll(psi, -1) + lroll(psi, 1)
    xsum = lroll(psi, -4) + lroll(psi, 4)
    qx = W1 * psi + W2 * (ys + zsum)
    qy = W1 * psi + W2 * (xsum + zsum)
    qz = W1 * psi + W2 * (xsum + ys)
    g = (lroll(qx, -4) - lroll(qx, 4), yroll(qy, 1) - yroll(qy, -1), lroll(qz, -1) - lroll(qz, 1))
    b = [msh(mini[i], DIRECTIONS[i]) for i in range(19)]
    force_bar = cell(b, mini[RHO], [mini[MOM + k] for k in range(3)], psi, g)[5]
    fx, fy, fz = (psi * v for v in force_bar)
    across = W2 * ((lroll(fx, -4) - lroll(fx, 4)) + (yroll(fy, 1) - yroll(fy, -1)))
    along = W1 * fz + W2 * ((lroll(fz, -4) + lroll(fz, 4)) + (yroll(fz, 1) + yroll(fz, -1)))
    return z_ends(psi, psi), z_ends(across + along, across - along)


def zpair(above, below, ends, plane):
    lane = lane_ids(above.shape[0])
    g = lroll(ends, 255 - 4 * plane)
    return jnp.where(lane == 127, g, lroll(above, 127)), jnp.where(lane == 0, g, lroll(below, 1))


def potential(p, ext, ends, psi, zs, zd, rows):
    v = 1.0 - jnp.exp(-ext[RHO, p, rows, :])
    psi[p, rows, :] = v
    a, b = zpair(v, v, ends[rows, :], p)
    zs[p, rows, :] = a + b
    zd[p, rows, :] = a - b


def collide(p, ext, psi, zs, zd, flux, out):
    v, xp, xm = psi[p], psi[p + 1], psi[p - 1]
    qxp = W1 * xp + W2 * (yroll(xp, 1) + yroll(xp, -1) + zs[p + 1])
    qxm = W1 * xm + W2 * (yroll(xm, 1) + yroll(xm, -1) + zs[p - 1])
    qy = W1 * v + W2 * (xp + xm + zs[p])
    zz = zd[p]
    g = (
        qxp - qxm,
        yroll(qy, 1) - yroll(qy, -1),
        W1 * zz + W2 * (zd[p + 1] + zd[p - 1] + yroll(zz, 1) + yroll(zz, -1)),
    )
    b = [yroll(ext[i, p + DIRECTIONS[i][0]], DIRECTIONS[i][1]) for i in range(19)]
    a0, a1, u, w, bf, fb = cell(b, ext[RHO, p], [ext[MOM + k, p] for k in range(3)], v, g)
    for k in range(3):
        flux[k, p] = v * fb[k]

    def top(a):
        return a[:16]

    vv = [top(INV_TAU * wk + bk) for wk, bk in zip(w, bf)]
    uu = [top(a) for a in u]
    base = INV_TAU * (top(a0) + 0.5 * dot([top(r + q) for r, q in zip(a1, w)], uu)) - dot(vv, uu)
    base = base + (-COUPLING * (1.0 - top(v))) * top(dot(fb, g))
    for i in range(19):
        o = (1.0 - INV_TAU) * top(b[i]) + base
        for k in range(3):
            if DIRECTIONS[i][k] > 0:
                o = o + vv[k]
            elif DIRECTIONS[i][k] < 0:
                o = o - vv[k]
        out[i, p - 1] = o


def finish(p, psi, flux, ends, out):
    fx, fxm, fy = flux[0, p + 1], flux[0, p - 1], flux[1, p]
    fz = flux[2, p]
    xd = fx - fxm
    fyx = flux[1, p + 1] + flux[1, p - 1]
    dx = xd[:16]
    dy = (yroll(fy, 1) - yroll(fy, -1))[:16]
    here = W1 * (dx + dy) + W2 * (
        (yroll(xd, 1) + yroll(xd, -1))[:16] + (yroll(fyx, 1) - yroll(fyx, -1))[:16]
    )
    across = W2 * (dx + dy)
    along = W1 * fz[:16] + W2 * (flux[2, p + 1, pl.ds(0, 16), :] + flux[2, p - 1, pl.ds(0, 16), :] + (yroll(fz, 1) + yroll(fz, -1))[:16])
    a, b = zpair(across + along, across - along, ends[pl.ds(0, 16), :], p)
    term = (COUPLING * (1.0 - psi[p, pl.ds(0, 16), :])) * (here + (a + b))
    for i in range(19):
        out[i, p - 1] = out[i, p - 1] + term


def planes(count, of, step, unroll=4):
    def body(k, _):
        step(of(k))
        return 0

    lax.fori_loop(0, count, body, 0, unroll=unroll)


def send_planes(out, out_hbm, sem, first, count):
    return pltpu.make_async_copy(out.at[:, pl.ds(first - 1, count)], out_hbm.at[:, pl.ds(first - 2, count)], sem)


def mid_kernel(ext_in, mini, sa, sb, r2, rb, psi_ends, flux_ends, psi_in, zs_in, zd_in, ext, psi, zs, zd, flux, out, ends, low, high):
    nx = ext.shape[1] - 4
    rows = pl.ds(16, 8)
    low[...], high[...] = by_parity("gy", rb[pl.ds(sa.shape[0], low.shape[0]), :], r2[...])
    for up, small, large in ((-1, sa, low), (1, sb, high)):
        for e, (f, d, first) in enumerate(y_entries(up)):
            ext[f, pl.ds(first, nx - 2), 23 - d if up < 0 else 16 + d, :] = large[pl.ds((nx - 2) * e, nx - 2), :]
        lines = [(side, *entry) for side in (-1, 1) for entry in edge_entries(side, up)]
        for e, (side, f, dx, dy) in enumerate(lines):
            plane, row = nx + 1 - dx if side < 0 else 2 + dx, 23 - dy if up < 0 else 16 + dy
            ext[f, plane, pl.ds(row, 1), :] = small[pl.ds(len(side_entries(1, up)) + e, 1), :]
    for k, (up, down) in enumerate(Z_PAIRS):
        ends[k] = z_ends(mini[up, rows, :], mini[down, rows, :])

    def close(p, _):
        for f, v in close_pairs(p, Z_PAIRS, [ends[k] for k in range(len(Z_PAIRS))], ext, rows):
            ext[f, p, rows, :] = v
        return 0

    lax.fori_loop(2, nx + 2, close, 0, unroll=4)
    for p in range(2, nx + 2):
        potential(p, ext, psi_ends, psi, zs, zd, rows)
    planes(nx - 2, lambda k: k + 3, lambda p: collide(p, ext, psi, zs, zd, flux, out))

    planes(nx - 4, lambda k: k + 4, lambda p: finish(p, psi, flux, flux_ends, out))


def fill_kernel(ext_in, r1, ext):
    nx = ext.shape[1] - 4
    for s, side in enumerate((-1, 1)):
        for e, (f, d) in enumerate(side_entries(0, side)):
            ext[f, 1 - d if side < 0 else nx + 2 + d, pl.ds(0, 16), :] = r1[s, e]


def last_kernel(ext_in, mini_in, r2, psi_in, zs_in, zd_in, flux_in, out_in, ext, mini, psi, zs, zd, flux, out, out_hbm, psi_ends, flux_ends, sems):
    nx = ext.shape[1] - 4
    copies = [
        send_planes(out, out_hbm, sems.at[k], first, count) for k, (first, count) in enumerate(((4, nx - 4), (2, 2), (nx, 2)))
    ]
    copies[0].start()
    lane = lane_ids(ROWS)
    group = (lane % 64) // 4
    for s, side in enumerate((-1, 1)):
        lines = [(up, *entry) for up in (-1, 1) for entry in edge_entries(side, up)]
        for e, (up, f, dx, dy) in enumerate(lines):
            plane, row = 1 - dx if side < 0 else nx + 2 + dx, 23 - dy if up < 0 else 16 + dy
            ext[f, plane, pl.ds(row, 1), :] = r2[s, pl.ds(e, 1), :]
        small = jnp.concatenate([r2[s, pl.ds(EDGE_LINES, 16), :], pltpu.roll(r2[s, pl.ds(EDGE_LINES - 8, 8), :], 2, 0)], axis=0)
        for groups, shift, parts in x_units(side):
            near = 1 if side < 0 else nx + 2
            here = any_group(group, (near, near + side)[: len(groups)])
            v = lroll(small, 4 * near - 4 * groups[0] - shift)
            for f, low, high in parts:
                mini[f] = jnp.where(here & slot_mask(lane, 0, low, high), v, mini[f])
    ends = [z_ends(mini[up], mini[down]) for up, down in Z_PAIRS]
    for p in (0, 1, nx + 2, nx + 3):
        keep = [k for k, (f, _) in enumerate(Z_PAIRS) if DIRECTIONS[f][0] == (-1 if p < 2 else 1) or (p in (1, nx + 2) and DIRECTIONS[f][0] == 0)]
        for f, v in close_pairs(p, [Z_PAIRS[k] for k in keep], [ends[k] for k in keep], ext, pl.ds(0, ROWS)):
            ext[f, p] = v
    psi_ends[...], flux_ends[...] = mini_adjoint(mini)
    for p in (0, 1, nx + 2, nx + 3):
        potential(p, ext, psi_ends, psi, zs, zd, pl.ds(0, ROWS))

    def outer(low, k):
        return low + k + jnp.where(k >= 2, nx - 2, 0)

    planes(4, lambda k: outer(1, k), lambda p: collide(p, ext, psi, zs, zd, flux, out))
    planes(4, lambda k: outer(2, k) - jnp.where(k >= 2, 2, 0), lambda p: finish(p, psi, flux, flux_ends, out))
    for copy in copies[1:]:
        copy.start()
    for copy in copies:
        copy.wait()


def swap(low, high, axis):
    n = lax.axis_size(axis)
    up = [(i, (i + 1) % n) for i in range(n)]
    return lax.ppermute(low, axis, up), lax.ppermute(high, axis, [(j, i) for i, j in up])


def ppermute_pairs(msg, axis, first):
    n = lax.axis_size(axis)
    found = []
    for i in range(first, n + first, 2):
        found += [(i % n, (i + 1) % n), ((i + 1) % n, i % n)]
    return lax.ppermute(msg, axis, found)


def swap_both(msg, axis):
    n = lax.axis_size(axis)
    if n == 2:
        return lax.ppermute(msg, axis, [(0, 1), (1, 0)])
    return jnp.stack(swap(msg[0], msg[1], axis))


def per_device(populations, adjoint_next):
    nx = populations.shape[1]
    ext_shape, mini_shape, plane_shape = (FIELDS, nx + 4, ROWS, 128), (FIELDS, ROWS, 128), (nx + 4, ROWS, 128)
    small_y = (len(side_entries(1, 1)) + EDGE_LINES, 128)
    ext, mini, ya, yb = call(
        load_kernel,
        tuple(pltpu.with_memory_space_constraint(v, pltpu.HBM) for v in (populations, adjoint_next)),
        (ext_shape, mini_shape, small_y, small_y),
        scratch=[pltpu.VMEM((19, nx, 16, 128), F32), pltpu.SemaphoreType.DMA((10,))],
        in_specs=[HB, HB],
        name="load",
    )
    large_y = (24 * (nx - 2) + 8, 128)
    two_large = [pltpu.VMEM(large_y, F32), pltpu.VMEM(large_y, F32)]
    (yb,) = call(
        pair_kernel, (ext, yb), ((small_y[0] + large_y[0], 128),), scratch=two_large, name="pair", cost=COSTLY
    )
    (xmsg,) = call(x_kernel, (ext,), ((2, 24, 16, 128),), name="xpack", cost=COSTLY)
    x1 = swap_both(xmsg, "gx")
    ya, y2b = ppermute_pairs(ya, "gy", 1), ppermute_pairs(yb, "gy", 0)
    mini, za, zb, ya, yb = call(
        yz_kernel,
        (mini, ya, y2b),
        (mini_shape, (ROWS + 16, 128), (ROWS + 16, 128), small_y, small_y),
        aliases={0: 0},
        name="yz",
    )
    (y2a,) = call(y_kernel, (ext, mini), (large_y,), scratch=two_large, name="ypack", cost=COSTLY)
    y2a = ppermute_pairs(y2a, "gy", 1)
    za, zb = swap(za, zb, "gz")
    mini, xmsg2 = call(
        zx_kernel,
        (mini, za, zb, ya, yb),
        (mini_shape, (2, EDGE_LINES + 16, 128)),
        aliases={0: 0},
        name="zx",
    )
    tile, out_shape = (ROWS, 128), (19, nx + 2, 16, 128)
    ext, psi_ends, flux_ends, psi, zs, zd = call(
        turn_kernel,
        (ext, mini),
        (ext_shape, tile, tile, plane_shape, plane_shape, plane_shape),
        scratch=[pltpu.VMEM((len(Z_PAIRS), 16, 128), F32)],
        aliases={0: 0},
        name="turn",
    )
    x2 = swap_both(xmsg2, "gx")
    ext, psi, zs, zd, flux, part = call(
        mid_kernel,
        (ext, mini, ya, yb, y2a, y2b, psi_ends, flux_ends, psi, zs, zd),
        (ext_shape, plane_shape, plane_shape, plane_shape, (3, *plane_shape), out_shape),
        scratch=[pltpu.VMEM(v, F32) for v in ((len(Z_PAIRS), 8, 128), large_y, large_y)],
        aliases={0: 0, 8: 1, 9: 2, 10: 3},
        name="mid",
    )
    (ext,) = call(fill_kernel, (ext, x1), (ext_shape,), aliases={0: 0}, name="fill")
    return call(
        last_kernel,
        (ext, mini, x2, psi, zs, zd, flux, part),
        (ext_shape, mini_shape, plane_shape, plane_shape, plane_shape, (3, *plane_shape), out_shape, populations.shape),
        scratch=[pltpu.VMEM(tile, F32), pltpu.VMEM(tile, F32), pltpu.SemaphoreType.DMA((3,))],
        aliases={0: 0, 1: 1, 3: 2, 4: 3, 5: 4, 6: 5, 7: 6},
        out_specs=[VM] * 7 + [HB],
        name="last",
    )[-1]


def solution(mesh):
    return jax.shard_map(
        per_device,
        mesh=mesh,
        in_specs=(P(None, "gx", "gy", "gz"), P(None, "gx", "gy", "gz")),
        out_specs=P(None, "gx", "gy", "gz"),
        check_vma=False,
    )
```

```python
import jax
import jax.numpy as jnp
from jax import lax
from jax.experimental import pallas as pl
from jax.experimental.pallas import tpu as pltpu
from jax.sharding import PartitionSpec as P

DIRECTIONS = (
    (0, 0, 0),
    (1, 0, 0),
    (-1, 0, 0),
    (0, 1, 0),
    (0, -1, 0),
    (0, 0, 1),
    (0, 0, -1),
    (1, 1, 0),
    (-1, -1, 0),
    (1, -1, 0),
    (-1, 1, 0),
    (1, 0, 1),
    (-1, 0, -1),
    (1, 0, -1),
    (-1, 0, 1),
    (0, 1, 1),
    (0, -1, -1),
    (0, 1, -1),
    (0, -1, 1),
)
W0, W1, W2 = 1.0 / 3.0, 1.0 / 18.0, 1.0 / 36.0
RELAX_TIME = 0.8
COUPLING = -5.5
INV_TAU = 1.0 / RELAX_TIME
KAPPA = 1.0 - 0.5 / RELAX_TIME

RHO, MOM, FIELDS = 19, 20, 23
ROWS = 24
F32 = jnp.float32
COSTLY = pl.CostEstimate(flops=10**10, bytes_accessed=10**6, transcendentals=0)
VM = pl.BlockSpec(memory_space=pltpu.VMEM)
HB = pl.BlockSpec(memory_space=pltpu.HBM)


def deep_fields(dim, side):
    return [i for i in range(19) if DIRECTIONS[i][dim] == side] + [RHO]


def side_fields(dim, side):
    return deep_fields(dim, side) + [i for i in range(19) if DIRECTIONS[i][dim] == 0] + [MOM, MOM + 1, MOM + 2]


def side_entries(dim, side):
    return [(f, d) for d in (0, 1) for f in (side_fields(dim, side) if d == 0 else deep_fields(dim, side))]


def edge_entries(side, up):
    found = []
    for dx in (0, 1):
        for dy in (0, 1):
            across = deep_fields(0, side) if dx else side_fields(0, side)
            along = deep_fields(1, up) if dy else side_fields(1, up)
            found += [(f, dx, dy) for f in across if f in along]
    return sorted(found, key=lambda entry: z_part(entry[0]))


def z_pieces(side):
    deep = deep_fields(2, side)
    shallow = side_fields(2, side)[len(deep) :]
    found = [(f, u, 0) for u, f in enumerate(deep)]
    return found + [(f, len(deep) + k // 2, 1 + k % 2) for k, f in enumerate(shallow)]


def z_place(side, unit, kind):
    block, pair = unit % 8 // 2, unit % 2
    start = 32 * block + 2 * pair
    if side < 0:
        shift, slots = start - 8, {0: (0, 1), 1: (1,), 2: (0,)}[kind]
        shift -= kind == 2
    else:
        shift, slots = start - 10, {0: (0, 1), 1: (0,), 2: (1,)}[kind]
        shift += kind == 2
    return block, shift, [2 * pair + k for k in slots]


def x_units(side):
    found, group = [], 0
    deep = deep_fields(0, side)
    for depths, fields in ((2, deep), (1, side_fields(0, side)[len(deep) :])):
        up = [f for f in fields if z_part(f) > 0]
        down = [f for f in fields if z_part(f) < 0]
        flat = [f for f in fields if f != RHO and z_part(f) == 0]
        sets = [[(0, ((a, (2,), (2, 3)), (b, (0, 1), (1,))))] for a, b in zip(up, down)]
        for k in range(0, len(flat), 3):
            sets.append([(n - 1, ((f, (1,), (2,)),)) for n, f in enumerate(flat[k : k + 3])])
        if RHO in fields:
            sets.append([(0, ((RHO, (0, 1, 2), (1, 2, 3)),))])
        for units in sets:
            groups = (group,) if depths == 1 else (group + 1, group) if side < 0 else (group, group + 1)
            found += [(groups, shift, parts) for shift, parts in units]
            group += depths
    assert group <= 16
    return found


def any_group(group, groups):
    hit = group == groups[0]
    for g in groups[1:]:
        hit = hit | (group == g)
    return hit


def slot_mask(lane, shift, low, high):
    four = lane % 4
    inside = [None, None]
    for half, slots in enumerate((low, high)):
        for k in slots:
            hit = four == k + shift
            inside[half] = hit if inside[half] is None else inside[half] | hit
    return ((lane < 64) & inside[0]) | ((lane >= 64) & inside[1])


def z_part(f):
    return DIRECTIONS[f][2] if f < 19 else 0


CORNER = len(edge_entries(1, 1))
EDGE_LINES = -(-(2 * CORNER + 4) // 8) * 8


def by_parity(axis, v, w):
    odd = jnp.full(v.shape, lax.axis_index(axis) % 2, jnp.int32) == 1
    return jnp.where(odd, v, w), jnp.where(odd, w, v)


def lane_ids(rows):
    return lax.broadcasted_iota(jnp.int32, (rows, 128), 1)


def lroll(v, amount):
    amount = amount % 128
    return v if isinstance(amount, int) and amount == 0 else pltpu.roll(v, amount, 1)


def yroll(v, c):
    return v if c == 0 else pltpu.roll(v, (-c) % ROWS, 0)


def call(body, ins, outs, scratch=(), aliases=None, name=None, in_specs=None, out_specs=None, cost=None):
    return pl.pallas_call(
        body,
        in_specs=in_specs or [VM] * len(ins),
        out_specs=out_specs or [VM] * len(outs),
        out_shape=[jax.ShapeDtypeStruct(s, F32) for s in outs],
        scratch_shapes=list(scratch),
        input_output_aliases=aliases or {},
        name=name,
        cost_estimate=cost,
        compiler_params=pltpu.CompilerParams(vmem_limit_bytes=20 * 2**20),
    )(*ins)


def load_kernel(pop_hbm, adj_hbm, ext, mini, ya, yb, pops, columns, sems):
    nx = pop_hbm.shape[1]
    lane = lane_ids(16)
    group = lane // 4
    chunks = [(f, min(4, 19 - f)) for f in range(0, 19, 4)]
    copies = []
    for k, (f, n) in enumerate(chunks):
        own = ext.at[pl.ds(f, n), pl.ds(2, nx), pl.ds(0, 16), :]
        copies.append(pltpu.make_async_copy(adj_hbm.at[pl.ds(f, n)], own, sems.at[k]))
    for k, (f, n) in enumerate(chunks):
        copies.append(pltpu.make_async_copy(pop_hbm.at[pl.ds(f, n)], pops.at[pl.ds(f, n)], sems.at[5 + k]))
    for c in copies:
        c.start()

    def edges(f):
        e = lroll(ext[f, 2, pl.ds(0, 16), :], 10)
        for x in range(1, nx):
            e = jnp.where(group == x + 2, lroll(ext[f, x + 2, pl.ds(0, 16), :], 4 * x + 10), e)
        mini[f, pl.ds(0, 16), :] = e

    for k, (f, n) in enumerate(chunks):
        copies[k].wait()
        for i in range(n):
            edges(f + i)
    for c in copies[5:]:
        c.wait()

    def moments(x, _):
        rho = pops[0, x]
        mom = [None] * 3
        for i in range(1, 19):
            p = pops[i, x]
            rho = rho + p
            for k in range(3):
                c = DIRECTIONS[i][k]
                if c:
                    mom[k] = (p if c > 0 else -p) if mom[k] is None else (mom[k] + p if c > 0 else mom[k] - p)
        ext[RHO, x + 2, pl.ds(0, 16), :] = rho
        for k in range(3):
            ext[MOM + k, x + 2, pl.ds(0, 16), :] = mom[k]
        return 0

    lax.fori_loop(0, nx, moments, 0, unroll=2)
    for f in range(RHO, FIELDS):
        edges(f)
    place = lax.broadcasted_iota(jnp.int32, (EDGE_LINES, 128), 0)
    for up, msg in ((-1, ya), (1, yb)):
        entries = side_entries(1, up)
        for e, (f, d) in enumerate(entries):
            columns[pl.ds(e, 1), :] = mini[f, pl.ds(15 - d if up < 0 else d, 1), :]
        v = jnp.where(lane[:8] < 40, columns[pl.ds(0, 8), :], lroll(columns[pl.ds(8, 8), :], 32))
        msg[pl.ds(0, 8), :] = jnp.where(lane[:8] < 72, v, lroll(columns[pl.ds(16, 8), :], 64))
        lines = [(side, *entry) for side in (-1, 1) for entry in edge_entries(side, up)]
        for e, (side, f, dx, dy) in enumerate(lines):
            plane = nx + 1 - dx if side < 0 else 2 + dx
            msg[pl.ds(8 + e, 1), :] = ext[f, plane, pl.ds(15 - dy if up < 0 else dy, 1), :]
        v = msg[pl.ds(8, EDGE_LINES), :]
        turned = v
        for step in (-1, 1):
            here = None
            for k in (0, 1):
                hits = [e for e in range(CORNER) if z_part(lines[CORNER * k + e][1]) == step]
                hit = (place >= CORNER * k + hits[0]) & (place <= CORNER * k + hits[-1])
                here = hit if here is None else here | hit
            turned = jnp.where(here, lroll(v, -step), turned)
        msg[pl.ds(8, EDGE_LINES), :] = turned
    ya[...], yb[...] = by_parity("gy", ya[...], yb[...])


def y_entries(side):
    found = []
    for f, d in side_entries(1, side):
        cx = DIRECTIONS[f][0] if f < 19 else 0
        found.append((f, d, 3 + cx))
    return sorted(found, key=lambda entry: z_part(entry[0]))


def y_lines(ext, msg, on_odd, on_even):
    six = ext.shape[1] - 6

    def fill(side):
        entries = y_entries(side)
        for e, (f, d, first) in enumerate(entries):
            msg[pl.ds(six * e, six), :] = ext[f, pl.ds(first, six), 15 - d if side < 0 else d, :]
        msg[pl.ds(six * len(entries), 8), :] = jnp.zeros((8, 128), F32)
        for step in (-1, 1):
            hits = [e for e, (f, _, _) in enumerate(entries) if z_part(f) == step]
            start, stop = six * hits[0], six * (hits[-1] + 1)
            bottom, top = start // 8 * 8, -(-stop // 8) * 8
            v = msg[pl.ds(bottom, top - bottom), :]
            place = bottom + lax.broadcasted_iota(jnp.int32, v.shape, 0)
            msg[pl.ds(bottom, top - bottom), :] = jnp.where((place >= start) & (place < stop), lroll(v, -step), v)

    odd = lax.axis_index("gy") % 2
    pl.when(odd == 1)(lambda: fill(on_odd))
    pl.when(odd == 0)(lambda: fill(on_even))


def pair_kernel(ext, small, msg):
    msg[pl.ds(0, small.shape[0]), :] = small[...]
    y_lines(ext, msg.at[pl.ds(small.shape[0], msg.shape[0] - small.shape[0]), :], 1, -1)


def x_kernel(ext, xmsg):
    nx = ext.shape[1] - 4
    for s, side in enumerate((-1, 1)):
        for e, (f, d) in enumerate(side_entries(0, side)):
            plane = (nx + 1 - d) if side < 0 else (2 + d)
            xmsg[s, e] = lroll(ext[f, plane, pl.ds(0, 16), :], -z_part(f))


def yz_kernel(mini_in, ra, rb, mini, za, zb, low, high, columns):
    lane = lane_ids(ROWS)
    low[...], high[...] = by_parity("gy", rb[pl.ds(0, low.shape[0]), :], ra[...])
    for side, msg in ((-1, low), (1, high)):
        entries = side_entries(1, side)
        for k in range(3):
            columns[pl.ds(8 * k, 8), :] = lroll(msg[pl.ds(0, 8), :], -32 * k)
        for e, (f, d) in enumerate(entries):
            mini[f, pl.ds(23 - d if side < 0 else 16 + d, 1), :] = columns[pl.ds(e, 1), :]
    tile_row = lax.broadcasted_iota(jnp.int32, (8, 128), 0)
    for side, msg in ((-1, za), (1, zb)):
        tiles = [None, None]
        for f, unit, kind in z_pieces(side):
            block, shift, slots = z_place(side, unit, kind)
            v = lroll(mini[f], shift)
            here = lane % 4 == slots[0]
            for k in slots[1:]:
                here = here | (lane % 4 == k)
            t = unit // 8
            tiles[t] = v if tiles[t] is None else jnp.where((lane // 32 == block) & here, v, tiles[t])
        msg[pl.ds(0, 16), :] = tiles[0][:16]
        msg[pl.ds(16, 8), :] = jnp.where((tile_row >= 2) & (tile_row < 6), pltpu.roll(tiles[1][16:], 4, 0), tiles[0][16:])
        msg[pl.ds(ROWS, 8), :] = jnp.where(lane[:8] < 64, tiles[1][:8], lroll(tiles[1][8:16], 64))


def y_kernel(ext, mini, msg):
    y_lines(ext, msg, -1, 1)


Z_PAIRS = ((5, 6), (11, 13), (14, 12), (15, 17), (18, 16))


def z_ends(above, below):
    return jnp.where(lane_ids(above.shape[0]) % 4 == 0, lroll(above, 62), below)


def close_pairs(p, pairs, ends, ext, rows):
    lane = lane_ids(rows.size)
    found = []
    for (up, down), e in zip(pairs, ends):
        g = lroll(e, 255 - 4 * p)
        found.append((up, jnp.where(lane == 127, g, ext[up, p, rows, :])))
        found.append((down, jnp.where(lane == 0, g, ext[down, p, rows, :])))
    return found


def zx_kernel(mini_in, ra, rb, ya, yb, mini, xmsg):
    lane = lane_ids(ROWS)
    for f in range(FIELDS):
        e = mini_in[f]
        if f == RHO or z_part(f) < 0:
            e = jnp.where(lane < 64, e, lroll(e, 64))
        mini[f] = e
    for side, msg in ((-1, ra), (1, rb)):
        second = msg[pl.ds(ROWS, 8), :]
        tiles = (msg[pl.ds(0, ROWS), :], jnp.concatenate([second, lroll(second, 64), pltpu.roll(msg[pl.ds(16, 8), :], 4, 0)], axis=0))
        start, slots = (8, (0, 1)) if side < 0 else (72, (2, 3))
        near = slots[1] if side < 0 else slots[0]
        inside = (lane >= start) & (lane < start + 32)
        for f, unit, kind in z_pieces(side):
            shift = z_place(side, unit, kind)[1]
            keep = inside & ((lane % 4 // 2 == slots[0] // 2) if kind == 0 else (lane % 4 == near))
            v = lroll(tiles[unit // 8], -shift + (0 if side < 0 else 64))
            mini[f] = jnp.where(keep, v, mini[f])
    group = (lane % 64) // 4
    for s, side in enumerate((-1, 1)):
        acc = None
        for groups, shift, parts in x_units(side):
            v = mini[parts[0][0]]
            for f, low, high in parts[1:]:
                v = jnp.where(slot_mask(lane, 0, low, high), mini[f], v)
            v = lroll(v, 4 * groups[0] - 4 * (9 if side < 0 else 2) + shift)
            if acc is None:
                acc = v
            else:
                here = any_group(group, groups)
                if parts[0][1:] == ((1,), (2,)):
                    here = here & slot_mask(lane, shift, (1,), (2,))
                acc = jnp.where(here, v, acc)
        xmsg[s, pl.ds(EDGE_LINES - 8, 8), :] = pltpu.roll(acc[16:], 6, 0)
        xmsg[s, pl.ds(EDGE_LINES, 16), :] = acc[:16]
        for k, msg in enumerate((ya, yb)):
            start = 8 + CORNER * s
            xmsg[s, pl.ds(CORNER * k, CORNER), :] = msg[pl.ds(start, CORNER), :]


def turn_kernel(ext_in, mini, ext, psi_ends, flux_ends, psi, zs, zd, ends):
    nx = ext.shape[1] - 4
    lane = lane_ids(16)
    rows = pl.ds(0, 16)
    for k, (up, down) in enumerate(Z_PAIRS):
        ends[k] = z_ends(mini[up, rows, :], mini[down, rows, :])

    def turn(p, _):
        found = []
        for k, (up, down) in enumerate(Z_PAIRS):
            g = lroll(ends[k], 255 - 4 * p)
            found.append((up, jnp.where(lane == 127, g, lroll(ext_in[up, p, rows, :], 127))))
            found.append((down, jnp.where(lane == 0, g, lroll(ext_in[down, p, rows, :], 1))))
        for f, v in found:
            ext[f, p, rows, :] = v
        return 0

    lax.fori_loop(2, nx + 2, turn, 0, unroll=2)
    psi_ends[...], flux_ends[...] = mini_adjoint(mini)
    for p in range(2, nx + 2):
        potential(p, ext, psi_ends, psi, zs, zd, rows)


def cell(b, rho, mom, psi, g):
    pairs = {}
    for i in range(1, 19, 2):
        pairs[i] = (b[i] + b[i + 1], b[i] - b[i + 1])
    s = {i: v[0] for i, v in pairs.items()}
    d = {i: v[1] for i, v in pairs.items()}
    sxy, sxz, syz = s[7] + s[9], s[11] + s[13], s[15] + s[17]
    a0 = W0 * b[0] + W1 * (s[1] + s[3] + s[5]) + W2 * (sxy + sxz + syz)
    a1 = (
        (3 * W1) * d[1] + (3 * W2) * ((d[7] + d[9]) + (d[11] + d[13])),
        (3 * W1) * d[3] + (3 * W2) * ((d[7] - d[9]) + (d[15] + d[17])),
        (3 * W1) * d[5] + (3 * W2) * ((d[11] - d[13]) + (d[15] - d[17])),
    )
    a03 = 3.0 * a0
    bxx = (9 * W1) * s[1] + (9 * W2) * (sxy + sxz) - a03
    byy = (9 * W1) * s[3] + (9 * W2) * (sxy + syz) - a03
    bzz = (9 * W1) * s[5] + (9 * W2) * (sxz + syz) - a03
    bxy = (9 * W2) * (s[7] - s[9])
    bxz = (9 * W2) * (s[11] - s[13])
    byz = (9 * W2) * (s[15] - s[17])
    force = [(-COUPLING * psi) * gk for gk in g]
    inv = 1.0 / rho
    u = [(m + 0.5 * fk) * inv for m, fk in zip(mom, force)]

    def apply(v):
        return (
            bxx * v[0] + bxy * v[1] + bxz * v[2],
            bxy * v[0] + byy * v[1] + byz * v[2],
            bxz * v[0] + byz * v[1] + bzz * v[2],
        )

    w = [p + q for p, q in zip(a1, apply(u))]
    bf = [(KAPPA * inv) * q for q in apply(force)]
    force_bar = [p + 0.5 * q for p, q in zip(w, bf)]
    return a0, a1, u, w, bf, force_bar


def dot(p, q):
    return p[0] * q[0] + p[1] * q[1] + p[2] * q[2]


def mini_adjoint(mini):
    def msh(v, c):
        return lroll(yroll(v, c[1]), -4 * c[0] - c[2])

    psi = 1.0 - jnp.exp(-mini[RHO])
    ys = yroll(psi, 1) + yroll(psi, -1)
    zsum = lroll(psi, -1) + lroll(psi, 1)
    xsum = lroll(psi, -4) + lroll(psi, 4)
    qx = W1 * psi + W2 * (ys + zsum)
    qy = W1 * psi + W2 * (xsum + zsum)
    qz = W1 * psi + W2 * (xsum + ys)
    g = (lroll(qx, -4) - lroll(qx, 4), yroll(qy, 1) - yroll(qy, -1), lroll(qz, -1) - lroll(qz, 1))
    b = [msh(mini[i], DIRECTIONS[i]) for i in range(19)]
    force_bar = cell(b, mini[RHO], [mini[MOM + k] for k in range(3)], psi, g)[5]
    fx, fy, fz = (psi * v for v in force_bar)
    across = W2 * ((lroll(fx, -4) - lroll(fx, 4)) + (yroll(fy, 1) - yroll(fy, -1)))
    along = W1 * fz + W2 * ((lroll(fz, -4) + lroll(fz, 4)) + (yroll(fz, 1) + yroll(fz, -1)))
    return z_ends(psi, psi), z_ends(across + along, across - along)


def zpair(above, below, ends, plane):
    lane = lane_ids(above.shape[0])
    g = lroll(ends, 255 - 4 * plane)
    return jnp.where(lane == 127, g, lroll(above, 127)), jnp.where(lane == 0, g, lroll(below, 1))


def potential(p, ext, ends, psi, zs, zd, rows):
    v = 1.0 - jnp.exp(-ext[RHO, p, rows, :])
    psi[p, rows, :] = v
    a, b = zpair(v, v, ends[rows, :], p)
    zs[p, rows, :] = a + b
    zd[p, rows, :] = a - b


def collide(p, ext, psi, zs, zd, flux, out):
    v, xp, xm = psi[p], psi[p + 1], psi[p - 1]
    qxp = W1 * xp + W2 * (yroll(xp, 1) + yroll(xp, -1) + zs[p + 1])
    qxm = W1 * xm + W2 * (yroll(xm, 1) + yroll(xm, -1) + zs[p - 1])
    qy = W1 * v + W2 * (xp + xm + zs[p])
    zz = zd[p]
    g = (
        qxp - qxm,
        yroll(qy, 1) - yroll(qy, -1),
        W1 * zz + W2 * (zd[p + 1] + zd[p - 1] + yroll(zz, 1) + yroll(zz, -1)),
    )
    b = [yroll(ext[i, p + DIRECTIONS[i][0]], DIRECTIONS[i][1]) for i in range(19)]
    a0, a1, u, w, bf, fb = cell(b, ext[RHO, p], [ext[MOM + k, p] for k in range(3)], v, g)
    for k in range(3):
        flux[k, p] = v * fb[k]

    def top(a):
        return a[:16]

    vv = [top(INV_TAU * wk + bk) for wk, bk in zip(w, bf)]
    uu = [top(a) for a in u]
    base = INV_TAU * (top(a0) + 0.5 * dot([top(r + q) for r, q in zip(a1, w)], uu)) - dot(vv, uu)
    base = base + (-COUPLING * (1.0 - top(v))) * top(dot(fb, g))
    for i in range(19):
        o = (1.0 - INV_TAU) * top(b[i]) + base
        for k in range(3):
            if DIRECTIONS[i][k] > 0:
                o = o + vv[k]
            elif DIRECTIONS[i][k] < 0:
                o = o - vv[k]
        out[i, p - 1] = o


def finish(p, psi, flux, ends, out):
    fx, fxm, fy = flux[0, p + 1], flux[0, p - 1], flux[1, p]
    fz = flux[2, p]
    xd = fx - fxm
    fyx = flux[1, p + 1] + flux[1, p - 1]
    dx = xd[:16]
    dy = (yroll(fy, 1) - yroll(fy, -1))[:16]
    here = W1 * (dx + dy) + W2 * (
        (yroll(xd, 1) + yroll(xd, -1))[:16] + (yroll(fyx, 1) - yroll(fyx, -1))[:16]
    )
    across = W2 * (dx + dy)
    along = W1 * fz[:16] + W2 * (flux[2, p + 1, pl.ds(0, 16), :] + flux[2, p - 1, pl.ds(0, 16), :] + (yroll(fz, 1) + yroll(fz, -1))[:16])
    a, b = zpair(across + along, across - along, ends[pl.ds(0, 16), :], p)
    term = (COUPLING * (1.0 - psi[p, pl.ds(0, 16), :])) * (here + (a + b))
    for i in range(19):
        out[i, p - 1] = out[i, p - 1] + term


def planes(count, of, step, unroll=4):
    def body(k, _):
        step(of(k))
        return 0

    lax.fori_loop(0, count, body, 0, unroll=unroll)


def send_planes(out, out_hbm, sem, first, count):
    return pltpu.make_async_copy(out.at[:, pl.ds(first - 1, count)], out_hbm.at[:, pl.ds(first - 2, count)], sem)


def mid_kernel(ext_in, mini, sa, sb, r2, rb, psi_ends, flux_ends, psi_in, zs_in, zd_in, ext, psi, zs, zd, flux, out, ends, low, high):
    nx = ext.shape[1] - 4
    rows = pl.ds(16, 8)
    low[...], high[...] = by_parity("gy", rb[pl.ds(sa.shape[0], low.shape[0]), :], r2[...])
    for up, small, large in ((-1, sa, low), (1, sb, high)):
        for e, (f, d, first) in enumerate(y_entries(up)):
            ext[f, pl.ds(first, nx - 2), 23 - d if up < 0 else 16 + d, :] = large[pl.ds((nx - 2) * e, nx - 2), :]
        lines = [(side, *entry) for side in (-1, 1) for entry in edge_entries(side, up)]
        for e, (side, f, dx, dy) in enumerate(lines):
            plane, row = nx + 1 - dx if side < 0 else 2 + dx, 23 - dy if up < 0 else 16 + dy
            ext[f, plane, pl.ds(row, 1), :] = small[pl.ds(8 + e, 1), :]
    for k, (up, down) in enumerate(Z_PAIRS):
        ends[k] = z_ends(mini[up, rows, :], mini[down, rows, :])

    def close(p, _):
        for f, v in close_pairs(p, Z_PAIRS, [ends[k] for k in range(len(Z_PAIRS))], ext, rows):
            ext[f, p, rows, :] = v
        return 0

    lax.fori_loop(2, nx + 2, close, 0, unroll=4)
    for p in range(2, nx + 2):
        potential(p, ext, psi_ends, psi, zs, zd, rows)
    planes(nx - 2, lambda k: k + 3, lambda p: collide(p, ext, psi, zs, zd, flux, out))

    planes(nx - 4, lambda k: k + 4, lambda p: finish(p, psi, flux, flux_ends, out))


def fill_kernel(ext_in, r1, ext):
    nx = ext.shape[1] - 4
    for s, side in enumerate((-1, 1)):
        for e, (f, d) in enumerate(side_entries(0, side)):
            ext[f, 1 - d if side < 0 else nx + 2 + d, pl.ds(0, 16), :] = r1[s, e]


def last_kernel(ext_in, mini_in, r2, psi_in, zs_in, zd_in, flux_in, out_in, ext, mini, psi, zs, zd, flux, out, out_hbm, psi_ends, flux_ends, sems):
    nx = ext.shape[1] - 4
    copies = [
        send_planes(out, out_hbm, sems.at[k], first, count) for k, (first, count) in enumerate(((4, nx - 4), (2, 2), (nx, 2)))
    ]
    copies[0].start()
    lane = lane_ids(ROWS)
    group = (lane % 64) // 4
    for s, side in enumerate((-1, 1)):
        lines = [(up, *entry) for up in (-1, 1) for entry in edge_entries(side, up)]
        for e, (up, f, dx, dy) in enumerate(lines):
            plane, row = 1 - dx if side < 0 else nx + 2 + dx, 23 - dy if up < 0 else 16 + dy
            ext[f, plane, pl.ds(row, 1), :] = r2[s, pl.ds(e, 1), :]
        small = jnp.concatenate([r2[s, pl.ds(EDGE_LINES, 16), :], pltpu.roll(r2[s, pl.ds(EDGE_LINES - 8, 8), :], 2, 0)], axis=0)
        for groups, shift, parts in x_units(side):
            near = 1 if side < 0 else nx + 2
            here = any_group(group, (near, near + side)[: len(groups)])
            v = lroll(small, 4 * near - 4 * groups[0] - shift)
            for f, low, high in parts:
                mini[f] = jnp.where(here & slot_mask(lane, 0, low, high), v, mini[f])
    ends = [z_ends(mini[up], mini[down]) for up, down in Z_PAIRS]
    for p in (0, 1, nx + 2, nx + 3):
        keep = [k for k, (f, _) in enumerate(Z_PAIRS) if DIRECTIONS[f][0] == (-1 if p < 2 else 1) or (p in (1, nx + 2) and DIRECTIONS[f][0] == 0)]
        for f, v in close_pairs(p, [Z_PAIRS[k] for k in keep], [ends[k] for k in keep], ext, pl.ds(0, ROWS)):
            ext[f, p] = v
    psi_ends[...], flux_ends[...] = mini_adjoint(mini)
    for p in (0, 1, nx + 2, nx + 3):
        potential(p, ext, psi_ends, psi, zs, zd, pl.ds(0, ROWS))

    def outer(low, k):
        return low + k + jnp.where(k >= 2, nx - 2, 0)

    planes(4, lambda k: outer(1, k), lambda p: collide(p, ext, psi, zs, zd, flux, out))
    planes(4, lambda k: outer(2, k) - jnp.where(k >= 2, 2, 0), lambda p: finish(p, psi, flux, flux_ends, out))
    for copy in copies[1:]:
        copy.start()
    for copy in copies:
        copy.wait()


def swap(low, high, axis):
    n = lax.axis_size(axis)
    up = [(i, (i + 1) % n) for i in range(n)]
    return lax.ppermute(low, axis, up), lax.ppermute(high, axis, [(j, i) for i, j in up])


def ppermute_pairs(msg, axis, first):
    n = lax.axis_size(axis)
    found = []
    for i in range(first, n + first, 2):
        found += [(i % n, (i + 1) % n), ((i + 1) % n, i % n)]
    return lax.ppermute(msg, axis, found)


def swap_both(msg, axis):
    n = lax.axis_size(axis)
    if n == 2:
        return lax.ppermute(msg, axis, [(0, 1), (1, 0)])
    return jnp.stack(swap(msg[0], msg[1], axis))


def per_device(populations, adjoint_next):
    nx = populations.shape[1]
    ext_shape, mini_shape, plane_shape = (FIELDS, nx + 4, ROWS, 128), (FIELDS, ROWS, 128), (nx + 4, ROWS, 128)
    small_y = (8 + EDGE_LINES, 128)
    ext, mini, ya, yb = call(
        load_kernel,
        tuple(pltpu.with_memory_space_constraint(v, pltpu.HBM) for v in (populations, adjoint_next)),
        (ext_shape, mini_shape, small_y, small_y),
        scratch=[pltpu.VMEM((19, nx, 16, 128), F32), pltpu.VMEM((24, 128), F32), pltpu.SemaphoreType.DMA((10,))],
        in_specs=[HB, HB],
        name="load",
    )
    large_y = (24 * (nx - 2) + 8, 128)
    (yb,) = call(
        pair_kernel, (ext, yb), ((small_y[0] + large_y[0], 128),), name="pair", cost=COSTLY
    )
    (xmsg,) = call(x_kernel, (ext,), ((2, 24, 16, 128),), name="xpack", cost=COSTLY)
    x1 = swap_both(xmsg, "gx")
    ya, y2b = ppermute_pairs(ya, "gy", 1), ppermute_pairs(yb, "gy", 0)
    mini, za, zb, ya, yb = call(
        yz_kernel,
        (mini, ya, y2b),
        (mini_shape, (ROWS + 8, 128), (ROWS + 8, 128), small_y, small_y),
        scratch=[pltpu.VMEM((24, 128), F32)],
        aliases={0: 0},
        name="yz",
    )
    (y2a,) = call(y_kernel, (ext, mini), (large_y,), name="ypack", cost=COSTLY)
    y2a = ppermute_pairs(y2a, "gy", 1)
    za, zb = swap(za, zb, "gz")
    mini, xmsg2 = call(
        zx_kernel,
        (mini, za, zb, ya, yb),
        (mini_shape, (2, EDGE_LINES + 16, 128)),
        aliases={0: 0},
        name="zx",
    )
    tile, out_shape = (ROWS, 128), (19, nx + 2, 16, 128)
    ext, psi_ends, flux_ends, psi, zs, zd = call(
        turn_kernel,
        (ext, mini),
        (ext_shape, tile, tile, plane_shape, plane_shape, plane_shape),
        scratch=[pltpu.VMEM((len(Z_PAIRS), 16, 128), F32)],
        aliases={0: 0},
        name="turn",
    )
    x2 = swap_both(xmsg2, "gx")
    ext, psi, zs, zd, flux, part = call(
        mid_kernel,
        (ext, mini, ya, yb, y2a, y2b, psi_ends, flux_ends, psi, zs, zd),
        (ext_shape, plane_shape, plane_shape, plane_shape, (3, *plane_shape), out_shape),
        scratch=[pltpu.VMEM(v, F32) for v in ((len(Z_PAIRS), 8, 128), large_y, large_y)],
        aliases={0: 0, 8: 1, 9: 2, 10: 3},
        name="mid",
    )
    (ext,) = call(fill_kernel, (ext, x1), (ext_shape,), aliases={0: 0}, name="fill")
    return call(
        last_kernel,
        (ext, mini, x2, psi, zs, zd, flux, part),
        (ext_shape, mini_shape, plane_shape, plane_shape, plane_shape, (3, *plane_shape), out_shape, populations.shape),
        scratch=[pltpu.VMEM(tile, F32), pltpu.VMEM(tile, F32), pltpu.SemaphoreType.DMA((3,))],
        aliases={0: 0, 1: 1, 3: 2, 4: 3, 5: 4, 6: 5, 7: 6},
        out_specs=[VM] * 7 + [HB],
        name="last",
    )[-1]


def solution(mesh):
    return jax.shard_map(
        per_device,
        mesh=mesh,
        in_specs=(P(None, "gx", "gy", "gz"), P(None, "gx", "gy", "gz")),
        out_specs=P(None, "gx", "gy", "gz"),
        check_vma=False,
    )
```

```python
import jax
import jax.numpy as jnp
from jax import lax
from jax.experimental import pallas as pl
from jax.experimental.pallas import tpu as pltpu
from jax.sharding import PartitionSpec as P

DIRECTIONS = (
    (0, 0, 0),
    (1, 0, 0),
    (-1, 0, 0),
    (0, 1, 0),
    (0, -1, 0),
    (0, 0, 1),
    (0, 0, -1),
    (1, 1, 0),
    (-1, -1, 0),
    (1, -1, 0),
    (-1, 1, 0),
    (1, 0, 1),
    (-1, 0, -1),
    (1, 0, -1),
    (-1, 0, 1),
    (0, 1, 1),
    (0, -1, -1),
    (0, 1, -1),
    (0, -1, 1),
)
W0, W1, W2 = 1.0 / 3.0, 1.0 / 18.0, 1.0 / 36.0
RELAX_TIME = 0.8
COUPLING = -5.5
INV_TAU = 1.0 / RELAX_TIME
KAPPA = 1.0 - 0.5 / RELAX_TIME

RHO, MOM, FIELDS = 19, 20, 23
ROWS = 24
F32 = jnp.float32
COSTLY = pl.CostEstimate(flops=10**10, bytes_accessed=10**6, transcendentals=0)
VM = pl.BlockSpec(memory_space=pltpu.VMEM)
HB = pl.BlockSpec(memory_space=pltpu.HBM)


def deep_fields(dim, side):
    return [i for i in range(19) if DIRECTIONS[i][dim] == side] + [RHO]


def side_fields(dim, side):
    return deep_fields(dim, side) + [i for i in range(19) if DIRECTIONS[i][dim] == 0] + [MOM, MOM + 1, MOM + 2]


def side_entries(dim, side):
    return [(f, d) for d in (0, 1) for f in (side_fields(dim, side) if d == 0 else deep_fields(dim, side))]


def edge_entries(side, up):
    found = []
    for dx in (0, 1):
        for dy in (0, 1):
            across = deep_fields(0, side) if dx else side_fields(0, side)
            along = deep_fields(1, up) if dy else side_fields(1, up)
            found += [(f, dx, dy) for f in across if f in along]
    return sorted(found, key=lambda entry: z_part(entry[0]))


def z_pieces(side):
    deep = deep_fields(2, side)
    shallow = side_fields(2, side)[len(deep) :]
    found = [(f, u, 0) for u, f in enumerate(deep)]
    return found + [(f, len(deep) + k // 2, 1 + k % 2) for k, f in enumerate(shallow)]


def z_place(side, unit, kind):
    block, pair = unit % 8 // 2, unit % 2
    start = 32 * block + 2 * pair
    if side < 0:
        shift, slots = start - 8, {0: (0, 1), 1: (1,), 2: (0,)}[kind]
        shift -= kind == 2
    else:
        shift, slots = start - 10, {0: (0, 1), 1: (0,), 2: (1,)}[kind]
        shift += kind == 2
    return block, shift, [2 * pair + k for k in slots]


def x_units(side):
    found, group = [], 0
    deep = deep_fields(0, side)
    for depths, fields in ((2, deep), (1, side_fields(0, side)[len(deep) :])):
        up = [f for f in fields if z_part(f) > 0]
        down = [f for f in fields if z_part(f) < 0]
        flat = [f for f in fields if f != RHO and z_part(f) == 0]
        sets = [[(0, ((a, (2,), (2, 3)), (b, (0, 1), (1,))))] for a, b in zip(up, down)]
        for k in range(0, len(flat), 3):
            sets.append([(n - 1, ((f, (1,), (2,)),)) for n, f in enumerate(flat[k : k + 3])])
        if RHO in fields:
            sets.append([(0, ((RHO, (0, 1, 2), (1, 2, 3)),))])
        for units in sets:
            groups = (group,) if depths == 1 else (group + 1, group) if side < 0 else (group, group + 1)
            found += [(groups, shift, parts) for shift, parts in units]
            group += depths
    assert group <= 16
    return found


def any_group(group, groups):
    hit = group == groups[0]
    for g in groups[1:]:
        hit = hit | (group == g)
    return hit


def slot_mask(lane, shift, low, high):
    four = lane % 4
    inside = [None, None]
    for half, slots in enumerate((low, high)):
        for k in slots:
            hit = four == k + shift
            inside[half] = hit if inside[half] is None else inside[half] | hit
    return ((lane < 64) & inside[0]) | ((lane >= 64) & inside[1])


def z_part(f):
    return DIRECTIONS[f][2] if f < 19 else 0


CORNER = len(edge_entries(1, 1))
EDGE_LINES = -(-(2 * CORNER + 4) // 8) * 8


def by_parity(axis, v, w):
    odd = jnp.full(v.shape, lax.axis_index(axis) % 2, jnp.int32) == 1
    return jnp.where(odd, v, w), jnp.where(odd, w, v)


def lane_ids(rows):
    return lax.broadcasted_iota(jnp.int32, (rows, 128), 1)


def lroll(v, amount):
    amount = amount % 128
    return v if isinstance(amount, int) and amount == 0 else pltpu.roll(v, amount, 1)


def yroll(v, c):
    return v if c == 0 else pltpu.roll(v, (-c) % ROWS, 0)


def call(body, ins, outs, scratch=(), aliases=None, name=None, in_specs=None, out_specs=None, cost=None):
    return pl.pallas_call(
        body,
        in_specs=in_specs or [VM] * len(ins),
        out_specs=out_specs or [VM] * len(outs),
        out_shape=[jax.ShapeDtypeStruct(s, F32) for s in outs],
        scratch_shapes=list(scratch),
        input_output_aliases=aliases or {},
        name=name,
        cost_estimate=cost,
        compiler_params=pltpu.CompilerParams(vmem_limit_bytes=20 * 2**20),
    )(*ins)


def load_kernel(pop_hbm, adj_hbm, ext, mini, ya, yb, pops, sems):
    nx = pop_hbm.shape[1]
    lane = lane_ids(16)
    group = lane // 4
    chunks = [(f, min(4, 19 - f)) for f in range(0, 19, 4)]
    copies = []
    for k, (f, n) in enumerate(chunks):
        own = ext.at[pl.ds(f, n), pl.ds(2, nx), pl.ds(0, 16), :]
        copies.append(pltpu.make_async_copy(adj_hbm.at[pl.ds(f, n)], own, sems.at[k]))
    for k, (f, n) in enumerate(chunks):
        copies.append(pltpu.make_async_copy(pop_hbm.at[pl.ds(f, n)], pops.at[pl.ds(f, n)], sems.at[5 + k]))
    for c in copies:
        c.start()

    def edges(f):
        e = lroll(ext[f, 2, pl.ds(0, 16), :], 10)
        for x in range(1, nx):
            e = jnp.where(group == x + 2, lroll(ext[f, x + 2, pl.ds(0, 16), :], 4 * x + 10), e)
        mini[f, pl.ds(0, 16), :] = e

    for k, (f, n) in enumerate(chunks):
        copies[k].wait()
        for i in range(n):
            edges(f + i)

    def y_edges(wanted):
        for up, msg in ((-1, ya), (1, yb)):
            entries = side_entries(1, up)
            for e, (f, d) in enumerate(entries):
                if wanted(f):
                    msg[pl.ds(e, 1), :] = mini[f, pl.ds(15 - d if up < 0 else d, 1), :]
            lines = [(side, *entry) for side in (-1, 1) for entry in edge_entries(side, up)]
            for e, (side, f, dx, dy) in enumerate(lines):
                plane = nx + 1 - dx if side < 0 else 2 + dx
                if wanted(f):
                    msg[pl.ds(len(entries) + e, 1), :] = ext[f, plane, pl.ds(15 - dy if up < 0 else dy, 1), :]

    y_edges(lambda f: f < RHO)
    place = lax.broadcasted_iota(jnp.int32, (EDGE_LINES, 128), 0)
    for up, msg in ((-1, ya), (1, yb)):
        entries = side_entries(1, up)
        lines = [(side, *entry) for side in (-1, 1) for entry in edge_entries(side, up)]
        v = msg[pl.ds(len(entries), EDGE_LINES), :]
        turned = v
        for step in (-1, 1):
            here = None
            for k in (0, 1):
                hits = [e for e in range(CORNER) if z_part(lines[CORNER * k + e][1]) == step]
                hit = (place >= CORNER * k + hits[0]) & (place <= CORNER * k + hits[-1])
                here = hit if here is None else here | hit
            turned = jnp.where(here, lroll(v, -step), turned)
        msg[pl.ds(len(entries), EDGE_LINES), :] = turned
    for c in copies[5:]:
        c.wait()

    def moments(x, _):
        rho = pops[0, x]
        mom = [None] * 3
        for i in range(1, 19):
            p = pops[i, x]
            rho = rho + p
            for k in range(3):
                c = DIRECTIONS[i][k]
                if c:
                    mom[k] = (p if c > 0 else -p) if mom[k] is None else (mom[k] + p if c > 0 else mom[k] - p)
        ext[RHO, x + 2, pl.ds(0, 16), :] = rho
        for k in range(3):
            ext[MOM + k, x + 2, pl.ds(0, 16), :] = mom[k]
        return 0

    lax.fori_loop(0, nx, moments, 0, unroll=2)
    for f in range(RHO, FIELDS):
        edges(f)
    y_edges(lambda f: f >= RHO)
    ya[...], yb[...] = by_parity("gy", ya[...], yb[...])


def y_entries(side):
    found = []
    for f, d in side_entries(1, side):
        cx = DIRECTIONS[f][0] if f < 19 else 0
        found.append((f, d, 3 + cx))
    return sorted(found, key=lambda entry: z_part(entry[0]))


def y_lines(ext, msg, on_odd, on_even):
    six = ext.shape[1] - 6

    def fill(side):
        entries = y_entries(side)
        for e, (f, d, first) in enumerate(entries):
            msg[pl.ds(six * e, six), :] = ext[f, pl.ds(first, six), 15 - d if side < 0 else d, :]
        msg[pl.ds(six * len(entries), 8), :] = jnp.zeros((8, 128), F32)
        for step in (-1, 1):
            hits = [e for e, (f, _, _) in enumerate(entries) if z_part(f) == step]
            start, stop = six * hits[0], six * (hits[-1] + 1)
            bottom, top = start // 8 * 8, -(-stop // 8) * 8
            v = msg[pl.ds(bottom, top - bottom), :]
            place = bottom + lax.broadcasted_iota(jnp.int32, v.shape, 0)
            msg[pl.ds(bottom, top - bottom), :] = jnp.where((place >= start) & (place < stop), lroll(v, -step), v)

    odd = lax.axis_index("gy") % 2
    pl.when(odd == 1)(lambda: fill(on_odd))
    pl.when(odd == 0)(lambda: fill(on_even))


def pair_kernel(ext, small, msg):
    msg[pl.ds(0, small.shape[0]), :] = small[...]
    y_lines(ext, msg.at[pl.ds(small.shape[0], msg.shape[0] - small.shape[0]), :], 1, -1)


def x_kernel(ext, xmsg):
    nx = ext.shape[1] - 4
    for s, side in enumerate((-1, 1)):
        for e, (f, d) in enumerate(side_entries(0, side)):
            plane = (nx + 1 - d) if side < 0 else (2 + d)
            xmsg[s, e] = lroll(ext[f, plane, pl.ds(0, 16), :], -z_part(f))


def yz_kernel(mini_in, ra, rb, mini, za, zb, low, high):
    lane = lane_ids(ROWS)
    low[...], high[...] = by_parity("gy", rb[pl.ds(0, low.shape[0]), :], ra[...])
    for side, msg in ((-1, low), (1, high)):
        entries = side_entries(1, side)
        for e, (f, d) in enumerate(entries):
            mini[f, pl.ds(23 - d if side < 0 else 16 + d, 1), :] = msg[pl.ds(e, 1), :]
    for side, msg in ((-1, za), (1, zb)):
        tiles = [None, None]
        for f, unit, kind in z_pieces(side):
            block, shift, slots = z_place(side, unit, kind)
            v = lroll(mini[f], shift)
            here = lane % 4 == slots[0]
            for k in slots[1:]:
                here = here | (lane % 4 == k)
            t = unit // 8
            tiles[t] = v if tiles[t] is None else jnp.where((lane // 32 == block) & here, v, tiles[t])
        msg[pl.ds(0, ROWS), :] = tiles[0]
        msg[pl.ds(ROWS, 8), :] = jnp.where(lane[:8] < 64, tiles[1][:8], lroll(tiles[1][8:16], 64))
        msg[pl.ds(ROWS + 8, 8), :] = tiles[1][16:]


def y_kernel(ext, mini, msg):
    y_lines(ext, msg, -1, 1)


Z_PAIRS = ((5, 6), (11, 13), (14, 12), (15, 17), (18, 16))


def z_ends(above, below):
    return jnp.where(lane_ids(above.shape[0]) % 4 == 0, lroll(above, 62), below)


def close_pairs(p, pairs, ends, ext, rows):
    lane = lane_ids(rows.size)
    found = []
    for (up, down), e in zip(pairs, ends):
        g = lroll(e, 255 - 4 * p)
        found.append((up, jnp.where(lane == 127, g, ext[up, p, rows, :])))
        found.append((down, jnp.where(lane == 0, g, ext[down, p, rows, :])))
    return found


def zx_kernel(mini_in, ra, rb, ya, yb, mini, xmsg):
    lane = lane_ids(ROWS)
    for f in range(FIELDS):
        e = mini_in[f]
        if f == RHO or z_part(f) < 0:
            e = jnp.where(lane < 64, e, lroll(e, 64))
        mini[f] = e
    for side, msg in ((-1, ra), (1, rb)):
        second = msg[pl.ds(ROWS, 8), :]
        tiles = (msg[pl.ds(0, ROWS), :], jnp.concatenate([second, lroll(second, 64), msg[pl.ds(ROWS + 8, 8), :]], axis=0))
        start, slots = (8, (0, 1)) if side < 0 else (72, (2, 3))
        near = slots[1] if side < 0 else slots[0]
        inside = (lane >= start) & (lane < start + 32)
        for f, unit, kind in z_pieces(side):
            shift = z_place(side, unit, kind)[1]
            keep = inside & ((lane % 4 // 2 == slots[0] // 2) if kind == 0 else (lane % 4 == near))
            v = lroll(tiles[unit // 8], -shift + (0 if side < 0 else 64))
            mini[f] = jnp.where(keep, v, mini[f])
    group = (lane % 64) // 4
    for s, side in enumerate((-1, 1)):
        acc = None
        for groups, shift, parts in x_units(side):
            v = mini[parts[0][0]]
            for f, low, high in parts[1:]:
                v = jnp.where(slot_mask(lane, 0, low, high), mini[f], v)
            v = lroll(v, 4 * groups[0] - 4 * (9 if side < 0 else 2) + shift)
            if acc is None:
                acc = v
            else:
                here = any_group(group, groups)
                if parts[0][1:] == ((1,), (2,)):
                    here = here & slot_mask(lane, shift, (1,), (2,))
                acc = jnp.where(here, v, acc)
        xmsg[s, pl.ds(EDGE_LINES - 8, 8), :] = pltpu.roll(acc[16:], 6, 0)
        xmsg[s, pl.ds(EDGE_LINES, 16), :] = acc[:16]
        for k, msg in enumerate((ya, yb)):
            start = len(side_entries(1, 1)) + CORNER * s
            xmsg[s, pl.ds(CORNER * k, CORNER), :] = msg[pl.ds(start, CORNER), :]


def turn_kernel(ext_in, mini, ext, psi_ends, flux_ends, psi, zs, zd, ends):
    nx = ext.shape[1] - 4
    lane = lane_ids(16)
    rows = pl.ds(0, 16)
    for k, (up, down) in enumerate(Z_PAIRS):
        ends[k] = z_ends(mini[up, rows, :], mini[down, rows, :])

    def turn(p, _):
        found = []
        for k, (up, down) in enumerate(Z_PAIRS):
            g = lroll(ends[k], 255 - 4 * p)
            found.append((up, jnp.where(lane == 127, g, lroll(ext_in[up, p, rows, :], 127))))
            found.append((down, jnp.where(lane == 0, g, lroll(ext_in[down, p, rows, :], 1))))
        for f, v in found:
            ext[f, p, rows, :] = v
        return 0

    lax.fori_loop(2, nx + 2, turn, 0, unroll=2)
    psi_ends[...], flux_ends[...] = mini_adjoint(mini)
    for p in range(2, nx + 2):
        potential(p, ext, psi_ends, psi, zs, zd, rows)


def cell(b, rho, mom, psi, g):
    pairs = {}
    for i in range(1, 19, 2):
        pairs[i] = (b[i] + b[i + 1], b[i] - b[i + 1])
    s = {i: v[0] for i, v in pairs.items()}
    d = {i: v[1] for i, v in pairs.items()}
    sxy, sxz, syz = s[7] + s[9], s[11] + s[13], s[15] + s[17]
    a0 = W0 * b[0] + W1 * (s[1] + s[3] + s[5]) + W2 * (sxy + sxz + syz)
    a1 = (
        (3 * W1) * d[1] + (3 * W2) * ((d[7] + d[9]) + (d[11] + d[13])),
        (3 * W1) * d[3] + (3 * W2) * ((d[7] - d[9]) + (d[15] + d[17])),
        (3 * W1) * d[5] + (3 * W2) * ((d[11] - d[13]) + (d[15] - d[17])),
    )
    a03 = 3.0 * a0
    bxx = (9 * W1) * s[1] + (9 * W2) * (sxy + sxz) - a03
    byy = (9 * W1) * s[3] + (9 * W2) * (sxy + syz) - a03
    bzz = (9 * W1) * s[5] + (9 * W2) * (sxz + syz) - a03
    bxy = (9 * W2) * (s[7] - s[9])
    bxz = (9 * W2) * (s[11] - s[13])
    byz = (9 * W2) * (s[15] - s[17])
    force = [(-COUPLING * psi) * gk for gk in g]
    inv = 1.0 / rho
    u = [(m + 0.5 * fk) * inv for m, fk in zip(mom, force)]

    def apply(v):
        return (
            bxx * v[0] + bxy * v[1] + bxz * v[2],
            bxy * v[0] + byy * v[1] + byz * v[2],
            bxz * v[0] + byz * v[1] + bzz * v[2],
        )

    w = [p + q for p, q in zip(a1, apply(u))]
    bf = [(KAPPA * inv) * q for q in apply(force)]
    force_bar = [p + 0.5 * q for p, q in zip(w, bf)]
    return a0, a1, u, w, bf, force_bar


def dot(p, q):
    return p[0] * q[0] + p[1] * q[1] + p[2] * q[2]


def mini_adjoint(mini):
    def msh(v, c):
        return lroll(yroll(v, c[1]), -4 * c[0] - c[2])

    psi = 1.0 - jnp.exp(-mini[RHO])
    ys = yroll(psi, 1) + yroll(psi, -1)
    zsum = lroll(psi, -1) + lroll(psi, 1)
    xsum = lroll(psi, -4) + lroll(psi, 4)
    qx = W1 * psi + W2 * (ys + zsum)
    qy = W1 * psi + W2 * (xsum + zsum)
    qz = W1 * psi + W2 * (xsum + ys)
    g = (lroll(qx, -4) - lroll(qx, 4), yroll(qy, 1) - yroll(qy, -1), lroll(qz, -1) - lroll(qz, 1))
    b = [msh(mini[i], DIRECTIONS[i]) for i in range(19)]
    force_bar = cell(b, mini[RHO], [mini[MOM + k] for k in range(3)], psi, g)[5]
    fx, fy, fz = (psi * v for v in force_bar)
    across = W2 * ((lroll(fx, -4) - lroll(fx, 4)) + (yroll(fy, 1) - yroll(fy, -1)))
    along = W1 * fz + W2 * ((lroll(fz, -4) + lroll(fz, 4)) + (yroll(fz, 1) + yroll(fz, -1)))
    return z_ends(psi, psi), z_ends(across + along, across - along)


def zpair(above, below, ends, plane):
    lane = lane_ids(above.shape[0])
    g = lroll(ends, 255 - 4 * plane)
    return jnp.where(lane == 127, g, lroll(above, 127)), jnp.where(lane == 0, g, lroll(below, 1))


def potential(p, ext, ends, psi, zs, zd, rows):
    v = 1.0 - jnp.exp(-ext[RHO, p, rows, :])
    psi[p, rows, :] = v
    a, b = zpair(v, v, ends[rows, :], p)
    zs[p, rows, :] = a + b
    zd[p, rows, :] = a - b


def collide(p, ext, psi, zs, zd, flux, out):
    v, xp, xm = psi[p], psi[p + 1], psi[p - 1]
    qxp = W1 * xp + W2 * (yroll(xp, 1) + yroll(xp, -1) + zs[p + 1])
    qxm = W1 * xm + W2 * (yroll(xm, 1) + yroll(xm, -1) + zs[p - 1])
    qy = W1 * v + W2 * (xp + xm + zs[p])
    zz = zd[p]
    g = (
        qxp - qxm,
        yroll(qy, 1) - yroll(qy, -1),
        W1 * zz + W2 * (zd[p + 1] + zd[p - 1] + yroll(zz, 1) + yroll(zz, -1)),
    )
    b = [yroll(ext[i, p + DIRECTIONS[i][0]], DIRECTIONS[i][1]) for i in range(19)]
    a0, a1, u, w, bf, fb = cell(b, ext[RHO, p], [ext[MOM + k, p] for k in range(3)], v, g)
    for k in range(3):
        flux[k, p] = v * fb[k]

    def top(a):
        return a[:16]

    vv = [top(INV_TAU * wk + bk) for wk, bk in zip(w, bf)]
    uu = [top(a) for a in u]
    base = INV_TAU * (top(a0) + 0.5 * dot([top(r + q) for r, q in zip(a1, w)], uu)) - dot(vv, uu)
    base = base + (-COUPLING * (1.0 - top(v))) * top(dot(fb, g))
    for i in range(19):
        o = (1.0 - INV_TAU) * top(b[i]) + base
        for k in range(3):
            if DIRECTIONS[i][k] > 0:
                o = o + vv[k]
            elif DIRECTIONS[i][k] < 0:
                o = o - vv[k]
        out[i, p - 1] = o


def finish(p, psi, flux, ends, out):
    fx, fxm, fy = flux[0, p + 1], flux[0, p - 1], flux[1, p]
    fz = flux[2, p]
    xd = fx - fxm
    fyx = flux[1, p + 1] + flux[1, p - 1]
    dx = xd[:16]
    dy = (yroll(fy, 1) - yroll(fy, -1))[:16]
    here = W1 * (dx + dy) + W2 * (
        (yroll(xd, 1) + yroll(xd, -1))[:16] + (yroll(fyx, 1) - yroll(fyx, -1))[:16]
    )
    across = W2 * (dx + dy)
    along = W1 * fz[:16] + W2 * (flux[2, p + 1, pl.ds(0, 16), :] + flux[2, p - 1, pl.ds(0, 16), :] + (yroll(fz, 1) + yroll(fz, -1))[:16])
    a, b = zpair(across + along, across - along, ends[pl.ds(0, 16), :], p)
    term = (COUPLING * (1.0 - psi[p, pl.ds(0, 16), :])) * (here + (a + b))
    for i in range(19):
        out[i, p - 1] = out[i, p - 1] + term


def planes(count, of, step, unroll=4):
    def body(k, _):
        step(of(k))
        return 0

    lax.fori_loop(0, count, body, 0, unroll=unroll)


def send_planes(out, out_hbm, sem, first, count):
    return pltpu.make_async_copy(out.at[:, pl.ds(first - 1, count)], out_hbm.at[:, pl.ds(first - 2, count)], sem)


def mid_kernel(ext_in, mini, sa, sb, r2, rb, psi_ends, flux_ends, psi_in, zs_in, zd_in, ext, psi, zs, zd, flux, out, ends, low, high):
    nx = ext.shape[1] - 4
    rows = pl.ds(16, 8)
    low[...], high[...] = by_parity("gy", rb[pl.ds(sa.shape[0], low.shape[0]), :], r2[...])
    for up, small, large in ((-1, sa, low), (1, sb, high)):
        for e, (f, d, first) in enumerate(y_entries(up)):
            ext[f, pl.ds(first, nx - 2), 23 - d if up < 0 else 16 + d, :] = large[pl.ds((nx - 2) * e, nx - 2), :]
        lines = [(side, *entry) for side in (-1, 1) for entry in edge_entries(side, up)]
        for e, (side, f, dx, dy) in enumerate(lines):
            plane, row = nx + 1 - dx if side < 0 else 2 + dx, 23 - dy if up < 0 else 16 + dy
            ext[f, plane, pl.ds(row, 1), :] = small[pl.ds(len(side_entries(1, up)) + e, 1), :]
    for k, (up, down) in enumerate(Z_PAIRS):
        ends[k] = z_ends(mini[up, rows, :], mini[down, rows, :])

    def close(p, _):
        for f, v in close_pairs(p, Z_PAIRS, [ends[k] for k in range(len(Z_PAIRS))], ext, rows):
            ext[f, p, rows, :] = v
        return 0

    lax.fori_loop(2, nx + 2, close, 0, unroll=4)
    for p in range(2, nx + 2):
        potential(p, ext, psi_ends, psi, zs, zd, rows)
    planes(nx - 2, lambda k: k + 3, lambda p: collide(p, ext, psi, zs, zd, flux, out))

    planes(nx - 4, lambda k: k + 4, lambda p: finish(p, psi, flux, flux_ends, out))


def fill_kernel(ext_in, r1, ext):
    nx = ext.shape[1] - 4
    for s, side in enumerate((-1, 1)):
        for e, (f, d) in enumerate(side_entries(0, side)):
            ext[f, 1 - d if side < 0 else nx + 2 + d, pl.ds(0, 16), :] = r1[s, e]


def last_kernel(ext_in, mini_in, r2, psi_in, zs_in, zd_in, flux_in, out_in, ext, mini, psi, zs, zd, flux, out, out_hbm, psi_ends, flux_ends, sems):
    nx = ext.shape[1] - 4
    copies = [
        send_planes(out, out_hbm, sems.at[k], first, count) for k, (first, count) in enumerate(((4, nx - 4), (2, 2), (nx, 2)))
    ]
    copies[0].start()
    lane = lane_ids(ROWS)
    group = (lane % 64) // 4
    for s, side in enumerate((-1, 1)):
        lines = [(up, *entry) for up in (-1, 1) for entry in edge_entries(side, up)]
        for e, (up, f, dx, dy) in enumerate(lines):
            plane, row = 1 - dx if side < 0 else nx + 2 + dx, 23 - dy if up < 0 else 16 + dy
            ext[f, plane, pl.ds(row, 1), :] = r2[s, pl.ds(e, 1), :]
        small = jnp.concatenate([r2[s, pl.ds(EDGE_LINES, 16), :], pltpu.roll(r2[s, pl.ds(EDGE_LINES - 8, 8), :], 2, 0)], axis=0)
        for groups, shift, parts in x_units(side):
            near = 1 if side < 0 else nx + 2
            here = any_group(group, (near, near + side)[: len(groups)])
            v = lroll(small, 4 * near - 4 * groups[0] - shift)
            for f, low, high in parts:
                mini[f] = jnp.where(here & slot_mask(lane, 0, low, high), v, mini[f])
    ends = [z_ends(mini[up], mini[down]) for up, down in Z_PAIRS]
    for p in (0, 1, nx + 2, nx + 3):
        keep = [k for k, (f, _) in enumerate(Z_PAIRS) if DIRECTIONS[f][0] == (-1 if p < 2 else 1) or (p in (1, nx + 2) and DIRECTIONS[f][0] == 0)]
        for f, v in close_pairs(p, [Z_PAIRS[k] for k in keep], [ends[k] for k in keep], ext, pl.ds(0, ROWS)):
            ext[f, p] = v
    psi_ends[...], flux_ends[...] = mini_adjoint(mini)
    for p in (0, 1, nx + 2, nx + 3):
        potential(p, ext, psi_ends, psi, zs, zd, pl.ds(0, ROWS))

    def outer(low, k):
        return low + k + jnp.where(k >= 2, nx - 2, 0)

    planes(4, lambda k: outer(1, k), lambda p: collide(p, ext, psi, zs, zd, flux, out))
    planes(4, lambda k: outer(2, k) - jnp.where(k >= 2, 2, 0), lambda p: finish(p, psi, flux, flux_ends, out))
    for copy in copies[1:]:
        copy.start()
    for copy in copies:
        copy.wait()


def swap(low, high, axis):
    n = lax.axis_size(axis)
    up = [(i, (i + 1) % n) for i in range(n)]
    return lax.ppermute(low, axis, up), lax.ppermute(high, axis, [(j, i) for i, j in up])


def ppermute_pairs(msg, axis, first):
    n = lax.axis_size(axis)
    found = []
    for i in range(first, n + first, 2):
        found += [(i % n, (i + 1) % n), ((i + 1) % n, i % n)]
    return lax.ppermute(msg, axis, found)


def swap_both(msg, axis):
    n = lax.axis_size(axis)
    if n == 2:
        return lax.ppermute(msg, axis, [(0, 1), (1, 0)])
    return jnp.stack(swap(msg[0], msg[1], axis))


def per_device(populations, adjoint_next):
    nx = populations.shape[1]
    ext_shape, mini_shape, plane_shape = (FIELDS, nx + 4, ROWS, 128), (FIELDS, ROWS, 128), (nx + 4, ROWS, 128)
    small_y = (len(side_entries(1, 1)) + EDGE_LINES, 128)
    ext, mini, ya, yb = call(
        load_kernel,
        tuple(pltpu.with_memory_space_constraint(v, pltpu.HBM) for v in (populations, adjoint_next)),
        (ext_shape, mini_shape, small_y, small_y),
        scratch=[pltpu.VMEM((19, nx, 16, 128), F32), pltpu.SemaphoreType.DMA((10,))],
        in_specs=[HB, HB],
        name="load",
    )
    large_y = (24 * (nx - 2) + 8, 128)
    (yb,) = call(
        pair_kernel, (ext, yb), ((small_y[0] + large_y[0], 128),), name="pair", cost=COSTLY
    )
    (xmsg,) = call(x_kernel, (ext,), ((2, 24, 16, 128),), name="xpack", cost=COSTLY)
    x1 = swap_both(xmsg, "gx")
    ya, y2b = ppermute_pairs(ya, "gy", 1), ppermute_pairs(yb, "gy", 0)
    mini, za, zb, ya, yb = call(
        yz_kernel,
        (mini, ya, y2b),
        (mini_shape, (ROWS + 16, 128), (ROWS + 16, 128), small_y, small_y),
        aliases={0: 0},
        name="yz",
    )
    (y2a,) = call(y_kernel, (ext, mini), (large_y,), name="ypack", cost=COSTLY)
    y2a = ppermute_pairs(y2a, "gy", 1)
    za, zb = swap(za, zb, "gz")
    mini, xmsg2 = call(
        zx_kernel,
        (mini, za, zb, ya, yb),
        (mini_shape, (2, EDGE_LINES + 16, 128)),
        aliases={0: 0},
        name="zx",
    )
    tile, out_shape = (ROWS, 128), (19, nx + 2, 16, 128)
    ext, psi_ends, flux_ends, psi, zs, zd = call(
        turn_kernel,
        (ext, mini),
        (ext_shape, tile, tile, plane_shape, plane_shape, plane_shape),
        scratch=[pltpu.VMEM((len(Z_PAIRS), 16, 128), F32)],
        aliases={0: 0},
        name="turn",
    )
    x2 = swap_both(xmsg2, "gx")
    ext, psi, zs, zd, flux, part = call(
        mid_kernel,
        (ext, mini, ya, yb, y2a, y2b, psi_ends, flux_ends, psi, zs, zd),
        (ext_shape, plane_shape, plane_shape, plane_shape, (3, *plane_shape), out_shape),
        scratch=[pltpu.VMEM(v, F32) for v in ((len(Z_PAIRS), 8, 128), large_y, large_y)],
        aliases={0: 0, 8: 1, 9: 2, 10: 3},
        name="mid",
    )
    (ext,) = call(fill_kernel, (ext, x1), (ext_shape,), aliases={0: 0}, name="fill")
    return call(
        last_kernel,
        (ext, mini, x2, psi, zs, zd, flux, part),
        (ext_shape, mini_shape, plane_shape, plane_shape, plane_shape, (3, *plane_shape), out_shape, populations.shape),
        scratch=[pltpu.VMEM(tile, F32), pltpu.VMEM(tile, F32), pltpu.SemaphoreType.DMA((3,))],
        aliases={0: 0, 1: 1, 3: 2, 4: 3, 5: 4, 6: 5, 7: 6},
        out_specs=[VM] * 7 + [HB],
        name="last",
    )[-1]


def solution(mesh):
    return jax.shard_map(
        per_device,
        mesh=mesh,
        in_specs=(P(None, "gx", "gy", "gz"), P(None, "gx", "gy", "gz")),
        out_specs=P(None, "gx", "gy", "gz"),
        check_vma=False,
    )
```

```python
import jax
import jax.numpy as jnp
from jax import lax
from jax.experimental import pallas as pl
from jax.experimental.pallas import tpu as pltpu
from jax.sharding import PartitionSpec as P

DIRECTIONS = (
    (0, 0, 0),
    (1, 0, 0),
    (-1, 0, 0),
    (0, 1, 0),
    (0, -1, 0),
    (0, 0, 1),
    (0, 0, -1),
    (1, 1, 0),
    (-1, -1, 0),
    (1, -1, 0),
    (-1, 1, 0),
    (1, 0, 1),
    (-1, 0, -1),
    (1, 0, -1),
    (-1, 0, 1),
    (0, 1, 1),
    (0, -1, -1),
    (0, 1, -1),
    (0, -1, 1),
)
W0, W1, W2 = 1.0 / 3.0, 1.0 / 18.0, 1.0 / 36.0
RELAX_TIME = 0.8
COUPLING = -5.5
INV_TAU = 1.0 / RELAX_TIME
KAPPA = 1.0 - 0.5 / RELAX_TIME

RHO, MOM, FIELDS = 19, 20, 23
ROWS = 24
F32 = jnp.float32
COSTLY = pl.CostEstimate(flops=10**10, bytes_accessed=10**6, transcendentals=0)
VM = pl.BlockSpec(memory_space=pltpu.VMEM)
HB = pl.BlockSpec(memory_space=pltpu.HBM)


def deep_fields(dim, side):
    return [i for i in range(19) if DIRECTIONS[i][dim] == side] + [RHO]


def side_fields(dim, side):
    return deep_fields(dim, side) + [i for i in range(19) if DIRECTIONS[i][dim] == 0] + [MOM, MOM + 1, MOM + 2]


def side_entries(dim, side):
    return [(f, d) for d in (0, 1) for f in (side_fields(dim, side) if d == 0 else deep_fields(dim, side))]


def edge_entries(side, up):
    found = []
    for dx in (0, 1):
        for dy in (0, 1):
            across = deep_fields(0, side) if dx else side_fields(0, side)
            along = deep_fields(1, up) if dy else side_fields(1, up)
            found += [(f, dx, dy) for f in across if f in along]
    return sorted(found, key=lambda entry: z_part(entry[0]))


def z_pieces(side):
    deep = deep_fields(2, side)
    shallow = side_fields(2, side)[len(deep) :]
    found = [(f, u, 0) for u, f in enumerate(deep)]
    return found + [(f, len(deep) + k // 2, 1 + k % 2) for k, f in enumerate(shallow)]


def z_place(side, unit, kind):
    block, pair = unit % 8 // 2, unit % 2
    start = 32 * block + 2 * pair
    if side < 0:
        shift, slots = start - 8, {0: (0, 1), 1: (1,), 2: (0,)}[kind]
        shift -= kind == 2
    else:
        shift, slots = start - 10, {0: (0, 1), 1: (0,), 2: (1,)}[kind]
        shift += kind == 2
    return block, shift, [2 * pair + k for k in slots]


def x_units(side):
    found, group = [], 0
    deep = deep_fields(0, side)
    for depths, fields in ((2, deep), (1, side_fields(0, side)[len(deep) :])):
        up = [f for f in fields if z_part(f) > 0]
        down = [f for f in fields if z_part(f) < 0]
        flat = [f for f in fields if f != RHO and z_part(f) == 0]
        sets = [[(0, ((a, (2,), (2, 3)), (b, (0, 1), (1,))))] for a, b in zip(up, down)]
        for k in range(0, len(flat), 3):
            sets.append([(n - 1, ((f, (1,), (2,)),)) for n, f in enumerate(flat[k : k + 3])])
        if RHO in fields:
            sets.append([(0, ((RHO, (0, 1, 2), (1, 2, 3)),))])
        for units in sets:
            groups = (group,) if depths == 1 else (group + 1, group) if side < 0 else (group, group + 1)
            found += [(groups, shift, parts) for shift, parts in units]
            group += depths
    assert group <= 16
    return found


def any_group(group, groups):
    hit = group == groups[0]
    for g in groups[1:]:
        hit = hit | (group == g)
    return hit


def slot_mask(lane, shift, low, high):
    four = lane % 4
    inside = [None, None]
    for half, slots in enumerate((low, high)):
        for k in slots:
            hit = four == k + shift
            inside[half] = hit if inside[half] is None else inside[half] | hit
    return ((lane < 64) & inside[0]) | ((lane >= 64) & inside[1])


def z_part(f):
    return DIRECTIONS[f][2] if f < 19 else 0


CORNER = len(edge_entries(1, 1))
EDGE_LINES = -(-(2 * CORNER + 4) // 8) * 8


def by_parity(axis, v, w):
    odd = jnp.full(v.shape, lax.axis_index(axis) % 2, jnp.int32) == 1
    return jnp.where(odd, v, w), jnp.where(odd, w, v)


def lane_ids(rows):
    return lax.broadcasted_iota(jnp.int32, (rows, 128), 1)


def lroll(v, amount):
    amount = amount % 128
    return v if isinstance(amount, int) and amount == 0 else pltpu.roll(v, amount, 1)


def yroll(v, c):
    return v if c == 0 else pltpu.roll(v, (-c) % ROWS, 0)


def call(body, ins, outs, scratch=(), aliases=None, name=None, in_specs=None, out_specs=None, cost=None):
    return pl.pallas_call(
        body,
        in_specs=in_specs or [VM] * len(ins),
        out_specs=out_specs or [VM] * len(outs),
        out_shape=[jax.ShapeDtypeStruct(s, F32) for s in outs],
        scratch_shapes=list(scratch),
        input_output_aliases=aliases or {},
        name=name,
        cost_estimate=cost,
        compiler_params=pltpu.CompilerParams(vmem_limit_bytes=20 * 2**20),
    )(*ins)


def load_kernel(pop_hbm, adj_hbm, ext, mini, ya, yb, pops, sems):
    nx = pop_hbm.shape[1]
    lane = lane_ids(16)
    group = lane // 4
    chunks = [(f, min(4, 19 - f)) for f in range(0, 19, 4)]
    copies = []
    for k, (f, n) in enumerate(chunks):
        own = ext.at[pl.ds(f, n), pl.ds(2, nx), pl.ds(0, 16), :]
        copies.append(pltpu.make_async_copy(adj_hbm.at[pl.ds(f, n)], own, sems.at[k]))
    for k, (f, n) in enumerate(chunks):
        copies.append(pltpu.make_async_copy(pop_hbm.at[pl.ds(f, n)], pops.at[pl.ds(f, n)], sems.at[5 + k]))
    for c in copies:
        c.start()

    def edges(f):
        e = lroll(ext[f, 2, pl.ds(0, 16), :], 10)
        for x in range(1, nx):
            e = jnp.where(group == x + 2, lroll(ext[f, x + 2, pl.ds(0, 16), :], 4 * x + 10), e)
        mini[f, pl.ds(0, 16), :] = e

    for k, (f, n) in enumerate(chunks):
        copies[k].wait()
        for i in range(n):
            edges(f + i)
    for c in copies[5:]:
        c.wait()

    def moments(x, _):
        rho = pops[0, x]
        mom = [None] * 3
        for i in range(1, 19):
            p = pops[i, x]
            rho = rho + p
            for k in range(3):
                c = DIRECTIONS[i][k]
                if c:
                    mom[k] = (p if c > 0 else -p) if mom[k] is None else (mom[k] + p if c > 0 else mom[k] - p)
        ext[RHO, x + 2, pl.ds(0, 16), :] = rho
        for k in range(3):
            ext[MOM + k, x + 2, pl.ds(0, 16), :] = mom[k]
        return 0

    lax.fori_loop(0, nx, moments, 0, unroll=2)
    for f in range(RHO, FIELDS):
        edges(f)
    place = lax.broadcasted_iota(jnp.int32, (EDGE_LINES, 128), 0)
    for up, msg in ((-1, ya), (1, yb)):
        entries = side_entries(1, up)
        for e, (f, d) in enumerate(entries):
            msg[pl.ds(e, 1), :] = mini[f, pl.ds(15 - d if up < 0 else d, 1), :]
        lines = [(side, *entry) for side in (-1, 1) for entry in edge_entries(side, up)]
        for e, (side, f, dx, dy) in enumerate(lines):
            plane = nx + 1 - dx if side < 0 else 2 + dx
            msg[pl.ds(len(entries) + e, 1), :] = ext[f, plane, pl.ds(15 - dy if up < 0 else dy, 1), :]
        v = msg[pl.ds(len(entries), EDGE_LINES), :]
        turned = v
        for step in (-1, 1):
            here = None
            for k in (0, 1):
                hits = [e for e in range(CORNER) if z_part(lines[CORNER * k + e][1]) == step]
                hit = (place >= CORNER * k + hits[0]) & (place <= CORNER * k + hits[-1])
                here = hit if here is None else here | hit
            turned = jnp.where(here, lroll(v, -step), turned)
        msg[pl.ds(len(entries), EDGE_LINES), :] = turned
    ya[...], yb[...] = by_parity("gy", ya[...], yb[...])


def y_entries(side):
    found = []
    for f, d in side_entries(1, side):
        cx = DIRECTIONS[f][0] if f < 19 else 0
        found.append((f, d, 3 + cx))
    return sorted(found, key=lambda entry: z_part(entry[0]))


def y_lines(ext, low, high):
    for side, msg in ((-1, low), (1, high)):
        entries = y_entries(side)
        six = ext.shape[1] - 6
        msg[pl.ds(six * len(entries), 8), :] = jnp.zeros((8, 128), F32)
        for e, (f, d, first) in enumerate(entries):
            msg[pl.ds(six * e, six), :] = ext[f, pl.ds(first, six), 15 - d if side < 0 else d, :]
        for step in (-1, 1):
            hits = [e for e, (f, _, _) in enumerate(entries) if z_part(f) == step]
            start, stop = six * hits[0], six * (hits[-1] + 1)
            bottom, top = start // 8 * 8, -(-stop // 8) * 8
            v = msg[pl.ds(bottom, top - bottom), :]
            place = bottom + lax.broadcasted_iota(jnp.int32, v.shape, 0)
            msg[pl.ds(bottom, top - bottom), :] = jnp.where((place >= start) & (place < stop), lroll(v, -step), v)


def pair_kernel(ext, small, msg, low, high):
    y_lines(ext, low, high)
    msg[pl.ds(0, small.shape[0]), :] = small[...]
    msg[pl.ds(small.shape[0], low.shape[0]), :] = by_parity("gy", low[...], high[...])[1]


def x_kernel(ext, xmsg):
    nx = ext.shape[1] - 4
    for s, side in enumerate((-1, 1)):
        for e, (f, d) in enumerate(side_entries(0, side)):
            plane = (nx + 1 - d) if side < 0 else (2 + d)
            xmsg[s, e] = lroll(ext[f, plane, pl.ds(0, 16), :], -z_part(f))


def z_tiles(side, mini, rows):
    lane = lane_ids(rows.size)
    tiles = [None, None]
    for f, unit, kind in z_pieces(side):
        block, shift, slots = z_place(side, unit, kind)
        v = lroll(mini[f, rows, :], shift)
        here = lane % 4 == slots[0]
        for k in slots[1:]:
            here = here | (lane % 4 == k)
        t = unit // 8
        tiles[t] = v if tiles[t] is None else jnp.where((lane // 32 == block) & here, v, tiles[t])
    return tiles


def z_kernel(mini, za, zb):
    for side, msg in ((-1, za), (1, zb)):
        tiles = z_tiles(side, mini, pl.ds(0, 16))
        msg[pl.ds(0, 16), :] = tiles[0]
        msg[pl.ds(ROWS, 8), :] = jnp.where(lane_ids(8) < 64, tiles[1][:8], lroll(tiles[1][8:], 64))


def yz_kernel(mini_in, ra, rb, za_in, zb_in, mini, za, zb, low, high):
    low[...], high[...] = by_parity("gy", rb[pl.ds(0, low.shape[0]), :], ra[...])
    for side, msg in ((-1, low), (1, high)):
        entries = side_entries(1, side)
        for e, (f, d) in enumerate(entries):
            mini[f, pl.ds(23 - d if side < 0 else 16 + d, 1), :] = msg[pl.ds(e, 1), :]
    for side, msg in ((-1, za), (1, zb)):
        tiles = z_tiles(side, mini, pl.ds(16, 8))
        msg[pl.ds(16, 8), :] = tiles[0]
        msg[pl.ds(ROWS + 8, 8), :] = tiles[1]


def y_kernel(ext, mini, msg, low, high):
    y_lines(ext, low, high)
    msg[...] = by_parity("gy", low[...], high[...])[0]


Z_PAIRS = ((5, 6), (11, 13), (14, 12), (15, 17), (18, 16))


def z_ends(above, below):
    return jnp.where(lane_ids(above.shape[0]) % 4 == 0, lroll(above, 62), below)


def close_pairs(p, pairs, ends, ext, rows):
    lane = lane_ids(rows.size)
    found = []
    for (up, down), e in zip(pairs, ends):
        g = lroll(e, 255 - 4 * p)
        found.append((up, jnp.where(lane == 127, g, ext[up, p, rows, :])))
        found.append((down, jnp.where(lane == 0, g, ext[down, p, rows, :])))
    return found


def zx_kernel(mini_in, ra, rb, ya, yb, mini, xmsg):
    lane = lane_ids(ROWS)
    for f in range(FIELDS):
        e = mini_in[f]
        if f == RHO or z_part(f) < 0:
            e = jnp.where(lane < 64, e, lroll(e, 64))
        mini[f] = e
    for side, msg in ((-1, ra), (1, rb)):
        second = msg[pl.ds(ROWS, 8), :]
        tiles = (msg[pl.ds(0, ROWS), :], jnp.concatenate([second, lroll(second, 64), msg[pl.ds(ROWS + 8, 8), :]], axis=0))
        start, slots = (8, (0, 1)) if side < 0 else (72, (2, 3))
        near = slots[1] if side < 0 else slots[0]
        inside = (lane >= start) & (lane < start + 32)
        for f, unit, kind in z_pieces(side):
            shift = z_place(side, unit, kind)[1]
            keep = inside & ((lane % 4 // 2 == slots[0] // 2) if kind == 0 else (lane % 4 == near))
            v = lroll(tiles[unit // 8], -shift + (0 if side < 0 else 64))
            mini[f] = jnp.where(keep, v, mini[f])
    group = (lane % 64) // 4
    for s, side in enumerate((-1, 1)):
        acc = None
        for groups, shift, parts in x_units(side):
            v = mini[parts[0][0]]
            for f, low, high in parts[1:]:
                v = jnp.where(slot_mask(lane, 0, low, high), mini[f], v)
            v = lroll(v, 4 * groups[0] - 4 * (9 if side < 0 else 2) + shift)
            if acc is None:
                acc = v
            else:
                here = any_group(group, groups)
                if parts[0][1:] == ((1,), (2,)):
                    here = here & slot_mask(lane, shift, (1,), (2,))
                acc = jnp.where(here, v, acc)
        xmsg[s, pl.ds(EDGE_LINES - 8, 8), :] = pltpu.roll(acc[16:], 6, 0)
        xmsg[s, pl.ds(EDGE_LINES, 16), :] = acc[:16]
        for k, msg in enumerate((ya, yb)):
            start = len(side_entries(1, 1)) + CORNER * s
            xmsg[s, pl.ds(CORNER * k, CORNER), :] = msg[pl.ds(start, CORNER), :]


def turn_kernel(ext_in, mini, ext, psi_ends, flux_ends, psi, zs, zd, ends):
    nx = ext.shape[1] - 4
    lane = lane_ids(16)
    rows = pl.ds(0, 16)
    for k, (up, down) in enumerate(Z_PAIRS):
        ends[k] = z_ends(mini[up, rows, :], mini[down, rows, :])

    def turn(p, _):
        found = []
        for k, (up, down) in enumerate(Z_PAIRS):
            g = lroll(ends[k], 255 - 4 * p)
            found.append((up, jnp.where(lane == 127, g, lroll(ext_in[up, p, rows, :], 127))))
            found.append((down, jnp.where(lane == 0, g, lroll(ext_in[down, p, rows, :], 1))))
        for f, v in found:
            ext[f, p, rows, :] = v
        return 0

    lax.fori_loop(2, nx + 2, turn, 0, unroll=2)
    psi_ends[...], flux_ends[...] = mini_adjoint(mini)
    for p in range(2, nx + 2):
        potential(p, ext, psi_ends, psi, zs, zd, rows)


def cell(b, rho, mom, psi, g):
    pairs = {}
    for i in range(1, 19, 2):
        pairs[i] = (b[i] + b[i + 1], b[i] - b[i + 1])
    s = {i: v[0] for i, v in pairs.items()}
    d = {i: v[1] for i, v in pairs.items()}
    sxy, sxz, syz = s[7] + s[9], s[11] + s[13], s[15] + s[17]
    a0 = W0 * b[0] + W1 * (s[1] + s[3] + s[5]) + W2 * (sxy + sxz + syz)
    a1 = (
        (3 * W1) * d[1] + (3 * W2) * ((d[7] + d[9]) + (d[11] + d[13])),
        (3 * W1) * d[3] + (3 * W2) * ((d[7] - d[9]) + (d[15] + d[17])),
        (3 * W1) * d[5] + (3 * W2) * ((d[11] - d[13]) + (d[15] - d[17])),
    )
    a03 = 3.0 * a0
    bxx = (9 * W1) * s[1] + (9 * W2) * (sxy + sxz) - a03
    byy = (9 * W1) * s[3] + (9 * W2) * (sxy + syz) - a03
    bzz = (9 * W1) * s[5] + (9 * W2) * (sxz + syz) - a03
    bxy = (9 * W2) * (s[7] - s[9])
    bxz = (9 * W2) * (s[11] - s[13])
    byz = (9 * W2) * (s[15] - s[17])
    force = [(-COUPLING * psi) * gk for gk in g]
    inv = 1.0 / rho
    u = [(m + 0.5 * fk) * inv for m, fk in zip(mom, force)]

    def apply(v):
        return (
            bxx * v[0] + bxy * v[1] + bxz * v[2],
            bxy * v[0] + byy * v[1] + byz * v[2],
            bxz * v[0] + byz * v[1] + bzz * v[2],
        )

    w = [p + q for p, q in zip(a1, apply(u))]
    bf = [(KAPPA * inv) * q for q in apply(force)]
    force_bar = [p + 0.5 * q for p, q in zip(w, bf)]
    return a0, a1, u, w, bf, force_bar


def dot(p, q):
    return p[0] * q[0] + p[1] * q[1] + p[2] * q[2]


def mini_adjoint(mini):
    def msh(v, c):
        return lroll(yroll(v, c[1]), -4 * c[0] - c[2])

    psi = 1.0 - jnp.exp(-mini[RHO])
    ys = yroll(psi, 1) + yroll(psi, -1)
    zsum = lroll(psi, -1) + lroll(psi, 1)
    xsum = lroll(psi, -4) + lroll(psi, 4)
    qx = W1 * psi + W2 * (ys + zsum)
    qy = W1 * psi + W2 * (xsum + zsum)
    qz = W1 * psi + W2 * (xsum + ys)
    g = (lroll(qx, -4) - lroll(qx, 4), yroll(qy, 1) - yroll(qy, -1), lroll(qz, -1) - lroll(qz, 1))
    b = [msh(mini[i], DIRECTIONS[i]) for i in range(19)]
    force_bar = cell(b, mini[RHO], [mini[MOM + k] for k in range(3)], psi, g)[5]
    fx, fy, fz = (psi * v for v in force_bar)
    across = W2 * ((lroll(fx, -4) - lroll(fx, 4)) + (yroll(fy, 1) - yroll(fy, -1)))
    along = W1 * fz + W2 * ((lroll(fz, -4) + lroll(fz, 4)) + (yroll(fz, 1) + yroll(fz, -1)))
    return z_ends(psi, psi), z_ends(across + along, across - along)


def zpair(above, below, ends, plane):
    lane = lane_ids(above.shape[0])
    g = lroll(ends, 255 - 4 * plane)
    return jnp.where(lane == 127, g, lroll(above, 127)), jnp.where(lane == 0, g, lroll(below, 1))


def potential(p, ext, ends, psi, zs, zd, rows):
    v = 1.0 - jnp.exp(-ext[RHO, p, rows, :])
    psi[p, rows, :] = v
    a, b = zpair(v, v, ends[rows, :], p)
    zs[p, rows, :] = a + b
    zd[p, rows, :] = a - b


def collide(p, ext, psi, zs, zd, flux, out):
    v, xp, xm = psi[p], psi[p + 1], psi[p - 1]
    qxp = W1 * xp + W2 * (yroll(xp, 1) + yroll(xp, -1) + zs[p + 1])
    qxm = W1 * xm + W2 * (yroll(xm, 1) + yroll(xm, -1) + zs[p - 1])
    qy = W1 * v + W2 * (xp + xm + zs[p])
    zz = zd[p]
    g = (
        qxp - qxm,
        yroll(qy, 1) - yroll(qy, -1),
        W1 * zz + W2 * (zd[p + 1] + zd[p - 1] + yroll(zz, 1) + yroll(zz, -1)),
    )
    b = [yroll(ext[i, p + DIRECTIONS[i][0]], DIRECTIONS[i][1]) for i in range(19)]
    a0, a1, u, w, bf, fb = cell(b, ext[RHO, p], [ext[MOM + k, p] for k in range(3)], v, g)
    for k in range(3):
        flux[k, p] = v * fb[k]

    def top(a):
        return a[:16]

    vv = [top(INV_TAU * wk + bk) for wk, bk in zip(w, bf)]
    uu = [top(a) for a in u]
    base = INV_TAU * (top(a0) + 0.5 * dot([top(r + q) for r, q in zip(a1, w)], uu)) - dot(vv, uu)
    base = base + (-COUPLING * (1.0 - top(v))) * top(dot(fb, g))
    for i in range(19):
        o = (1.0 - INV_TAU) * top(b[i]) + base
        for k in range(3):
            if DIRECTIONS[i][k] > 0:
                o = o + vv[k]
            elif DIRECTIONS[i][k] < 0:
                o = o - vv[k]
        out[i, p - 1] = o


def finish(p, psi, flux, ends, out):
    fx, fxm, fy = flux[0, p + 1], flux[0, p - 1], flux[1, p]
    fz = flux[2, p]
    xd = fx - fxm
    fyx = flux[1, p + 1] + flux[1, p - 1]
    dx = xd[:16]
    dy = (yroll(fy, 1) - yroll(fy, -1))[:16]
    here = W1 * (dx + dy) + W2 * (
        (yroll(xd, 1) + yroll(xd, -1))[:16] + (yroll(fyx, 1) - yroll(fyx, -1))[:16]
    )
    across = W2 * (dx + dy)
    along = W1 * fz[:16] + W2 * (flux[2, p + 1, pl.ds(0, 16), :] + flux[2, p - 1, pl.ds(0, 16), :] + (yroll(fz, 1) + yroll(fz, -1))[:16])
    a, b = zpair(across + along, across - along, ends[pl.ds(0, 16), :], p)
    term = (COUPLING * (1.0 - psi[p, pl.ds(0, 16), :])) * (here + (a + b))
    for i in range(19):
        out[i, p - 1] = out[i, p - 1] + term


def planes(count, of, step, unroll=4):
    def body(k, _):
        step(of(k))
        return 0

    lax.fori_loop(0, count, body, 0, unroll=unroll)


def send_planes(out, out_hbm, sem, first, count):
    return pltpu.make_async_copy(out.at[:, pl.ds(first - 1, count)], out_hbm.at[:, pl.ds(first - 2, count)], sem)


def mid_kernel(ext_in, mini, sa, sb, r2, rb, psi_ends, flux_ends, psi_in, zs_in, zd_in, ext, psi, zs, zd, flux, out, ends, low, high):
    nx = ext.shape[1] - 4
    rows = pl.ds(16, 8)
    low[...], high[...] = by_parity("gy", rb[pl.ds(sa.shape[0], low.shape[0]), :], r2[...])
    for up, small, large in ((-1, sa, low), (1, sb, high)):
        for e, (f, d, first) in enumerate(y_entries(up)):
            ext[f, pl.ds(first, nx - 2), 23 - d if up < 0 else 16 + d, :] = large[pl.ds((nx - 2) * e, nx - 2), :]
        lines = [(side, *entry) for side in (-1, 1) for entry in edge_entries(side, up)]
        for e, (side, f, dx, dy) in enumerate(lines):
            plane, row = nx + 1 - dx if side < 0 else 2 + dx, 23 - dy if up < 0 else 16 + dy
            ext[f, plane, pl.ds(row, 1), :] = small[pl.ds(len(side_entries(1, up)) + e, 1), :]
    for k, (up, down) in enumerate(Z_PAIRS):
        ends[k] = z_ends(mini[up, rows, :], mini[down, rows, :])

    def close(p, _):
        for f, v in close_pairs(p, Z_PAIRS, [ends[k] for k in range(len(Z_PAIRS))], ext, rows):
            ext[f, p, rows, :] = v
        return 0

    lax.fori_loop(2, nx + 2, close, 0, unroll=4)
    for p in range(2, nx + 2):
        potential(p, ext, psi_ends, psi, zs, zd, rows)
    planes(nx - 2, lambda k: k + 3, lambda p: collide(p, ext, psi, zs, zd, flux, out))

    planes(nx - 4, lambda k: k + 4, lambda p: finish(p, psi, flux, flux_ends, out))


def fill_kernel(ext_in, r1, ext):
    nx = ext.shape[1] - 4
    for s, side in enumerate((-1, 1)):
        for e, (f, d) in enumerate(side_entries(0, side)):
            ext[f, 1 - d if side < 0 else nx + 2 + d, pl.ds(0, 16), :] = r1[s, e]


def last_kernel(ext_in, mini_in, r2, psi_in, zs_in, zd_in, flux_in, out_in, ext, mini, psi, zs, zd, flux, out, out_hbm, psi_ends, flux_ends, sems):
    nx = ext.shape[1] - 4
    copies = [
        send_planes(out, out_hbm, sems.at[k], first, count) for k, (first, count) in enumerate(((4, nx - 4), (2, 2), (nx, 2)))
    ]
    copies[0].start()
    lane = lane_ids(ROWS)
    group = (lane % 64) // 4
    for s, side in enumerate((-1, 1)):
        lines = [(up, *entry) for up in (-1, 1) for entry in edge_entries(side, up)]
        for e, (up, f, dx, dy) in enumerate(lines):
            plane, row = 1 - dx if side < 0 else nx + 2 + dx, 23 - dy if up < 0 else 16 + dy
            ext[f, plane, pl.ds(row, 1), :] = r2[s, pl.ds(e, 1), :]
        small = jnp.concatenate([r2[s, pl.ds(EDGE_LINES, 16), :], pltpu.roll(r2[s, pl.ds(EDGE_LINES - 8, 8), :], 2, 0)], axis=0)
        for groups, shift, parts in x_units(side):
            near = 1 if side < 0 else nx + 2
            here = any_group(group, (near, near + side)[: len(groups)])
            v = lroll(small, 4 * near - 4 * groups[0] - shift)
            for f, low, high in parts:
                mini[f] = jnp.where(here & slot_mask(lane, 0, low, high), v, mini[f])
    ends = [z_ends(mini[up], mini[down]) for up, down in Z_PAIRS]
    for p in (0, 1, nx + 2, nx + 3):
        keep = [k for k, (f, _) in enumerate(Z_PAIRS) if DIRECTIONS[f][0] == (-1 if p < 2 else 1) or (p in (1, nx + 2) and DIRECTIONS[f][0] == 0)]
        for f, v in close_pairs(p, [Z_PAIRS[k] for k in keep], [ends[k] for k in keep], ext, pl.ds(0, ROWS)):
            ext[f, p] = v
    psi_ends[...], flux_ends[...] = mini_adjoint(mini)
    for p in (0, 1, nx + 2, nx + 3):
        potential(p, ext, psi_ends, psi, zs, zd, pl.ds(0, ROWS))

    def outer(low, k):
        return low + k + jnp.where(k >= 2, nx - 2, 0)

    planes(4, lambda k: outer(1, k), lambda p: collide(p, ext, psi, zs, zd, flux, out))
    planes(4, lambda k: outer(2, k) - jnp.where(k >= 2, 2, 0), lambda p: finish(p, psi, flux, flux_ends, out))
    for copy in copies[1:]:
        copy.start()
    for copy in copies:
        copy.wait()


def swap(low, high, axis):
    n = lax.axis_size(axis)
    up = [(i, (i + 1) % n) for i in range(n)]
    return lax.ppermute(low, axis, up), lax.ppermute(high, axis, [(j, i) for i, j in up])


def ppermute_pairs(msg, axis, first):
    n = lax.axis_size(axis)
    found = []
    for i in range(first, n + first, 2):
        found += [(i % n, (i + 1) % n), ((i + 1) % n, i % n)]
    return lax.ppermute(msg, axis, found)


def swap_both(msg, axis):
    n = lax.axis_size(axis)
    if n == 2:
        return lax.ppermute(msg, axis, [(0, 1), (1, 0)])
    return jnp.stack(swap(msg[0], msg[1], axis))


def per_device(populations, adjoint_next):
    nx = populations.shape[1]
    ext_shape, mini_shape, plane_shape = (FIELDS, nx + 4, ROWS, 128), (FIELDS, ROWS, 128), (nx + 4, ROWS, 128)
    small_y = (len(side_entries(1, 1)) + EDGE_LINES, 128)
    ext, mini, ya, yb = call(
        load_kernel,
        tuple(pltpu.with_memory_space_constraint(v, pltpu.HBM) for v in (populations, adjoint_next)),
        (ext_shape, mini_shape, small_y, small_y),
        scratch=[pltpu.VMEM((19, nx, 16, 128), F32), pltpu.SemaphoreType.DMA((10,))],
        in_specs=[HB, HB],
        name="load",
    )
    large_y = (24 * (nx - 2) + 8, 128)
    two_large = [pltpu.VMEM(large_y, F32), pltpu.VMEM(large_y, F32)]
    (yb,) = call(
        pair_kernel, (ext, yb), ((small_y[0] + large_y[0], 128),), scratch=two_large, name="pair", cost=COSTLY
    )
    (xmsg,) = call(x_kernel, (ext,), ((2, 24, 16, 128),), name="xpack", cost=COSTLY)
    x1 = swap_both(xmsg, "gx")
    ya, y2b = ppermute_pairs(ya, "gy", 1), ppermute_pairs(yb, "gy", 0)
    za, zb = call(z_kernel, (mini,), ((ROWS + 16, 128), (ROWS + 16, 128)), name="zpack", cost=COSTLY)
    mini, za, zb, ya, yb = call(
        yz_kernel,
        (mini, ya, y2b, za, zb),
        (mini_shape, (ROWS + 16, 128), (ROWS + 16, 128), small_y, small_y),
        aliases={0: 0, 3: 1, 4: 2},
        name="yz",
    )
    (y2a,) = call(y_kernel, (ext, mini), (large_y,), scratch=two_large, name="ypack", cost=COSTLY)
    y2a = ppermute_pairs(y2a, "gy", 1)
    za, zb = swap(za, zb, "gz")
    mini, xmsg2 = call(
        zx_kernel,
        (mini, za, zb, ya, yb),
        (mini_shape, (2, EDGE_LINES + 16, 128)),
        aliases={0: 0},
        name="zx",
    )
    tile, out_shape = (ROWS, 128), (19, nx + 2, 16, 128)
    ext, psi_ends, flux_ends, psi, zs, zd = call(
        turn_kernel,
        (ext, mini),
        (ext_shape, tile, tile, plane_shape, plane_shape, plane_shape),
        scratch=[pltpu.VMEM((len(Z_PAIRS), 16, 128), F32)],
        aliases={0: 0},
        name="turn",
    )
    x2 = swap_both(xmsg2, "gx")
    ext, psi, zs, zd, flux, part = call(
        mid_kernel,
        (ext, mini, ya, yb, y2a, y2b, psi_ends, flux_ends, psi, zs, zd),
        (ext_shape, plane_shape, plane_shape, plane_shape, (3, *plane_shape), out_shape),
        scratch=[pltpu.VMEM(v, F32) for v in ((len(Z_PAIRS), 8, 128), large_y, large_y)],
        aliases={0: 0, 8: 1, 9: 2, 10: 3},
        name="mid",
    )
    (ext,) = call(fill_kernel, (ext, x1), (ext_shape,), aliases={0: 0}, name="fill")
    return call(
        last_kernel,
        (ext, mini, x2, psi, zs, zd, flux, part),
        (ext_shape, mini_shape, plane_shape, plane_shape, plane_shape, (3, *plane_shape), out_shape, populations.shape),
        scratch=[pltpu.VMEM(tile, F32), pltpu.VMEM(tile, F32), pltpu.SemaphoreType.DMA((3,))],
        aliases={0: 0, 1: 1, 3: 2, 4: 3, 5: 4, 6: 5, 7: 6},
        out_specs=[VM] * 7 + [HB],
        name="last",
    )[-1]


def solution(mesh):
    return jax.shard_map(
        per_device,
        mesh=mesh,
        in_specs=(P(None, "gx", "gy", "gz"), P(None, "gx", "gy", "gz")),
        out_specs=P(None, "gx", "gy", "gz"),
        check_vma=False,
    )
```

```python
import jax
import jax.numpy as jnp
from jax import lax
from jax.experimental import pallas as pl
from jax.experimental.pallas import tpu as pltpu
from jax.sharding import PartitionSpec as P

DIRECTIONS = (
    (0, 0, 0),
    (1, 0, 0),
    (-1, 0, 0),
    (0, 1, 0),
    (0, -1, 0),
    (0, 0, 1),
    (0, 0, -1),
    (1, 1, 0),
    (-1, -1, 0),
    (1, -1, 0),
    (-1, 1, 0),
    (1, 0, 1),
    (-1, 0, -1),
    (1, 0, -1),
    (-1, 0, 1),
    (0, 1, 1),
    (0, -1, -1),
    (0, 1, -1),
    (0, -1, 1),
)
W0, W1, W2 = 1.0 / 3.0, 1.0 / 18.0, 1.0 / 36.0
RELAX_TIME = 0.8
COUPLING = -5.5
INV_TAU = 1.0 / RELAX_TIME
KAPPA = 1.0 - 0.5 / RELAX_TIME

RHO, MOM, FIELDS = 19, 20, 23
ROWS = 24
F32 = jnp.float32
COSTLY = pl.CostEstimate(flops=10**10, bytes_accessed=10**6, transcendentals=0)
VM = pl.BlockSpec(memory_space=pltpu.VMEM)
HB = pl.BlockSpec(memory_space=pltpu.HBM)


def deep_fields(dim, side):
    return [i for i in range(19) if DIRECTIONS[i][dim] == side] + [RHO]


def side_fields(dim, side):
    return deep_fields(dim, side) + [i for i in range(19) if DIRECTIONS[i][dim] == 0] + [MOM, MOM + 1, MOM + 2]


def side_entries(dim, side):
    return [(f, d) for d in (0, 1) for f in (side_fields(dim, side) if d == 0 else deep_fields(dim, side))]


def edge_entries(side, up):
    found = []
    for dx in (0, 1):
        for dy in (0, 1):
            across = deep_fields(0, side) if dx else side_fields(0, side)
            along = deep_fields(1, up) if dy else side_fields(1, up)
            found += [(f, dx, dy) for f in across if f in along]
    return sorted(found, key=lambda entry: z_part(entry[0]))


def z_pieces(side):
    deep = deep_fields(2, side)
    shallow = side_fields(2, side)[len(deep) :]
    found = [(f, u, 0) for u, f in enumerate(deep)]
    return found + [(f, len(deep) + k // 2, 1 + k % 2) for k, f in enumerate(shallow)]


def z_place(side, unit, kind):
    block, pair = unit % 8 // 2, unit % 2
    start = 32 * block + 2 * pair
    if side < 0:
        shift, slots = start - 8, {0: (0, 1), 1: (1,), 2: (0,)}[kind]
        shift -= kind == 2
    else:
        shift, slots = start - 10, {0: (0, 1), 1: (0,), 2: (1,)}[kind]
        shift += kind == 2
    return block, shift, [2 * pair + k for k in slots]


def x_units(side):
    found, group = [], 0
    deep = deep_fields(0, side)
    for depths, fields in ((2, deep), (1, side_fields(0, side)[len(deep) :])):
        up = [f for f in fields if z_part(f) > 0]
        down = [f for f in fields if z_part(f) < 0]
        flat = [f for f in fields if f != RHO and z_part(f) == 0]
        sets = [[(0, ((a, (2,), (2, 3)), (b, (0, 1), (1,))))] for a, b in zip(up, down)]
        for k in range(0, len(flat), 3):
            sets.append([(n - 1, ((f, (1,), (2,)),)) for n, f in enumerate(flat[k : k + 3])])
        if RHO in fields:
            sets.append([(0, ((RHO, (0, 1, 2), (1, 2, 3)),))])
        for units in sets:
            groups = (group,) if depths == 1 else (group + 1, group) if side < 0 else (group, group + 1)
            found += [(groups, shift, parts) for shift, parts in units]
            group += depths
    assert group <= 16
    return found


def any_group(group, groups):
    hit = group == groups[0]
    for g in groups[1:]:
        hit = hit | (group == g)
    return hit


def slot_mask(lane, shift, low, high):
    four = lane % 4
    inside = [None, None]
    for half, slots in enumerate((low, high)):
        for k in slots:
            hit = four == k + shift
            inside[half] = hit if inside[half] is None else inside[half] | hit
    return ((lane < 64) & inside[0]) | ((lane >= 64) & inside[1])


def z_part(f):
    return DIRECTIONS[f][2] if f < 19 else 0


CORNER = len(edge_entries(1, 1))
EDGE_LINES = -(-(2 * CORNER + 4) // 8) * 8


def by_parity(axis, v, w):
    odd = jnp.full(v.shape, lax.axis_index(axis) % 2, jnp.int32) == 1
    return jnp.where(odd, v, w), jnp.where(odd, w, v)


def lane_ids(rows):
    return lax.broadcasted_iota(jnp.int32, (rows, 128), 1)


def lroll(v, amount):
    amount = amount % 128
    return v if isinstance(amount, int) and amount == 0 else pltpu.roll(v, amount, 1)


def yroll(v, c):
    return v if c == 0 else pltpu.roll(v, (-c) % ROWS, 0)


def call(body, ins, outs, scratch=(), aliases=None, name=None, in_specs=None, out_specs=None, cost=None):
    return pl.pallas_call(
        body,
        in_specs=in_specs or [VM] * len(ins),
        out_specs=out_specs or [VM] * len(outs),
        out_shape=[jax.ShapeDtypeStruct(s, F32) for s in outs],
        scratch_shapes=list(scratch),
        input_output_aliases=aliases or {},
        name=name,
        cost_estimate=cost,
        compiler_params=pltpu.CompilerParams(vmem_limit_bytes=20 * 2**20),
    )(*ins)


def load_kernel(pop_hbm, adj_hbm, ext, mini, ya, yb, pops, sems):
    nx = pop_hbm.shape[1]
    lane = lane_ids(16)
    group = lane // 4
    chunks = [(f, min(4, 19 - f)) for f in range(0, 19, 4)]
    copies = []
    for k, (f, n) in enumerate(chunks):
        own = ext.at[pl.ds(f, n), pl.ds(2, nx), pl.ds(0, 16), :]
        copies.append(pltpu.make_async_copy(adj_hbm.at[pl.ds(f, n)], own, sems.at[k]))
    for k, (f, n) in enumerate(chunks):
        copies.append(pltpu.make_async_copy(pop_hbm.at[pl.ds(f, n)], pops.at[pl.ds(f, n)], sems.at[5 + k]))
    for c in copies:
        c.start()

    def edges(f):
        e = lroll(ext[f, 2, pl.ds(0, 16), :], 10)
        for x in range(1, nx):
            e = jnp.where(group == x + 2, lroll(ext[f, x + 2, pl.ds(0, 16), :], 4 * x + 10), e)
        mini[f, pl.ds(0, 16), :] = e

    for k, (f, n) in enumerate(chunks):
        copies[k].wait()
        for i in range(n):
            edges(f + i)

    def y_edges(wanted):
        for up, msg in ((-1, ya), (1, yb)):
            entries = side_entries(1, up)
            for e, (f, d) in enumerate(entries):
                if wanted(f):
                    msg[pl.ds(e, 1), :] = mini[f, pl.ds(15 - d if up < 0 else d, 1), :]
            lines = [(side, *entry) for side in (-1, 1) for entry in edge_entries(side, up)]
            for e, (side, f, dx, dy) in enumerate(lines):
                plane = nx + 1 - dx if side < 0 else 2 + dx
                if wanted(f):
                    msg[pl.ds(len(entries) + e, 1), :] = ext[f, plane, pl.ds(15 - dy if up < 0 else dy, 1), :]

    y_edges(lambda f: f < RHO)
    place = lax.broadcasted_iota(jnp.int32, (EDGE_LINES, 128), 0)
    for up, msg in ((-1, ya), (1, yb)):
        entries = side_entries(1, up)
        lines = [(side, *entry) for side in (-1, 1) for entry in edge_entries(side, up)]
        v = msg[pl.ds(len(entries), EDGE_LINES), :]
        turned = v
        for step in (-1, 1):
            here = None
            for k in (0, 1):
                hits = [e for e in range(CORNER) if z_part(lines[CORNER * k + e][1]) == step]
                hit = (place >= CORNER * k + hits[0]) & (place <= CORNER * k + hits[-1])
                here = hit if here is None else here | hit
            turned = jnp.where(here, lroll(v, -step), turned)
        msg[pl.ds(len(entries), EDGE_LINES), :] = turned
    for c in copies[5:]:
        c.wait()

    def moments(x, _):
        rho = pops[0, x]
        mom = [None] * 3
        for i in range(1, 19):
            p = pops[i, x]
            rho = rho + p
            for k in range(3):
                c = DIRECTIONS[i][k]
                if c:
                    mom[k] = (p if c > 0 else -p) if mom[k] is None else (mom[k] + p if c > 0 else mom[k] - p)
        ext[RHO, x + 2, pl.ds(0, 16), :] = rho
        for k in range(3):
            ext[MOM + k, x + 2, pl.ds(0, 16), :] = mom[k]
        return 0

    lax.fori_loop(0, nx, moments, 0, unroll=2)
    for f in range(RHO, FIELDS):
        edges(f)
    y_edges(lambda f: f >= RHO)
    ya[...], yb[...] = by_parity("gy", ya[...], yb[...])


def y_entries(side):
    found = []
    for f, d in side_entries(1, side):
        cx = DIRECTIONS[f][0] if f < 19 else 0
        found.append((f, d, 3 + cx))
    return sorted(found, key=lambda entry: z_part(entry[0]))


def y_lines(ext, low, high):
    for side, msg in ((-1, low), (1, high)):
        entries = y_entries(side)
        six = ext.shape[1] - 6
        msg[pl.ds(six * len(entries), 8), :] = jnp.zeros((8, 128), F32)
        for e, (f, d, first) in enumerate(entries):
            msg[pl.ds(six * e, six), :] = ext[f, pl.ds(first, six), 15 - d if side < 0 else d, :]
        for step in (-1, 1):
            hits = [e for e, (f, _, _) in enumerate(entries) if z_part(f) == step]
            start, stop = six * hits[0], six * (hits[-1] + 1)
            bottom, top = start // 8 * 8, -(-stop // 8) * 8
            v = msg[pl.ds(bottom, top - bottom), :]
            place = bottom + lax.broadcasted_iota(jnp.int32, v.shape, 0)
            msg[pl.ds(bottom, top - bottom), :] = jnp.where((place >= start) & (place < stop), lroll(v, -step), v)


def pair_kernel(ext, small, msg, low, high):
    y_lines(ext, low, high)
    msg[pl.ds(0, small.shape[0]), :] = small[...]
    msg[pl.ds(small.shape[0], low.shape[0]), :] = by_parity("gy", low[...], high[...])[1]


def x_kernel(ext, xmsg):
    nx = ext.shape[1] - 4
    for s, side in enumerate((-1, 1)):
        for e, (f, d) in enumerate(side_entries(0, side)):
            plane = (nx + 1 - d) if side < 0 else (2 + d)
            xmsg[s, e] = lroll(ext[f, plane, pl.ds(0, 16), :], -z_part(f))


def yz_kernel(mini_in, ra, rb, mini, za, zb, low, high):
    lane = lane_ids(ROWS)
    low[...], high[...] = by_parity("gy", rb[pl.ds(0, low.shape[0]), :], ra[...])
    for side, msg in ((-1, low), (1, high)):
        entries = side_entries(1, side)
        for e, (f, d) in enumerate(entries):
            mini[f, pl.ds(23 - d if side < 0 else 16 + d, 1), :] = msg[pl.ds(e, 1), :]
    for side, msg in ((-1, za), (1, zb)):
        tiles = [None, None]
        for f, unit, kind in z_pieces(side):
            block, shift, slots = z_place(side, unit, kind)
            v = lroll(mini[f], shift)
            here = lane % 4 == slots[0]
            for k in slots[1:]:
                here = here | (lane % 4 == k)
            t = unit // 8
            tiles[t] = v if tiles[t] is None else jnp.where((lane // 32 == block) & here, v, tiles[t])
        msg[pl.ds(0, ROWS), :] = tiles[0]
        msg[pl.ds(ROWS, 8), :] = jnp.where(lane[:8] < 64, tiles[1][:8], lroll(tiles[1][8:16], 64))
        msg[pl.ds(ROWS + 8, 8), :] = tiles[1][16:]


def y_kernel(ext, mini, msg, low, high):
    y_lines(ext, low, high)
    msg[...] = by_parity("gy", low[...], high[...])[0]


Z_PAIRS = ((5, 6), (11, 13), (14, 12), (15, 17), (18, 16))


def z_ends(above, below):
    return jnp.where(lane_ids(above.shape[0]) % 4 == 0, lroll(above, 62), below)


def close_pairs(p, pairs, ends, ext, rows):
    lane = lane_ids(rows.size)
    found = []
    for (up, down), e in zip(pairs, ends):
        g = lroll(e, 255 - 4 * p)
        found.append((up, jnp.where(lane == 127, g, ext[up, p, rows, :])))
        found.append((down, jnp.where(lane == 0, g, ext[down, p, rows, :])))
    return found


def zx_kernel(mini_in, ra, rb, ya, yb, mini, xmsg):
    lane = lane_ids(ROWS)
    for f in range(FIELDS):
        e = mini_in[f]
        if f == RHO or z_part(f) < 0:
            e = jnp.where(lane < 64, e, lroll(e, 64))
        mini[f] = e
    for side, msg in ((-1, ra), (1, rb)):
        second = msg[pl.ds(ROWS, 8), :]
        tiles = (msg[pl.ds(0, ROWS), :], jnp.concatenate([second, lroll(second, 64), msg[pl.ds(ROWS + 8, 8), :]], axis=0))
        start, slots = (8, (0, 1)) if side < 0 else (72, (2, 3))
        near = slots[1] if side < 0 else slots[0]
        inside = (lane >= start) & (lane < start + 32)
        for f, unit, kind in z_pieces(side):
            shift = z_place(side, unit, kind)[1]
            keep = inside & ((lane % 4 // 2 == slots[0] // 2) if kind == 0 else (lane % 4 == near))
            v = lroll(tiles[unit // 8], -shift + (0 if side < 0 else 64))
            mini[f] = jnp.where(keep, v, mini[f])
    group = (lane % 64) // 4
    for s, side in enumerate((-1, 1)):
        acc = None
        for groups, shift, parts in x_units(side):
            v = mini[parts[0][0]]
            for f, low, high in parts[1:]:
                v = jnp.where(slot_mask(lane, 0, low, high), mini[f], v)
            v = lroll(v, 4 * groups[0] - 4 * (9 if side < 0 else 2) + shift)
            if acc is None:
                acc = v
            else:
                here = any_group(group, groups)
                if parts[0][1:] == ((1,), (2,)):
                    here = here & slot_mask(lane, shift, (1,), (2,))
                acc = jnp.where(here, v, acc)
        xmsg[s, pl.ds(EDGE_LINES - 8, 8), :] = pltpu.roll(acc[16:], 6, 0)
        xmsg[s, pl.ds(EDGE_LINES, 16), :] = acc[:16]
        for k, msg in enumerate((ya, yb)):
            start = len(side_entries(1, 1)) + CORNER * s
            xmsg[s, pl.ds(CORNER * k, CORNER), :] = msg[pl.ds(start, CORNER), :]


def turn_kernel(ext_in, mini, ext, psi_ends, flux_ends, psi, zs, zd, ends):
    nx = ext.shape[1] - 4
    lane = lane_ids(16)
    rows = pl.ds(0, 16)
    for k, (up, down) in enumerate(Z_PAIRS):
        ends[k] = z_ends(mini[up, rows, :], mini[down, rows, :])

    def turn(p, _):
        found = []
        for k, (up, down) in enumerate(Z_PAIRS):
            g = lroll(ends[k], 255 - 4 * p)
            found.append((up, jnp.where(lane == 127, g, lroll(ext_in[up, p, rows, :], 127))))
            found.append((down, jnp.where(lane == 0, g, lroll(ext_in[down, p, rows, :], 1))))
        for f, v in found:
            ext[f, p, rows, :] = v
        return 0

    lax.fori_loop(2, nx + 2, turn, 0, unroll=2)
    psi_ends[...], flux_ends[...] = mini_adjoint(mini)
    for p in range(2, nx + 2):
        potential(p, ext, psi_ends, psi, zs, zd, rows)


def cell(b, rho, mom, psi, g):
    pairs = {}
    for i in range(1, 19, 2):
        pairs[i] = (b[i] + b[i + 1], b[i] - b[i + 1])
    s = {i: v[0] for i, v in pairs.items()}
    d = {i: v[1] for i, v in pairs.items()}
    sxy, sxz, syz = s[7] + s[9], s[11] + s[13], s[15] + s[17]
    a0 = W0 * b[0] + W1 * (s[1] + s[3] + s[5]) + W2 * (sxy + sxz + syz)
    a1 = (
        (3 * W1) * d[1] + (3 * W2) * ((d[7] + d[9]) + (d[11] + d[13])),
        (3 * W1) * d[3] + (3 * W2) * ((d[7] - d[9]) + (d[15] + d[17])),
        (3 * W1) * d[5] + (3 * W2) * ((d[11] - d[13]) + (d[15] - d[17])),
    )
    a03 = 3.0 * a0
    bxx = (9 * W1) * s[1] + (9 * W2) * (sxy + sxz) - a03
    byy = (9 * W1) * s[3] + (9 * W2) * (sxy + syz) - a03
    bzz = (9 * W1) * s[5] + (9 * W2) * (sxz + syz) - a03
    bxy = (9 * W2) * (s[7] - s[9])
    bxz = (9 * W2) * (s[11] - s[13])
    byz = (9 * W2) * (s[15] - s[17])
    force = [(-COUPLING * psi) * gk for gk in g]
    inv = 1.0 / rho
    u = [(m + 0.5 * fk) * inv for m, fk in zip(mom, force)]

    def apply(v):
        return (
            bxx * v[0] + bxy * v[1] + bxz * v[2],
            bxy * v[0] + byy * v[1] + byz * v[2],
            bxz * v[0] + byz * v[1] + bzz * v[2],
        )

    w = [p + q for p, q in zip(a1, apply(u))]
    bf = [(KAPPA * inv) * q for q in apply(force)]
    force_bar = [p + 0.5 * q for p, q in zip(w, bf)]
    return a0, a1, u, w, bf, force_bar


def dot(p, q):
    return p[0] * q[0] + p[1] * q[1] + p[2] * q[2]


def mini_adjoint(mini):
    def msh(v, c):
        return lroll(yroll(v, c[1]), -4 * c[0] - c[2])

    psi = 1.0 - jnp.exp(-mini[RHO])
    ys = yroll(psi, 1) + yroll(psi, -1)
    zsum = lroll(psi, -1) + lroll(psi, 1)
    xsum = lroll(psi, -4) + lroll(psi, 4)
    qx = W1 * psi + W2 * (ys + zsum)
    qy = W1 * psi + W2 * (xsum + zsum)
    qz = W1 * psi + W2 * (xsum + ys)
    g = (lroll(qx, -4) - lroll(qx, 4), yroll(qy, 1) - yroll(qy, -1), lroll(qz, -1) - lroll(qz, 1))
    b = [msh(mini[i], DIRECTIONS[i]) for i in range(19)]
    force_bar = cell(b, mini[RHO], [mini[MOM + k] for k in range(3)], psi, g)[5]
    fx, fy, fz = (psi * v for v in force_bar)
    across = W2 * ((lroll(fx, -4) - lroll(fx, 4)) + (yroll(fy, 1) - yroll(fy, -1)))
    along = W1 * fz + W2 * ((lroll(fz, -4) + lroll(fz, 4)) + (yroll(fz, 1) + yroll(fz, -1)))
    return z_ends(psi, psi), z_ends(across + along, across - along)


def zpair(above, below, ends, plane):
    lane = lane_ids(above.shape[0])
    g = lroll(ends, 255 - 4 * plane)
    return jnp.where(lane == 127, g, lroll(above, 127)), jnp.where(lane == 0, g, lroll(below, 1))


def potential(p, ext, ends, psi, zs, zd, rows):
    v = 1.0 - jnp.exp(-ext[RHO, p, rows, :])
    psi[p, rows, :] = v
    a, b = zpair(v, v, ends[rows, :], p)
    zs[p, rows, :] = a + b
    zd[p, rows, :] = a - b


def collide(p, ext, psi, zs, zd, flux, out):
    v, xp, xm = psi[p], psi[p + 1], psi[p - 1]
    qxp = W1 * xp + W2 * (yroll(xp, 1) + yroll(xp, -1) + zs[p + 1])
    qxm = W1 * xm + W2 * (yroll(xm, 1) + yroll(xm, -1) + zs[p - 1])
    qy = W1 * v + W2 * (xp + xm + zs[p])
    zz = zd[p]
    g = (
        qxp - qxm,
        yroll(qy, 1) - yroll(qy, -1),
        W1 * zz + W2 * (zd[p + 1] + zd[p - 1] + yroll(zz, 1) + yroll(zz, -1)),
    )
    b = [yroll(ext[i, p + DIRECTIONS[i][0]], DIRECTIONS[i][1]) for i in range(19)]
    a0, a1, u, w, bf, fb = cell(b, ext[RHO, p], [ext[MOM + k, p] for k in range(3)], v, g)
    for k in range(3):
        flux[k, p] = v * fb[k]

    def top(a):
        return a[:16]

    vv = [top(INV_TAU * wk + bk) for wk, bk in zip(w, bf)]
    uu = [top(a) for a in u]
    base = INV_TAU * (top(a0) + 0.5 * dot([top(r + q) for r, q in zip(a1, w)], uu)) - dot(vv, uu)
    base = base + (-COUPLING * (1.0 - top(v))) * top(dot(fb, g))
    for i in range(19):
        o = (1.0 - INV_TAU) * top(b[i]) + base
        for k in range(3):
            if DIRECTIONS[i][k] > 0:
                o = o + vv[k]
            elif DIRECTIONS[i][k] < 0:
                o = o - vv[k]
        out[i, p - 1] = o


def finish(p, psi, flux, ends, out):
    fx, fxm, fy = flux[0, p + 1], flux[0, p - 1], flux[1, p]
    fz = flux[2, p]
    xd = fx - fxm
    fyx = flux[1, p + 1] + flux[1, p - 1]
    dx = xd[:16]
    dy = (yroll(fy, 1) - yroll(fy, -1))[:16]
    here = W1 * (dx + dy) + W2 * (
        (yroll(xd, 1) + yroll(xd, -1))[:16] + (yroll(fyx, 1) - yroll(fyx, -1))[:16]
    )
    across = W2 * (dx + dy)
    along = W1 * fz[:16] + W2 * (flux[2, p + 1, pl.ds(0, 16), :] + flux[2, p - 1, pl.ds(0, 16), :] + (yroll(fz, 1) + yroll(fz, -1))[:16])
    a, b = zpair(across + along, across - along, ends[pl.ds(0, 16), :], p)
    term = (COUPLING * (1.0 - psi[p, pl.ds(0, 16), :])) * (here + (a + b))
    for i in range(19):
        out[i, p - 1] = out[i, p - 1] + term


def planes(count, of, step, unroll=4):
    def body(k, _):
        step(of(k))
        return 0

    lax.fori_loop(0, count, body, 0, unroll=unroll)


def send_planes(out, out_hbm, sem, first, count):
    return pltpu.make_async_copy(out.at[:, pl.ds(first - 1, count)], out_hbm.at[:, pl.ds(first - 2, count)], sem)


def mid_kernel(ext_in, mini, sa, sb, r2, rb, psi_ends, flux_ends, psi_in, zs_in, zd_in, ext, psi, zs, zd, flux, out, ends, low, high):
    nx = ext.shape[1] - 4
    rows = pl.ds(16, 8)
    low[...], high[...] = by_parity("gy", rb[pl.ds(sa.shape[0], low.shape[0]), :], r2[...])
    for up, small, large in ((-1, sa, low), (1, sb, high)):
        for e, (f, d, first) in enumerate(y_entries(up)):
            ext[f, pl.ds(first, nx - 2), 23 - d if up < 0 else 16 + d, :] = large[pl.ds((nx - 2) * e, nx - 2), :]
        lines = [(side, *entry) for side in (-1, 1) for entry in edge_entries(side, up)]
        for e, (side, f, dx, dy) in enumerate(lines):
            plane, row = nx + 1 - dx if side < 0 else 2 + dx, 23 - dy if up < 0 else 16 + dy
            ext[f, plane, pl.ds(row, 1), :] = small[pl.ds(len(side_entries(1, up)) + e, 1), :]
    for k, (up, down) in enumerate(Z_PAIRS):
        ends[k] = z_ends(mini[up, rows, :], mini[down, rows, :])

    def close(p, _):
        for f, v in close_pairs(p, Z_PAIRS, [ends[k] for k in range(len(Z_PAIRS))], ext, rows):
            ext[f, p, rows, :] = v
        return 0

    lax.fori_loop(2, nx + 2, close, 0, unroll=4)
    for p in range(2, nx + 2):
        potential(p, ext, psi_ends, psi, zs, zd, rows)
    planes(nx - 2, lambda k: k + 3, lambda p: collide(p, ext, psi, zs, zd, flux, out))

    planes(nx - 4, lambda k: k + 4, lambda p: finish(p, psi, flux, flux_ends, out))


def fill_kernel(ext_in, r1, ext):
    nx = ext.shape[1] - 4
    for s, side in enumerate((-1, 1)):
        for e, (f, d) in enumerate(side_entries(0, side)):
            ext[f, 1 - d if side < 0 else nx + 2 + d, pl.ds(0, 16), :] = r1[s, e]


def last_kernel(ext_in, mini_in, r2, psi_in, zs_in, zd_in, flux_in, out_in, ext, mini, psi, zs, zd, flux, out, out_hbm, psi_ends, flux_ends, sems):
    nx = ext.shape[1] - 4
    copies = [
        send_planes(out, out_hbm, sems.at[k], first, count) for k, (first, count) in enumerate(((4, nx - 4), (2, 2), (nx, 2)))
    ]
    copies[0].start()
    lane = lane_ids(ROWS)
    group = (lane % 64) // 4
    for s, side in enumerate((-1, 1)):
        lines = [(up, *entry) for up in (-1, 1) for entry in edge_entries(side, up)]
        for e, (up, f, dx, dy) in enumerate(lines):
            plane, row = 1 - dx if side < 0 else nx + 2 + dx, 23 - dy if up < 0 else 16 + dy
            ext[f, plane, pl.ds(row, 1), :] = r2[s, pl.ds(e, 1), :]
        small = jnp.concatenate([r2[s, pl.ds(EDGE_LINES, 16), :], pltpu.roll(r2[s, pl.ds(EDGE_LINES - 8, 8), :], 2, 0)], axis=0)
        for groups, shift, parts in x_units(side):
            near = 1 if side < 0 else nx + 2
            here = any_group(group, (near, near + side)[: len(groups)])
            v = lroll(small, 4 * near - 4 * groups[0] - shift)
            for f, low, high in parts:
                mini[f] = jnp.where(here & slot_mask(lane, 0, low, high), v, mini[f])
    ends = [z_ends(mini[up], mini[down]) for up, down in Z_PAIRS]
    for p in (0, 1, nx + 2, nx + 3):
        keep = [k for k, (f, _) in enumerate(Z_PAIRS) if DIRECTIONS[f][0] == (-1 if p < 2 else 1) or (p in (1, nx + 2) and DIRECTIONS[f][0] == 0)]
        for f, v in close_pairs(p, [Z_PAIRS[k] for k in keep], [ends[k] for k in keep], ext, pl.ds(0, ROWS)):
            ext[f, p] = v
    psi_ends[...], flux_ends[...] = mini_adjoint(mini)
    for p in (0, 1, nx + 2, nx + 3):
        potential(p, ext, psi_ends, psi, zs, zd, pl.ds(0, ROWS))

    def outer(low, k):
        return low + k + jnp.where(k >= 2, nx - 2, 0)

    planes(4, lambda k: outer(1, k), lambda p: collide(p, ext, psi, zs, zd, flux, out))
    planes(4, lambda k: outer(2, k) - jnp.where(k >= 2, 2, 0), lambda p: finish(p, psi, flux, flux_ends, out))
    for copy in copies[1:]:
        copy.start()
    for copy in copies:
        copy.wait()


def swap(low, high, axis):
    n = lax.axis_size(axis)
    up = [(i, (i + 1) % n) for i in range(n)]
    return lax.ppermute(low, axis, up), lax.ppermute(high, axis, [(j, i) for i, j in up])


def ppermute_pairs(msg, axis, first):
    n = lax.axis_size(axis)
    found = []
    for i in range(first, n + first, 2):
        found += [(i % n, (i + 1) % n), ((i + 1) % n, i % n)]
    return lax.ppermute(msg, axis, found)


def swap_both(msg, axis):
    n = lax.axis_size(axis)
    if n == 2:
        return lax.ppermute(msg, axis, [(0, 1), (1, 0)])
    return jnp.stack(swap(msg[0], msg[1], axis))


def per_device(populations, adjoint_next):
    nx = populations.shape[1]
    ext_shape, mini_shape, plane_shape = (FIELDS, nx + 4, ROWS, 128), (FIELDS, ROWS, 128), (nx + 4, ROWS, 128)
    small_y = (len(side_entries(1, 1)) + EDGE_LINES, 128)
    ext, mini, ya, yb = call(
        load_kernel,
        tuple(pltpu.with_memory_space_constraint(v, pltpu.HBM) for v in (populations, adjoint_next)),
        (ext_shape, mini_shape, small_y, small_y),
        scratch=[pltpu.VMEM((19, nx, 16, 128), F32), pltpu.SemaphoreType.DMA((10,))],
        in_specs=[HB, HB],
        name="load",
    )
    large_y = (24 * (nx - 2) + 8, 128)
    two_large = [pltpu.VMEM(large_y, F32), pltpu.VMEM(large_y, F32)]
    (yb,) = call(
        pair_kernel, (ext, yb), ((small_y[0] + large_y[0], 128),), scratch=two_large, name="pair", cost=COSTLY
    )
    (xmsg,) = call(x_kernel, (ext,), ((2, 24, 16, 128),), name="xpack", cost=COSTLY)
    x1 = swap_both(xmsg, "gx")
    ya, y2b = ppermute_pairs(ya, "gy", 1), ppermute_pairs(yb, "gy", 0)
    mini, za, zb, ya, yb = call(
        yz_kernel,
        (mini, ya, y2b),
        (mini_shape, (ROWS + 16, 128), (ROWS + 16, 128), small_y, small_y),
        aliases={0: 0},
        name="yz",
    )
    (y2a,) = call(y_kernel, (ext, mini), (large_y,), scratch=two_large, name="ypack", cost=COSTLY)
    y2a = ppermute_pairs(y2a, "gy", 1)
    za, zb = swap(za, zb, "gz")
    mini, xmsg2 = call(
        zx_kernel,
        (mini, za, zb, ya, yb),
        (mini_shape, (2, EDGE_LINES + 16, 128)),
        aliases={0: 0},
        name="zx",
    )
    tile, out_shape = (ROWS, 128), (19, nx + 2, 16, 128)
    ext, psi_ends, flux_ends, psi, zs, zd = call(
        turn_kernel,
        (ext, mini),
        (ext_shape, tile, tile, plane_shape, plane_shape, plane_shape),
        scratch=[pltpu.VMEM((len(Z_PAIRS), 16, 128), F32)],
        aliases={0: 0},
        name="turn",
    )
    x2 = swap_both(xmsg2, "gx")
    ext, psi, zs, zd, flux, part = call(
        mid_kernel,
        (ext, mini, ya, yb, y2a, y2b, psi_ends, flux_ends, psi, zs, zd),
        (ext_shape, plane_shape, plane_shape, plane_shape, (3, *plane_shape), out_shape),
        scratch=[pltpu.VMEM(v, F32) for v in ((len(Z_PAIRS), 8, 128), large_y, large_y)],
        aliases={0: 0, 8: 1, 9: 2, 10: 3},
        name="mid",
    )
    (ext,) = call(fill_kernel, (ext, x1), (ext_shape,), aliases={0: 0}, name="fill")
    return call(
        last_kernel,
        (ext, mini, x2, psi, zs, zd, flux, part),
        (ext_shape, mini_shape, plane_shape, plane_shape, plane_shape, (3, *plane_shape), out_shape, populations.shape),
        scratch=[pltpu.VMEM(tile, F32), pltpu.VMEM(tile, F32), pltpu.SemaphoreType.DMA((3,))],
        aliases={0: 0, 1: 1, 3: 2, 4: 3, 5: 4, 6: 5, 7: 6},
        out_specs=[VM] * 7 + [HB],
        name="last",
    )[-1]


def solution(mesh):
    return jax.shard_map(
        per_device,
        mesh=mesh,
        in_specs=(P(None, "gx", "gy", "gz"), P(None, "gx", "gy", "gz")),
        out_specs=P(None, "gx", "gy", "gz"),
        check_vma=False,
    )
```
